256 devices in a mesh: wide: 16 (over x, y), medium: 2 (over z_lo), narrow: 8 (over z_hi, core).
Axes of the slice: x: 4, y: 4, z: 8 (z_hi: 4, z_lo: 2; z = z_hi * 2 + z_lo), core: 2. Of those that a mesh axis runs over, the one named last changes fastest.
Arguments:
- obj_tile: float32 [2, 4096, 1024], P(None, ('wide', 'narrow'), 'medium'), may hold values from -4 to 4
- probe: float32 [2, 4, 256, 256], replicated, may hold values from -4 to 4
- amplitude: float32 [16, 2, 8, 256, 256], P('wide', 'medium', 'narrow'), may hold values from 0.2 to 2
- row_offsets: int32 [16, 2, 8], P('wide', 'medium', 'narrow'), may hold values from 0 to 256, as said below
- col_offsets: int32 [16, 2, 8], P('wide', 'medium', 'narrow'), may hold values from 0 to 512, as said below
Outputs:
- object_step: float32 [2, 4096, 1024], P(None, ('wide', 'narrow'), 'medium')
- probe_gradient: float32 [2, 4, 256, 256], replicated
The draws below stay inside these ranges and needn't reach their ends.
Inputs may be any that keep to these rules, and one draw needn't show every extreme that they name: `row_offsets`: in every tile one position has row offset 0 and another one the largest, 256. `col_offsets`: in every tile one position has column offset 0 and another one the largest, 512.
All inputs are finite; a program needn't handle non-finite values.
Results may differ from the reference program's by a relative error of at most 0.0003.
Values sent between devices are 32-bit elements; how exact they have to be, the bound alone decides.
A program may use at most 128 MiB of HBM per device.

```python
import jax
import jax.numpy as jnp
from jax import lax

FRAME = 256
MODES = 4
TILE_ROWS = 256
TILE_COLS = 512
HALO = 128
POS_TILE = 8
GRID_ROWS = 16
GRID_COLS = 2
OBJ_ROWS = 4096
OBJ_COLS = 1024


def extremes(key, largest):
    key_base, key_low, key_step = jax.random.split(key, 3)
    base = jax.random.randint(key_base, (GRID_ROWS, GRID_COLS, POS_TILE), 0, largest + 1)
    lowest = jax.random.randint(key_low, (GRID_ROWS, GRID_COLS, 1), 0, POS_TILE)
    offset = jax.random.randint(key_step, (GRID_ROWS, GRID_COLS, 1), 1, POS_TILE)
    highest = (lowest + offset) % POS_TILE
    slot = jnp.arange(POS_TILE, dtype=jnp.int32)[None, None, :]
    base = jnp.where(slot == lowest, 0, base)
    base = jnp.where(slot == highest, largest, base)
    return base.astype(jnp.int32)


def draw_row_offsets(key, part):
    key = jax.random.fold_in(key, 11)
    return extremes(key, TILE_ROWS + 2 * HALO - FRAME)


def draw_col_offsets(key, part):
    key = jax.random.fold_in(key, 12)
    return extremes(key, TILE_COLS + 2 * HALO - FRAME)


def draw_probe(key, part):
    key = jax.random.fold_in(key, 13)
    steps = jnp.arange(FRAME, dtype=jnp.float32)
    centre = 0.5 * (FRAME - 1)
    width = 0.25 * FRAME
    spread = ((steps[:, None] - centre) * (steps[:, None] - centre) + (steps[None, :] - centre) * (steps[None, :] - centre)) / (width * width)
    envelope = jnp.exp(-0.5 * spread)
    shape = (2, MODES, FRAME, FRAME)
    rough = jax.random.truncated_normal(key, -4.0, 4.0, shape, jnp.float32)
    return (rough * envelope[None, None]).astype(jnp.float32)


def steps_of(stream_key, dims, shards, smallest, high):
    factor_of = 1.0
    for dim, blocks in shards:
        draws = jax.random.uniform(jax.random.fold_in(jax.random.fold_in(stream_key, 6), dim), (blocks,), jnp.float32, smallest / len(shards), high / len(shards))
        factor_of = factor_of * jnp.repeat(jnp.exp(draws), dims[dim] // blocks).reshape((-1,) + (1,) * (len(dims) - 1 - dim))
    return factor_of


def scatter_about(own_key, extent, scale, reach, pieces=(), kind=jnp.bfloat16):
    array = scale * jax.random.normal(own_key, extent, jnp.float32)
    if pieces:
        array = array * steps_of(own_key, extent, pieces, -0.22, 0.18)
    return jnp.clip(array, -reach, reach).astype(kind)


def setup_inputs(seed: int = 0) -> dict:
    keys = jax.random.split(jax.random.key(seed), 6)
    return {
        "obj_tile": scatter_about(keys[0], (2, OBJ_ROWS, OBJ_COLS), 0.5, 4.0, ((1, 128), (2, 2)), jnp.float32),
        "probe": draw_probe(jax.random.fold_in(keys[5], 71), 0),
        "amplitude": jnp.clip(0.2 + 1.8 * jax.random.uniform(keys[2], (GRID_ROWS, GRID_COLS, POS_TILE, FRAME, FRAME), jnp.float32) ** steps_of(keys[2], (GRID_ROWS, GRID_COLS, POS_TILE, FRAME, FRAME), ((0, 16), (1, 2), (2, 8)), -0.2, 0.2), 0.2, 2.0),
        "row_offsets": draw_row_offsets(jax.random.fold_in(keys[5], 71), 0),
        "col_offsets": draw_col_offsets(jax.random.fold_in(keys[5], 71), 0),
    }


intensity_floor = 0.1
damping = 4.0

def reference(obj_tile, probe, amplitude, row_offsets, col_offsets):
    padded = jnp.pad(obj_tile, ((0, 0), (HALO, HALO), (HALO, HALO)))
    base_rows = (jnp.arange(GRID_ROWS, dtype=jnp.int32) * TILE_ROWS)[:, None, None]
    base_cols = (jnp.arange(GRID_COLS, dtype=jnp.int32) * TILE_COLS)[None, :, None]
    row_starts = (row_offsets + base_rows).reshape(-1).astype(jnp.int32)
    col_starts = (col_offsets + base_cols).reshape(-1).astype(jnp.int32)
    amplitudes = amplitude.reshape((-1, FRAME, FRAME))
    probe_wave = lax.complex(probe[0], probe[1])
    lighting = lax.optimization_barrier(jnp.sum(probe[0] * probe[0] + probe[1] * probe[1], axis=0))
    zero_index = jnp.int32(0)

    def visit(carry, item):
        accumulated, grad_re, grad_im = carry
        row_start, col_start, measured = item
        patch = lax.dynamic_slice(padded, (zero_index, row_start, col_start), (2, FRAME, FRAME))
        wave = probe_wave * lax.complex(patch[0], patch[1])[None]
        far = jnp.fft.fft2(wave, norm='ortho')
        far_re = jnp.real(far)
        far_im = jnp.imag(far)
        inten = lax.optimization_barrier(jnp.sum(far_re * far_re + far_im * far_im, axis=0))
        factor = measured / jnp.sqrt(jnp.maximum(inten, intensity_floor)) - 1.0
        chi = jnp.fft.ifft2(lax.complex(far_re * factor[None], far_im * factor[None]), norm='ortho')
        chi_re = jnp.real(chi)
        chi_im = jnp.imag(chi)
        g_re = lax.optimization_barrier(jnp.sum(probe[0] * chi_re + probe[1] * chi_im, axis=0))
        g_im = lax.optimization_barrier(jnp.sum(probe[0] * chi_im - probe[1] * chi_re, axis=0))
        piece = jnp.stack([g_re, g_im, lighting])
        old = lax.dynamic_slice(accumulated, (zero_index, row_start, col_start), (3, FRAME, FRAME))
        accumulated = lax.dynamic_update_slice(accumulated, old + piece, (zero_index, row_start, col_start))
        grad_re = grad_re + patch[0][None] * chi_re + patch[1][None] * chi_im
        grad_im = grad_im + patch[0][None] * chi_im - patch[1][None] * chi_re
        return ((accumulated, grad_re, grad_im), None)
    start = (jnp.zeros((3, OBJ_ROWS + 2 * HALO, OBJ_COLS + 2 * HALO), jnp.float32), jnp.zeros((MODES, FRAME, FRAME), jnp.float32), jnp.zeros((MODES, FRAME, FRAME), jnp.float32))
    (accumulated, grad_re, grad_im), _ = lax.scan(visit, start, (row_starts, col_starts, amplitudes))
    cropped = accumulated[:, HALO:HALO + OBJ_ROWS, HALO:HALO + OBJ_COLS]
    direction = cropped[:2] / (cropped[2] + damping)
    numerator = jnp.sum(direction * cropped[:2])
    denominator = jnp.sum((direction[0] * direction[0] + direction[1] * direction[1]) * cropped[2])
    return (numerator / denominator * direction, jnp.stack([grad_re, grad_im]))
```

```python
import functools
import math

import jax
import jax.numpy as jnp
import numpy as np
from jax import lax
from jax.experimental import pallas as pl
from jax.experimental.pallas import tpu as pltpu
from jax.sharding import PartitionSpec as P

MESH = pl.DeviceIdType.MESH
f32 = jnp.float32
bf16 = jnp.bfloat16
FRAME = 256
MODES = 4
HALO = 128
STRIP = 32
NX, NY, NZ = 4, 4, 8
ROW_TILES = 16
INTENSITY_FLOOR = 0.1
DAMPING = 4.0


def here():
    w = lax.axis_index("wide")
    m = lax.axis_index("medium")
    n = lax.axis_index("narrow")
    return w // NY, w % NY, (n // 2) * 2 + m, n % 2


def device(x, y, z, c):
    return (x * NY + y, z % 2, (z // 2) * 2 + c)


class Sends:
    def __init__(self, sem):
        self.sem = sem
        self.copies = []

    def start(self, src, dst, recv_sem, target):
        copy = pltpu.make_async_remote_copy(
            src_ref=src,
            dst_ref=dst,
            send_sem=self.sem.at[len(self.copies)],
            recv_sem=recv_sem,
            device_id=target,
            device_id_type=MESH,
        )
        copy.start()
        self.copies.append(copy)

    def arrived(self, dst, recv_sem, source):
        pltpu.make_async_remote_copy(
            src_ref=dst,
            dst_ref=dst,
            send_sem=self.sem.at[0],
            recv_sem=recv_sem,
            device_id=source,
            device_id_type=MESH,
        ).wait_recv()

    def finish(self):
        for copy in self.copies:
            copy.wait_send()


def greet(peers):
    barrier = pltpu.get_barrier_semaphore()
    for peer in peers:
        pl.semaphore_signal(barrier, inc=1, device_id=peer, device_id_type=MESH)
    pl.semaphore_wait(barrier, len(peers))


def dft_tables():
    steps = np.arange(FRAME)
    angle = (steps[:, None] * steps[None, :] % FRAME) * (2.0 * math.pi / FRAME)
    cosine = np.cos(angle) / math.sqrt(FRAME)
    sine = np.sin(angle) / math.sqrt(FRAME)
    found = []
    for table in (
        np.block([[cosine, -sine], [sine, cosine]]),
        np.block([[cosine, sine], [-sine, cosine]]),
    ):
        table = table.astype(np.float32)
        high = table.astype(jnp.bfloat16)
        found += [high, (table - high.astype(np.float32)).astype(jnp.bfloat16)]
    return np.stack(found)


def split(x):
    high = x.astype(bf16)
    return high, (x - high.astype(f32)).astype(bf16)


def dot(a, b):
    return jnp.dot(a, b, preferred_element_type=f32)


def transform(field, tables, right, left):
    high, low = split(field)
    mid = dot(high, tables[right]) + dot(high, tables[right + 1]) + dot(low, tables[right])
    mid = jnp.concatenate([mid[:, :FRAME], mid[:, FRAME:]], axis=0)
    high, low = split(mid)
    return dot(tables[left], high) + dot(tables[left], low) + dot(tables[left + 1], high)


BLOCKS = ((1, 0), (1, 1), (2, 0), (2, 1), (3, 0), (3, 1), (4, 0), (0, 0))
N_SENDS = 200


def one_hot(shape, hit):
    return jnp.where(hit(lax.broadcasted_iota(jnp.int32, shape, 0), lax.broadcasted_iota(jnp.int32, shape, 1)), 1.0, 0.0).astype(bf16)


def pick_columns(x, table):
    high, low = split(x)
    return dot(high, table) + dot(low, table)


def pick_rows(table, x):
    high, low = split(x)
    return dot(table, high) + dot(table, low)


def update_kernel(
    obj, probe_in, amp_in, tables_in, own_row, offsets,
    step_out, probe_out,
    rows_tile, probe, amp, tables, far, factor, light, grad, where,
    sib_out, sib_in, total, halo_in, ring_in, ring_start, weight, direction,
    probe_part, part_in, part, in1, sum1, in2, sum2, in3, all3, all2, tile, tiles_in,
    send_sem, local_sem, gring_sem, gsib_sem, ghalo_sem, gsibhalo_sem, where_sem,
    sib_sem, halo_sem, ring_sem, part_sem, part_send_sem, sem1, sem2, sem3, asem3, asem2, asem1, asem0,
    tile_sem,
):
    x, y, z, c = here()
    m = z % 2
    w = x * NY + y
    n = (z // 2) * 2 + c
    xs = [((x + i) % NX) for i in range(NX)]
    ys = [((y + i) % NY) for i in range(NY)]
    zs = [((z + i) % NZ) for i in range(NZ)]
    x_peer = [device(v, y, z, c) for v in xs]
    y_peer = [device(x, v, z, c) for v in ys]
    z_peer = [device(x, y, v, c) for v in zs]
    sibling = device(x, y, z, 1 - c)
    up, down = z_peer[1], z_peer[7]
    onward = (up, down)
    behind = (down, up)
    wide_up = ((w + 1) % ROW_TILES, m, n)
    wide_down = ((w + ROW_TILES - 1) % ROW_TILES, m, n)
    sends = Sends(send_sem)

    locals_ = [
        pltpu.make_async_copy(a, b, local_sem.at[i])
        for i, (a, b) in enumerate(
            ((probe_in, probe), (amp_in, amp), (tables_in, tables))
        )
    ]
    for copy in locals_:
        copy.start()
    greet([sibling, wide_up, wide_down] + x_peer[1:] + y_peer[1:] + z_peer[1:])

    def strip_of(zb, core):
        return (zb // 2) * 2 + core

    def place(zb, core):
        rows = pl.ds(pl.multiple_of(HALO + STRIP * strip_of(zb, core), STRIP), STRIP)
        return rows, pl.ds(pl.multiple_of(512 * (zb % 2), 128), 512)

    def halo_place(zb, core, distance):
        s = strip_of(zb, core)
        rows = pl.ds(pl.multiple_of(HALO + STRIP * s + 256 * (1 - 2 * (s // 4)), STRIP), STRIP)
        if distance % 2 == 0:
            return rows, pl.ds(pl.multiple_of(512 * m, 128), 512)
        return rows, pl.ds(pl.multiple_of(512 - 128 * m, 128), 128)

    def block_of(distance, way):
        return (z + NZ - distance) % NZ if way == 0 else (z + distance) % NZ

    def pass_on(slot, src=None):
        distance, way = BLOCKS[slot]
        zb = block_of(distance, way)
        rows, cols = place(zb, c)
        whole = rows_tile.at[:, rows, cols]
        sends.start(whole if src is None else src, whole, gsib_sem.at[slot], sibling)
        hrows, hcols = halo_place(zb, c, distance)
        towards = (w + ROW_TILES + 2 * (strip_of(zb, c) // 4) - 1) % ROW_TILES
        sends.start(
            rows_tile.at[:, rows, hcols] if src is None else src,
            rows_tile.at[:, hrows, hcols], ghalo_sem.at[slot], (towards, m, n),
        )

    rows, cols = place(z, c)
    for plane in range(2):
        for way in range(2):
            sends.start(
                obj.at[plane], rows_tile.at[plane, rows, cols], gring_sem.at[way, 0, plane], onward[way]
            )
    pass_on(7, obj)
    own = pltpu.make_async_copy(obj, rows_tile.at[:, rows, cols], local_sem.at[3])
    own.start()
    mine = where.at[1, pl.ds(8 * c + z, 1)]
    for i in range(1, 8):
        sends.start(own_row, mine, where_sem.at[i - 1], z_peer[i])
    keep = pltpu.make_async_copy(own_row, mine, local_sem.at[4])
    keep.start()

    slot = 0
    for distance in (1, 2, 3):
        for plane in range(2):
            for way in range(2):
                rows, cols = place(block_of(distance, way), c)
                ref = rows_tile.at[plane, rows, cols]
                sends.arrived(ref, gring_sem.at[way, distance - 1, plane], behind[way])
                if distance < 3 or plane == way:
                    sends.start(ref, ref, gring_sem.at[way, distance, plane], onward[way])
        for way in range(2):
            pass_on(slot)
            slot += 1
        if distance == 1:
            keep.wait()
            for i in range(1, 8):
                sends.arrived(where.at[1, pl.ds(8 * c + zs[8 - i], 1)], where_sem.at[i - 1], z_peer[8 - i])
            half = where.at[1, pl.ds(pl.multiple_of(8 * c, 8), 8)]
            sends.start(half, half, where_sem.at[7], sibling)
        if distance == 2:
            sends.arrived(where.at[1, pl.ds(pl.multiple_of(8 * (1 - c), 8), 8)], where_sem.at[7], sibling)
            sends.start(where.at[1], where.at[0], where_sem.at[8], wide_up)
            sends.start(where.at[1], where.at[2], where_sem.at[9], wide_down)
    rows, cols = place(block_of(4, 0), c)
    for way in range(2):
        sends.arrived(rows_tile.at[way, rows, cols], gring_sem.at[way, 3, way], behind[way])
    pass_on(6)
    order = (7, 0, 1, 2, 3, 4, 5, 6)
    for slot in order:
        distance, way = BLOCKS[slot]
        hrows, hcols = halo_place(block_of(distance, way), c, distance)
        ref = rows_tile.at[:, hrows, hcols]
        sends.arrived(ref, ghalo_sem.at[slot], wide_up)
        sends.start(ref, ref, gsibhalo_sem.at[slot], sibling)
    for slot in order:
        distance, way = BLOCKS[slot]
        zb = block_of(distance, way)
        rows, cols = place(zb, 1 - c)
        sends.arrived(rows_tile.at[:, rows, cols], gsib_sem.at[slot], sibling)
        hrows, hcols = halo_place(zb, 1 - c, distance)
        sends.arrived(rows_tile.at[:, hrows, hcols], gsibhalo_sem.at[slot], sibling)
    own.wait()
    for copy in locals_:
        copy.wait()

    r0 = offsets[0]
    c0 = offsets[1] - HALO * (1 - m)

    def on_object(row):
        at = row + (256 * w - HALO)
        return (at >= 0) & (at < 256 * ROW_TILES)

    columns = one_hot((640, FRAME), lambda i, j: i == j + c0)
    lines = one_hot((FRAME, 512), lambda i, j: (j == i + r0) & on_object(j))
    window = pl.ds(pl.multiple_of(384 * m, 128), 640)
    patch = far.at[MODES]

    @pl.loop(0, 2)
    def _(plane):
        narrowed = pick_columns(rows_tile[plane, :, window], columns)
        patch[pl.ds(pl.multiple_of(plane * FRAME, FRAME), FRAME)] = pick_rows(lines, narrowed)

    factor[...] = jnp.zeros_like(factor)
    light[...] = jnp.zeros_like(light)
    grad[...] = jnp.zeros_like(grad)

    @pl.loop(0, MODES)
    def _(k):
        a, b = probe[0, k], probe[1, k]
        pr, pi = patch[:FRAME], patch[FRAME:]
        light[...] += a * a + b * b
        wave = jnp.concatenate([a * pr - b * pi, a * pi + b * pr], axis=1)
        result = transform(wave, tables, 0, 2)
        far[k] = result
        factor[...] += result[:FRAME] * result[:FRAME] + result[FRAME:] * result[FRAME:]

    factor[...] = amp[...] / jnp.sqrt(jnp.maximum(factor[...], INTENSITY_FLOOR)) - 1.0

    def part_copy(k):
        rows = pl.ds(pl.multiple_of(256 * k, 256), 256)
        return pltpu.make_async_remote_copy(
            src_ref=probe_part.at[1 - c, rows], dst_ref=part_in.at[rows],
            send_sem=part_send_sem.at[k], recv_sem=part_sem.at[k],
            device_id=sibling, device_id_type=MESH,
        )

    @pl.loop(0, MODES)
    def _(k):
        scale = factor[...]
        field = jnp.concatenate([far[k, :FRAME] * scale, far[k, FRAME:] * scale], axis=1)
        chi = transform(field, tables, 2, 0)
        cre, cim = chi[:FRAME], chi[FRAME:]
        a, b = probe[0, k], probe[1, k]
        pr, pi = patch[:FRAME], patch[FRAME:]
        grad[0] += a * cre + b * cim
        grad[1] += a * cim - b * cre
        rows = pl.ds(pl.multiple_of(256 * k, 256), 256)
        probe_part[0, rows] = pr * cre + pi * cim
        probe_part[1, rows] = pr * cim - pi * cre
        part_copy(k).start()

    columns_back = one_hot((FRAME, 640), lambda i, j: j == i + c0)

    def put(core, dst):
        lines_back = one_hot(
            (FRAME, FRAME), lambda i, j: 64 * (i // STRIP) + STRIP * core + i % STRIP == j + r0
        )
        for plane in range(2):
            found = pick_columns(pick_rows(lines_back, grad[plane]), columns_back)
            for j in range(8):
                dst[j, plane] = found[STRIP * j : STRIP * (j + 1)]

    put(1 - c, sib_out)
    for k in (0, 3, 1, 2):
        both = pl.ds(2 * k, 2)
        sends.start(sib_out.at[both], sib_in.at[both], sib_sem.at[k], sibling)
    put(c, total)

    def take_parts(half):
        for k in (2 * half, 2 * half + 1):
            rows = pl.ds(256 * k, 256)
            part_copy(k).wait_recv()
            part[rows] = part_in[rows] + probe_part[c, rows]
        for i in range(1, 4):
            q = (xs if half == 0 else ys)[i]
            sends.start(
                part.at[pl.ds(pl.multiple_of(512 * half + 128 * q, 128), 128)],
                in1.at[half, i - 1], sem1.at[half, i - 1],
                (x_peer if half == 0 else y_peer)[i],
            )

    take_parts(0)
    for k in (0, 3, 1, 2):
        both = pl.ds(2 * k, 2)
        sends.arrived(sib_in.at[both], sib_sem.at[k], sibling)
        total[both] += sib_in[both]
        if k in (0, 3):
            for i in range(2):
                sends.start(
                    total.at[2 * k + i], halo_in.at[k // 3, i], halo_sem.at[k // 3, i],
                    wide_down if k == 0 else wide_up,
                )
    take_parts(1)

    light_high, light_low = split(light[...])
    sends.arrived(where.at[0], where_sem.at[8], wide_down)
    sends.arrived(where.at[2], where_sem.at[9], wide_up)
    weight[...] = jnp.zeros_like(weight)

    @pl.loop(0, 48)
    def _(i):
        a = w - 1 + i // 16
        b = i % 2
        at = where[i // 16, i % 16]
        rs = STRIP * n + 256 * (w - a) + HALO - at[:, 0:1]
        cs = 512 * (m - b) + HALO - at[:, 1:2]
        real = (a >= 0) & (a < ROW_TILES)
        lines = one_hot((STRIP, FRAME), lambda p, q: (q == p + rs) & real)
        columns = one_hot((FRAME, 512), lambda p, q: p == q + cs)
        rows = jnp.concatenate([dot(lines, light_high), dot(lines, light_low)], axis=0).astype(bf16)
        found = dot(rows, columns)
        weight[...] += found[:STRIP] + found[STRIP:]

    for side in range(2):
        real = (w < ROW_TILES - 1) if side == 0 else (w > 0)
        for k in range(2):
            sends.arrived(halo_in.at[side, k], halo_sem.at[side, k], wide_up if side == 0 else wide_down)
            j = (4 if side == 0 else 2) + k
            total[j] += jnp.where(real, halo_in[side, k], 0.0)

    def near(zb, plane):
        return total.at[2 + zb // 2, plane, :, pl.ds(pl.multiple_of(128 * m, 128), 512)]

    def further(zb, plane):
        return total[2 + zb // 2, plane, :, pl.ds(pl.multiple_of(512 * (1 - m), 128), 128)]

    far_cols = pl.ds(pl.multiple_of(384 * m, 128), 128)
    for way in range(2):
        sends.start(
            near((z + 4) % NZ, way), ring_in.at[way, 3, way], ring_sem.at[way, 3, way], onward[way]
        )
    ring_start[...] = jnp.zeros_like(ring_start)
    for way in range(2):
        zb = (z + 3) % NZ if way == 0 else (z + NZ - 3) % NZ
        ring_start[way, :, far_cols] = further(zb, 1 - way)
        sends.start(
            ring_start.at[way], ring_in.at[way, 2, 1 - way], ring_sem.at[way, 2, 1 - way], onward[way]
        )

    def ring_step(distance):
        for first in range(2):
            for way in range(2):
                plane = way if first == 0 else 1 - way
                if distance == 3 and plane != way:
                    continue
                zb = (z + distance) % NZ if way == 0 else (z + NZ - distance) % NZ
                slot = ring_in.at[way, distance, plane]
                sends.arrived(slot, ring_sem.at[way, distance, plane], behind[way])
                if distance % 2 == 0:
                    slot[...] += near(zb, plane)[...]
                else:
                    slot[:, far_cols] += further(zb, plane)
                sends.start(
                    slot, ring_in.at[way, distance - 1, plane], ring_sem.at[way, distance - 1, plane], onward[way]
                )

    ring_step(3)
    for half in range(2):
        first = (x if half == 0 else y)
        peers = (x_peer if half == 0 else y_peer)
        for i in range(1, 4):
            sends.arrived(in1.at[half, i - 1], sem1.at[half, i - 1], peers[4 - i])
        rows = pl.ds(pl.multiple_of(512 * half + 128 * first, 128), 128)
        sum1[half] = part[rows] + in1[half, 0] + in1[half, 1] + in1[half, 2]
        for i in range(1, 4):
            q = (ys if half == 0 else xs)[i]
            sends.start(
                sum1.at[half, pl.ds(pl.multiple_of(32 * q, 32), 32)],
                in2.at[half, i - 1], sem2.at[half, i - 1],
                (y_peer if half == 0 else x_peer)[i],
            )
    ring_step(2)
    for half in range(2):
        second = (y if half == 0 else x)
        peers = (y_peer if half == 0 else x_peer)
        for i in range(1, 4):
            sends.arrived(in2.at[half, i - 1], sem2.at[half, i - 1], peers[4 - i])
        rows = pl.ds(pl.multiple_of(32 * second, 32), 32)
        sum2[half] = sum1[half, rows] + in2[half, 0] + in2[half, 1] + in2[half, 2]

    def z_tile(v):
        return pl.ds(pl.multiple_of(8 * (v // 2), 8), 8), pl.ds(pl.multiple_of(128 * (v % 2), 128), 128)

    for i in range(1, 8):
        rows, cols = z_tile(zs[i])
        sends.start(sum2.at[:, rows, cols], in3.at[i - 1], sem3.at[i - 1], z_peer[i])
    ring_step(1)
    for i in range(1, 8):
        sends.arrived(in3.at[i - 1], sem3.at[i - 1], z_peer[8 - i])
    rows, cols = z_tile(z)
    whole = sum2[:, rows, cols]
    for i in range(1, 8):
        whole = whole + in3[i - 1]
    all3[:, rows, cols] = whole
    for i in range(1, 8):
        sends.start(all3.at[:, rows, cols], all3.at[:, rows, cols], asem3.at[i - 1], z_peer[i])

    for way in range(2):
        for plane in range(2):
            sends.arrived(ring_in.at[way, 0, plane], ring_sem.at[way, 0, plane], behind[way])
    numerator = jnp.zeros((), f32)
    under = 1.0 / (weight[...] + DAMPING)
    squares = jnp.zeros((STRIP, 512), f32)
    for plane in range(2):
        strip = near(z, plane)[...] + ring_in[0, 0, plane] + ring_in[1, 0, plane]
        step = strip * under
        direction[plane] = step
        numerator += jnp.sum(step * strip)
        squares += step * step
    denominator = jnp.sum(squares * weight[...])
    line = lax.broadcasted_iota(jnp.int32, (8, 128), 0)
    tile[0] = jnp.where(line == 0, numerator, denominator)

    def tile_send(stage, peers, first):
        for i in range(1, len(peers)):
            sends.start(tile.at[stage], tiles_in.at[first + i - 1], tile_sem.at[first + i - 1], peers[i])

    def tile_sum(stage, peers, first):
        found = tile[stage]
        for i in range(1, len(peers)):
            sends.arrived(tiles_in.at[first + i - 1], tile_sem.at[first + i - 1], peers[len(peers) - i])
        for i in range(1, len(peers)):
            found = found + tiles_in[first + i - 1]
        tile[stage + 1] = found

    tile_send(0, z_peer, 0)

    for i in range(1, 8):
        prows, pcols = z_tile(zs[8 - i])
        sends.arrived(all3.at[:, prows, pcols], asem3.at[i - 1], z_peer[8 - i])
    for half in range(2):
        second = (y if half == 0 else x)
        peers = (y_peer if half == 0 else x_peer)
        rows = pl.ds(pl.multiple_of(32 * second, 32), 32)
        all2[half, rows] = all3[half]
        for i in range(1, 4):
            sends.start(all3.at[half], all2.at[half, rows], asem2.at[half, i - 1], peers[i])
    tile_sum(0, z_peer, 0)
    tile_send(1, y_peer, 7)
    for half in range(2):
        theirs = (ys if half == 0 else xs)
        peers = (y_peer if half == 0 else x_peer)
        for i in range(1, 4):
            rows = pl.ds(pl.multiple_of(32 * theirs[4 - i], 32), 32)
            sends.arrived(all2.at[half, rows], asem2.at[half, i - 1], peers[4 - i])
        first = (x if half == 0 else y)
        peers = (x_peer if half == 0 else y_peer)
        rows = pl.ds(pl.multiple_of(512 * half + 128 * first, 128), 128)
        for i in range(1, 4):
            sends.start(all2.at[half], probe_out.at[c, rows], asem1.at[half, i - 1], peers[i])
        sends.start(all2.at[half], probe_out.at[c, rows], asem0.at[half, 0], sibling)
        probe_out[c, rows] = all2[half]
    tile_sum(1, y_peer, 7)
    tile_send(2, x_peer, 10)
    tile_sum(2, x_peer, 10)
    tile_send(3, [None, sibling], 13)
    for half in range(2):
        theirs = (xs if half == 0 else ys)
        peers = (x_peer if half == 0 else y_peer)
        for i in range(1, 4):
            rows = pl.ds(pl.multiple_of(512 * half + 128 * theirs[4 - i], 128), 128)
            ref = probe_out.at[c, rows]
            sends.arrived(ref, asem1.at[half, i - 1], peers[4 - i])
            sends.start(ref, ref, asem0.at[half, i], sibling)
    tile_sum(3, [None, sibling], 13)
    sums = tile[4]
    alpha = sums[0:1, 0:1] / sums[1:2, 0:1]
    step_out[...] = direction[...] * alpha
    for half in range(2):
        theirs = (xs if half == 0 else ys)
        for i in range(4):
            rows = pl.ds(pl.multiple_of(512 * half + 128 * theirs[(4 - i) % 4], 128), 128)
            sends.arrived(probe_out.at[1 - c, rows], asem0.at[half, i], sibling)
    for k in range(MODES):
        part_copy(k).wait_send()
    sends.finish()


VMEM = pl.BlockSpec(memory_space=pltpu.VMEM)
SMEM = pl.BlockSpec(memory_space=pltpu.SMEM)
ANY = pl.BlockSpec(memory_space=pl.ANY)
DMA = pltpu.SemaphoreType.DMA


def update(obj, probe, amp, tables, own_row, offsets):
    v = lambda *shape: pltpu.VMEM(shape, f32)
    return pl.pallas_call(
        update_kernel,
        out_shape=[
            jax.ShapeDtypeStruct((2, STRIP, 512), f32),
            jax.ShapeDtypeStruct((2, 1024, FRAME), f32),
        ],
        in_specs=[ANY, ANY, ANY, ANY, VMEM, SMEM],
        out_specs=[VMEM, VMEM],
        scratch_shapes=[
            v(2, 512, 1024),
            v(2, MODES, FRAME, FRAME),
            v(FRAME, FRAME),
            pltpu.VMEM((4, 512, 512), bf16),
            v(MODES + 1, 512, FRAME),
            v(FRAME, FRAME),
            v(FRAME, FRAME),
            v(2, FRAME, FRAME),
            pltpu.VMEM((3, 16, 1, 128), jnp.int32),
            v(8, 2, STRIP, 640),
            v(8, 2, STRIP, 640),
            v(8, 2, STRIP, 640),
            v(2, 2, 2, STRIP, 640),
            v(2, 4, 2, STRIP, 512),
            v(2, STRIP, 512),
            v(STRIP, 512),
            v(2, STRIP, 512),
            v(2, 1024, FRAME),
            v(1024, FRAME),
            v(1024, FRAME),
            v(2, 3, 128, FRAME),
            v(2, 128, FRAME),
            v(2, 3, 32, FRAME),
            v(2, 32, FRAME),
            v(7, 2, 8, 128),
            v(2, 32, FRAME),
            v(2, 128, FRAME),
            v(5, 8, 128),
            v(14, 8, 128),
            DMA((N_SENDS,)),
            DMA((5,)),
            DMA((2, 4, 2)),
            DMA((8,)),
            DMA((8,)),
            DMA((8,)),
            DMA((10,)),
            DMA((4,)),
            DMA((2, 2)),
            DMA((2, 4, 2)),
            DMA((MODES,)),
            DMA((MODES,)),
            DMA((2, 3)),
            DMA((2, 3)),
            DMA((7,)),
            DMA((7,)),
            DMA((2, 3)),
            DMA((2, 3)),
            DMA((2, 4)),
            DMA((14,)),
        ],
        compiler_params=pltpu.CompilerParams(
            collective_id=0, has_side_effects=True, vmem_limit_bytes=56 * 2**20
        ),
    )(obj, probe, amp, tables, own_row, offsets)


def per_device(obj_tile, probe, amplitude, row_offsets, col_offsets):
    own = jnp.stack([row_offsets.reshape(()), col_offsets.reshape(())])
    own_row = jnp.pad(own, (0, 126)).reshape((1, 1, 128))
    step, gradient = update(
        obj_tile, probe, amplitude.reshape((FRAME, FRAME)), jnp.asarray(dft_tables()), own_row, own
    )
    return step, gradient.reshape((2, MODES, FRAME, FRAME))


def solution(mesh):
    in_specs = (
        P(None, ("wide", "narrow"), "medium"),
        P(),
        P("wide", "medium", "narrow", None, None),
        P("wide", "medium", "narrow"),
        P("wide", "medium", "narrow"),
    )
    out_specs = (P(None, ("wide", "narrow"), "medium"), P())
    return jax.shard_map(
        per_device, mesh=mesh, in_specs=in_specs, out_specs=out_specs, check_vma=False
    )
```

```python
import functools
import math

import jax
import jax.numpy as jnp
import numpy as np
from jax import lax
from jax.experimental import pallas as pl
from jax.experimental.pallas import tpu as pltpu
from jax.sharding import PartitionSpec as P

MESH = pl.DeviceIdType.MESH
f32 = jnp.float32
bf16 = jnp.bfloat16
FRAME = 256
MODES = 4
HALO = 128
STRIP = 32
NX, NY, NZ = 4, 4, 8
ROW_TILES = 16
INTENSITY_FLOOR = 0.1
DAMPING = 4.0


def here():
    w = lax.axis_index("wide")
    m = lax.axis_index("medium")
    n = lax.axis_index("narrow")
    return w // NY, w % NY, (n // 2) * 2 + m, n % 2


def device(x, y, z, c):
    return (x * NY + y, z % 2, (z // 2) * 2 + c)


class Sends:
    def __init__(self, sem):
        self.sem = sem
        self.copies = []

    def start(self, src, dst, recv_sem, target):
        copy = pltpu.make_async_remote_copy(
            src_ref=src,
            dst_ref=dst,
            send_sem=self.sem.at[len(self.copies)],
            recv_sem=recv_sem,
            device_id=target,
            device_id_type=MESH,
        )
        copy.start()
        self.copies.append(copy)

    def arrived(self, dst, recv_sem, source):
        pltpu.make_async_remote_copy(
            src_ref=dst,
            dst_ref=dst,
            send_sem=self.sem.at[0],
            recv_sem=recv_sem,
            device_id=source,
            device_id_type=MESH,
        ).wait_recv()

    def finish(self):
        for copy in self.copies:
            copy.wait_send()


def greet(peers):
    barrier = pltpu.get_barrier_semaphore()
    for peer in peers:
        pl.semaphore_signal(barrier, inc=1, device_id=peer, device_id_type=MESH)
    pl.semaphore_wait(barrier, len(peers))


def dft_tables():
    steps = np.arange(FRAME)
    angle = (steps[:, None] * steps[None, :] % FRAME) * (2.0 * math.pi / FRAME)
    cosine = np.cos(angle) / math.sqrt(FRAME)
    sine = np.sin(angle) / math.sqrt(FRAME)
    found = []
    for table in (
        np.block([[cosine, -sine], [sine, cosine]]),
        np.block([[cosine, sine], [-sine, cosine]]),
    ):
        table = table.astype(np.float32)
        high = table.astype(jnp.bfloat16)
        found += [high, (table - high.astype(np.float32)).astype(jnp.bfloat16)]
    return np.stack(found)


def split(x):
    high = x.astype(bf16)
    return high, (x - high.astype(f32)).astype(bf16)


def dot(a, b):
    return jnp.dot(a, b, preferred_element_type=f32)


def transform(field, tables, right, left):
    high, low = split(field)
    mid = dot(high, tables[right]) + dot(high, tables[right + 1]) + dot(low, tables[right])
    mid = jnp.concatenate([mid[:, :FRAME], mid[:, FRAME:]], axis=0)
    high, low = split(mid)
    return dot(tables[left], high) + dot(tables[left], low) + dot(tables[left + 1], high)


BLOCKS = (0, 6, 2, 7, 1, 3, 5, 4)
N_SENDS = 160


def one_hot(shape, hit):
    return jnp.where(hit(lax.broadcasted_iota(jnp.int32, shape, 0), lax.broadcasted_iota(jnp.int32, shape, 1)), 1.0, 0.0).astype(bf16)


def pick_columns(x, table):
    high, low = split(x)
    return dot(high, table) + dot(low, table)


def pick_rows(table, x):
    high, low = split(x)
    return dot(table, high) + dot(table, low)


def update_kernel(
    obj, probe_in, amp_in, tables_in, row_in, col_in,
    step_out, probe_out,
    rows_tile, probe, amp, tables, far, factor, light, grad, where,
    sib_out, sib_in, total, halo_in, in_four, in_two, in_side, weight, direction,
    probe_part, part_in, part, in1, sum1, in2, sum2, in3, all3, all2, tile, tiles_in,
    send_sem, local_sem, gtwo_sem, gfour_sem, gside_sem, gsib_sem, ghalo_sem, gsibhalo_sem, where_sem,
    sib_sem, halo_sem, four_sem, two_sem, side_sem, part_sem, part_send_sem, sem1, send1_sem, sem2, sem3,
    asem3, asem2, asem1, asem0, tile_sem,
):
    x, y, z, c = here()
    m = z % 2
    zh = z // 2
    w = x * NY + y
    n = zh * 2 + c
    xs = [((x + i) % NX) for i in range(NX)]
    ys = [((y + i) % NY) for i in range(NY)]
    zs = [((z + i) % NZ) for i in range(NZ)]
    x_peer = [device(v, y, z, c) for v in xs]
    y_peer = [device(x, v, z, c) for v in ys]
    z_peer = [device(x, y, v, c) for v in zs]
    plane_peer = [((w + i) % ROW_TILES, m, n) for i in range(ROW_TILES)]
    sibling = device(x, y, z, 1 - c)
    wide_up, wide_down = plane_peer[1], plane_peer[15]
    onward = (z_peer[2], z_peer[6])
    behind = (z_peer[6], z_peer[2])
    sends = Sends(send_sem)

    locals_ = [
        pltpu.make_async_copy(a, b, local_sem.at[i])
        for i, (a, b) in enumerate(
            ((probe_in, probe), (amp_in, amp), (tables_in, tables))
        )
    ]
    for copy in locals_:
        copy.start()
    r0 = row_in[0, 0, 0]
    offset_col = col_in[0, 0, 0]
    c0 = offset_col - HALO * (1 - m)
    lane = lax.broadcasted_iota(jnp.int32, (1, 128), 1)
    where[1, 8 * c + z] = jnp.where(lane == 0, r0, offset_col)
    greet([sibling] + plane_peer[1:] + z_peer[1:])

    def strip_of(zb, core):
        return (zb // 2) * 2 + core

    own_cols = pl.ds(pl.multiple_of(128 * m, 128), 512)
    side_cols = pl.ds(pl.multiple_of(512 * (1 - m), 128), 128)

    def columns_of(distance):
        return side_cols if distance % 2 else own_cols

    def place(zb, core):
        return pl.ds(pl.multiple_of(HALO + STRIP * strip_of(zb, core), STRIP), STRIP)

    def halo_place(zb, core):
        s = strip_of(zb, core)
        return pl.ds(pl.multiple_of(HALO + STRIP * s + 256 * (1 - 2 * (s // 4)), STRIP), STRIP)

    def pass_on(slot, src=None):
        distance = BLOCKS[slot]
        zb = zs[distance]
        cols = columns_of(distance)
        ref = rows_tile.at[:, place(zb, c), cols]
        towards = (w + ROW_TILES + 2 * (strip_of(zb, c) // 4) - 1) % ROW_TILES
        sends.start(
            ref if src is None else src,
            rows_tile.at[:, halo_place(zb, c), cols], ghalo_sem.at[slot], (towards, m, n),
        )
        sends.start(ref if src is None else src, ref, gsib_sem.at[slot], sibling)

    rows = place(z, c)
    for plane in range(2):
        for way in range(2):
            p = plane if way == 0 else 1 - plane
            sends.start(
                obj.at[p], rows_tile.at[p, rows, own_cols], gtwo_sem.at[way, p], onward[way]
            )
    pass_on(0, obj)
    out_cols = pl.ds(pl.multiple_of(384 * (1 - m), 128), 128)
    there = pl.ds(pl.multiple_of(512 * m, 128), 128)
    for i, distance in enumerate((1, 7, 3, 5)):
        sends.start(
            obj.at[:, :, out_cols], rows_tile.at[:, rows, there], gside_sem.at[i], z_peer[distance]
        )
    own = pltpu.make_async_copy(obj, rows_tile.at[:, rows, own_cols], local_sem.at[3])
    own.start()
    mine = where.at[1, pl.ds(8 * c + z, 1)]
    for i in range(1, 8):
        sends.start(mine, mine, where_sem.at[i - 1], z_peer[i])


    locals_[0].wait()
    light[...] = jnp.zeros_like(light)

    @pl.loop(0, MODES)
    def _(k):
        light[...] += probe[0, k] * probe[0, k] + probe[1, k] * probe[1, k]

    weight[...] = jnp.zeros_like(weight)

    def lamp(t):
        light_high, light_low = split(light[...])
        a = w - 1 + t
        real = (a >= 0) & (a < ROW_TILES)

        def add(i, b, first, width):
            at = where[t, 8 * (i // 4) + 2 * (i % 4) + b]
            rs = STRIP * n + 256 * (1 - t) + HALO - at[:, 0:1]
            cs = 512 * (m - b) + first + HALO - at[:, 1:2]
            lines = one_hot((STRIP, FRAME), lambda p, q: (q == p + rs) & real)
            columns = one_hot((FRAME, width), lambda p, q: p == q + cs)
            rows = jnp.concatenate([dot(lines, light_high), dot(lines, light_low)], axis=0).astype(bf16)
            found = dot(rows, columns)
            return found[:STRIP] + found[STRIP:]

        @pl.loop(0, 8)
        def _(i):
            weight[...] += add(i, m, 0, 512)
            weight[:, out_cols] += add(i, 1 - m, 384 * (1 - m), 128)

    for i in range(1, 8):
        sends.arrived(where.at[1, pl.ds(8 * c + zs[8 - i], 1)], where_sem.at[i - 1], z_peer[8 - i])
    half = where.at[1, pl.ds(pl.multiple_of(8 * c, 8), 8)]
    sends.start(half, half, where_sem.at[7], sibling)
    sends.arrived(where.at[1, pl.ds(pl.multiple_of(8 * (1 - c), 8), 8)], where_sem.at[7], sibling)
    sends.start(where.at[1], where.at[0], where_sem.at[8], wide_up)
    sends.start(where.at[1], where.at[2], where_sem.at[9], wide_down)
    lamp(1)

    for way in range(2):
        zb = zs[6 if way == 0 else 2]
        ref = rows_tile.at[way, place(zb, c), own_cols]
        sends.arrived(ref, gtwo_sem.at[way, way], behind[way])
        sends.start(ref, ref, gfour_sem.at[way], onward[way])
    for way in range(2):
        zb = zs[6 if way == 0 else 2]
        sends.arrived(rows_tile.at[1 - way, place(zb, c), own_cols], gtwo_sem.at[way, 1 - way], behind[way])
        pass_on(1 + way)
    for i, distance in enumerate((7, 1, 5, 3)):
        sends.arrived(rows_tile.at[:, place(zs[distance], c), side_cols], gside_sem.at[i], z_peer[distance])
        pass_on(BLOCKS.index(distance))

    def halo_arrived(slot):
        distance = BLOCKS[slot]
        ref = rows_tile.at[:, halo_place(zs[distance], c), columns_of(distance)]
        sends.arrived(ref, ghalo_sem.at[slot], wide_up)
        sends.start(ref, ref, gsibhalo_sem.at[slot], sibling)

    halo_arrived(0)
    sends.arrived(where.at[0], where_sem.at[8], wide_down)
    lamp(0)
    for way in range(2):
        sends.arrived(rows_tile.at[way, place(zs[4], c), own_cols], gfour_sem.at[way], behind[way])
    pass_on(7)
    sends.arrived(where.at[2], where_sem.at[9], wide_up)
    lamp(2)
    for slot in range(1, 7):
        halo_arrived(slot)
    halo_arrived(7)
    for slot in range(8):
        distance = BLOCKS[slot]
        cols = columns_of(distance)
        sends.arrived(rows_tile.at[:, place(zs[distance], 1 - c), cols], gsib_sem.at[slot], sibling)
        sends.arrived(rows_tile.at[:, halo_place(zs[distance], 1 - c), cols], gsibhalo_sem.at[slot], sibling)
    own.wait()
    for copy in locals_[1:]:
        copy.wait()

    def on_object(row):
        at = row + (256 * w - HALO)
        return (at >= 0) & (at < 256 * ROW_TILES)

    columns = one_hot((640, FRAME), lambda i, j: i == j + c0)
    lines = one_hot((FRAME, 512), lambda i, j: (j == i + r0) & on_object(j))
    patch = far.at[MODES]

    @pl.loop(0, 2)
    def _(plane):
        narrowed = pick_columns(rows_tile[plane], columns)
        patch[pl.ds(pl.multiple_of(plane * FRAME, FRAME), FRAME)] = pick_rows(lines, narrowed)

    factor[...] = jnp.zeros_like(factor)
    grad[...] = jnp.zeros_like(grad)

    @pl.loop(0, MODES)
    def _(k):
        a, b = probe[0, k], probe[1, k]
        pr, pi = patch[:FRAME], patch[FRAME:]
        wave = jnp.concatenate([a * pr - b * pi, a * pi + b * pr], axis=1)
        result = transform(wave, tables, 0, 2)
        far[k] = result
        factor[...] += result[:FRAME] * result[:FRAME] + result[FRAME:] * result[FRAME:]

    factor[...] = amp[...] / jnp.sqrt(jnp.maximum(factor[...], INTENSITY_FLOOR)) - 1.0

    def part_copy(k):
        return pltpu.make_async_remote_copy(
            src_ref=probe_part.at[1 - c, k], dst_ref=part_in.at[k],
            send_sem=part_send_sem.at[k], recv_sem=part_sem.at[k],
            device_id=sibling, device_id_type=MESH,
        )

    def first_copy(k, i):
        h = k // 2
        tx, ty = (x + i * h) % NX, (y + i * (1 - h)) % NY
        q = h * tx + (1 - h) * ty
        return pltpu.make_async_remote_copy(
            src_ref=part.at[k, pl.ds(pl.multiple_of(64 * q, 64), 64)], dst_ref=in1.at[k, i - 1],
            send_sem=send1_sem.at[k, i - 1], recv_sem=sem1.at[k, i - 1],
            device_id=(tx * NY + ty, m, n), device_id_type=MESH,
        )

    def take_part(k):
        part_copy(k).wait_recv()
        part[k] = part_in[k] + probe_part[c, k]
        for i in range(1, 4):
            first_copy(k, i).start()

    @pl.loop(0, MODES)
    def _(k):
        scale = factor[...]
        field = jnp.concatenate([far[k, :FRAME] * scale, far[k, FRAME:] * scale], axis=1)
        chi = transform(field, tables, 2, 0)
        cre, cim = chi[:FRAME], chi[FRAME:]
        a, b = probe[0, k], probe[1, k]
        pr, pi = patch[:FRAME], patch[FRAME:]
        grad[0] += a * cre + b * cim
        grad[1] += a * cim - b * cre
        probe_part[0, k] = pr * cre + pi * cim
        probe_part[1, k] = pr * cim - pi * cre
        part_copy(k).start()

        @pl.when(k > 0)
        def _():
            take_part(k - 1)

    columns_back = one_hot((FRAME, 640), lambda i, j: j == i + c0)

    def put(core, dst):
        lines_back = one_hot(
            (FRAME, FRAME), lambda i, j: 64 * (i // STRIP) + STRIP * core + i % STRIP == j + r0
        )
        for plane in range(2):
            found = pick_columns(pick_rows(lines_back, grad[plane]), columns_back)
            for j in range(8):
                dst[j, plane] = found[STRIP * j : STRIP * (j + 1)]

    put(1 - c, sib_out)
    for k in (0, 3, 1, 2):
        both = pl.ds(2 * k, 2)
        sends.start(sib_out.at[both], sib_in.at[both], sib_sem.at[k], sibling)
    put(c, total)
    take_part(3)
    early = zh % 2
    for k in (0, 3, 1, 2):
        both = pl.ds(2 * k, 2)
        sends.arrived(sib_in.at[both], sib_sem.at[k], sibling)
        total[both] += sib_in[both]
        if k == 3:
            for i in (early, 1 - early):
                sends.start(total.at[i], halo_in.at[0, i], halo_sem.at[0, i], wide_down)
                sends.start(total.at[6 + i], halo_in.at[1, i], halo_sem.at[1, i], wide_up)

    def take_halo(i):
        for side in range(2):
            real = (w < ROW_TILES - 1) if side == 0 else (w > 0)
            sends.arrived(halo_in.at[side, i], halo_sem.at[side, i], wide_up if side == 0 else wide_down)
            total[(4 if side == 0 else 2) + i] += jnp.where(real, halo_in[side, i], 0.0)

    def block(zb):
        return total.at[2 + zb // 2, :, :, own_cols]

    def second_stage(half):
        first = (y if half == 0 else x)
        peers = (y_peer if half == 0 else x_peer)
        rows = pl.ds(pl.multiple_of(64 * first, 64), 64)
        for k in (2 * half, 2 * half + 1):
            for i in range(1, 4):
                first_copy(k, i).wait_recv()
            sum1[k] = part[k, rows] + in1[k, 0] + in1[k, 1] + in1[k, 2]
        both = pl.ds(2 * half, 2)
        for i in range(1, 4):
            q = (xs if half == 0 else ys)[i]
            sends.start(
                sum1.at[both, pl.ds(pl.multiple_of(16 * q, 16), 16)],
                in2.at[half, i - 1], sem2.at[half, i - 1],
                (x_peer if half == 0 else y_peer)[i],
            )

    second_stage(0)
    second_stage(1)
    take_halo(early)
    for way in range(2):
        sends.start(block(zs[4]).at[way], in_four.at[way], four_sem.at[way], onward[way])

    for half in range(2):
        second = (x if half == 0 else y)
        peers = (x_peer if half == 0 else y_peer)
        for i in range(1, 4):
            sends.arrived(in2.at[half, i - 1], sem2.at[half, i - 1], peers[4 - i])
        rows = pl.ds(pl.multiple_of(16 * second, 16), 16)
        both = pl.ds(2 * half, 2)
        sum2[both] = sum1[both, rows] + in2[half, 0] + in2[half, 1] + in2[half, 2]

    def z_tile(v):
        return (
            pl.ds(2 * (v // 4), 2),
            pl.ds(pl.multiple_of(8 * ((v // 2) % 2), 8), 8),
            pl.ds(pl.multiple_of(128 * (v % 2), 128), 128),
        )

    for i in range(1, 8):
        sends.start(sum2.at[z_tile(zs[i])], in3.at[i - 1], sem3.at[i - 1], z_peer[i])
    take_halo(1 - early)
    for way in range(2):
        sends.start(
            block(zs[2 if way == 0 else 6]).at[1 - way], in_two.at[way, 1 - way], two_sem.at[way, 1 - way], onward[way]
        )
    for i, distance in enumerate((1, 7, 3, 5)):
        sends.start(
            total.at[2 + zs[distance] // 2, :, :, side_cols], in_side.at[i], side_sem.at[i], z_peer[distance]
        )
    for i in range(1, 8):
        sends.arrived(in3.at[i - 1], sem3.at[i - 1], z_peer[8 - i])
    whole = sum2[z_tile(z)]
    for i in range(1, 8):
        whole = whole + in3[i - 1]
    all3[z_tile(z)] = whole
    for i in range(1, 8):
        ref = all3.at[z_tile(z)]
        sends.start(ref, ref, asem3.at[i - 1], z_peer[i])
    for way in range(2):
        sends.arrived(in_four.at[way], four_sem.at[way], behind[way])
        in_four[way] += block(zs[2 if way == 0 else 6])[way]
        sends.start(in_four.at[way], in_two.at[way, way], two_sem.at[way, way], onward[way])

    for i in range(1, 8):
        sends.arrived(all3.at[z_tile(zs[8 - i])], asem3.at[i - 1], z_peer[8 - i])
    for half in range(2):
        second = (x if half == 0 else y)
        peers = (x_peer if half == 0 else y_peer)
        rows = pl.ds(pl.multiple_of(16 * second, 16), 16)
        both = pl.ds(2 * half, 2)
        all2[both, rows] = all3[both]
        for i in range(1, 4):
            sends.start(all3.at[both], all2.at[both, rows], asem2.at[half, i - 1], peers[i])

    near = pl.ds(pl.multiple_of(384 - 256 * m, 128), 128)
    for i, distance in enumerate((7, 1, 5, 3)):
        sends.arrived(in_side.at[i], side_sem.at[i], z_peer[distance])
    total[2 + zh, :, :, near] += in_side[0] + in_side[1] + in_side[2] + in_side[3]
    for way in range(2):
        for plane in range(2):
            sends.arrived(in_two.at[way, plane], two_sem.at[way, plane], behind[way])
    numerator = jnp.zeros((), f32)
    under = 1.0 / (weight[...] + DAMPING)
    squares = jnp.zeros((STRIP, 512), f32)
    for plane in range(2):
        strip = total[2 + zh, plane, :, own_cols] + in_two[0, plane] + in_two[1, plane]
        step = strip * under
        direction[plane] = step
        numerator += jnp.sum(step * strip)
        squares += step * step
    denominator = jnp.sum(squares * weight[...])
    line = lax.broadcasted_iota(jnp.int32, (8, 128), 0)
    tile[0] = jnp.where(line == 0, numerator, denominator)

    def tile_send(stage, peers, first):
        for i in range(1, len(peers)):
            sends.start(tile.at[stage], tiles_in.at[first + i - 1], tile_sem.at[first + i - 1], peers[i])

    def tile_sum(stage, peers, first):
        for i in range(1, len(peers)):
            sends.arrived(tiles_in.at[first + i - 1], tile_sem.at[first + i - 1], peers[len(peers) - i])
        found = tile[stage]
        for i in range(1, len(peers)):
            found = found + tiles_in[first + i - 1]
        tile[stage + 1] = found

    tile_send(0, [None, sibling], 0)
    tile_sum(0, [None, sibling], 0)
    tile_send(1, plane_peer, 1)
    for half in range(2):
        theirs = (xs if half == 0 else ys)
        peers = (x_peer if half == 0 else y_peer)
        both = pl.ds(2 * half, 2)
        for i in range(1, 4):
            rows = pl.ds(pl.multiple_of(16 * theirs[4 - i], 16), 16)
            sends.arrived(all2.at[both, rows], asem2.at[half, i - 1], peers[4 - i])
        first = (y if half == 0 else x)
        peers = (y_peer if half == 0 else x_peer)
        rows = pl.ds(pl.multiple_of(64 * first, 64), 64)
        for i in range(1, 4):
            sends.start(all2.at[both], probe_out.at[c, both, rows], asem1.at[half, i - 1], peers[i])
        sends.start(all2.at[both], probe_out.at[c, both, rows], asem0.at[half, 0], sibling)
        probe_out[c, both, rows] = all2[both]
    tile_sum(1, plane_peer, 1)
    tile_send(2, z_peer, 16)
    tile_sum(2, z_peer, 16)
    sums = tile[3]
    alpha = sums[0:1, 0:1] / sums[1:2, 0:1]
    step_out[...] = direction[...] * alpha
    for half in range(2):
        theirs = (ys if half == 0 else xs)
        peers = (y_peer if half == 0 else x_peer)
        both = pl.ds(2 * half, 2)
        for i in range(1, 4):
            rows = pl.ds(pl.multiple_of(64 * theirs[4 - i], 64), 64)
            ref = probe_out.at[c, both, rows]
            sends.arrived(ref, asem1.at[half, i - 1], peers[4 - i])
            sends.start(ref, ref, asem0.at[half, i], sibling)
    for half in range(2):
        theirs = (ys if half == 0 else xs)
        both = pl.ds(2 * half, 2)
        for i in range(4):
            rows = pl.ds(pl.multiple_of(64 * theirs[(4 - i) % 4], 64), 64)
            sends.arrived(probe_out.at[1 - c, both, rows], asem0.at[half, i], sibling)
    for k in range(MODES):
        part_copy(k).wait_send()
        for i in range(1, 4):
            first_copy(k, i).wait_send()
    sends.finish()


VMEM = pl.BlockSpec(memory_space=pltpu.VMEM)
SMEM = pl.BlockSpec(memory_space=pltpu.SMEM)
ANY = pl.BlockSpec(memory_space=pl.ANY)
DMA = pltpu.SemaphoreType.DMA


def update(obj, probe, amp, tables, row, col):
    v = lambda *shape: pltpu.VMEM(shape, f32)
    return pl.pallas_call(
        update_kernel,
        out_shape=[
            pltpu.VMEM((2, STRIP, 512), f32),
            pltpu.VMEM((2, MODES, FRAME, FRAME), f32),
        ],
        in_specs=[ANY, ANY, ANY, ANY, SMEM, SMEM],
        out_specs=[VMEM, VMEM],
        scratch_shapes=[
            v(2, 512, 640),
            v(2, MODES, FRAME, FRAME),
            v(FRAME, FRAME),
            pltpu.VMEM((4, 512, 512), bf16),
            v(MODES + 1, 512, FRAME),
            v(FRAME, FRAME),
            v(FRAME, FRAME),
            v(2, FRAME, FRAME),
            pltpu.VMEM((3, 16, 1, 128), jnp.int32),
            v(8, 2, STRIP, 640),
            v(8, 2, STRIP, 640),
            v(8, 2, STRIP, 640),
            v(2, 2, 2, STRIP, 640),
            v(2, STRIP, 512),
            v(2, 2, STRIP, 512),
            v(4, 2, STRIP, 128),
            v(STRIP, 512),
            v(2, STRIP, 512),
            v(2, MODES, FRAME, FRAME),
            v(MODES, FRAME, FRAME),
            v(MODES, FRAME, FRAME),
            v(MODES, 3, 64, FRAME),
            v(MODES, 64, FRAME),
            v(2, 3, 2, 16, FRAME),
            v(MODES, 16, FRAME),
            v(7, 2, 8, 128),
            v(MODES, 16, FRAME),
            v(MODES, 64, FRAME),
            v(4, 8, 128),
            v(23, 8, 128),
            DMA((N_SENDS,)),
            DMA((4,)),
            DMA((2, 2)),
            DMA((2,)),
            DMA((4,)),
            DMA((8,)),
            DMA((8,)),
            DMA((8,)),
            DMA((10,)),
            DMA((4,)),
            DMA((2, 2)),
            DMA((2,)),
            DMA((2, 2)),
            DMA((4,)),
            DMA((MODES,)),
            DMA((MODES,)),
            DMA((MODES, 3)),
            DMA((MODES, 3)),
            DMA((2, 3)),
            DMA((7,)),
            DMA((7,)),
            DMA((2, 3)),
            DMA((2, 3)),
            DMA((2, 4)),
            DMA((23,)),
        ],
        compiler_params=pltpu.CompilerParams(
            collective_id=0, has_side_effects=True, vmem_limit_bytes=56 * 2**20
        ),
    )(obj, probe, amp, tables, row, col)


def per_device(obj_tile, probe, amplitude, row_offsets, col_offsets):
    step, gradient = update(
        obj_tile, probe, amplitude.reshape((FRAME, FRAME)), jnp.asarray(dft_tables()), row_offsets, col_offsets
    )
    return step, gradient


def solution(mesh):
    in_specs = (
        P(None, ("wide", "narrow"), "medium"),
        P(),
        P("wide", "medium", "narrow", None, None),
        P("wide", "medium", "narrow"),
        P("wide", "medium", "narrow"),
    )
    out_specs = (P(None, ("wide", "narrow"), "medium"), P())
    return jax.shard_map(
        per_device, mesh=mesh, in_specs=in_specs, out_specs=out_specs, check_vma=False
    )
```

```python
import functools
import math

import jax
import jax.numpy as jnp
import numpy as np
from jax import lax
from jax.experimental import pallas as pl
from jax.experimental.pallas import tpu as pltpu
from jax.sharding import PartitionSpec as P

MESH = pl.DeviceIdType.MESH
f32 = jnp.float32
bf16 = jnp.bfloat16
FRAME = 256
MODES = 4
HALO = 128
STRIP = 32
NX, NY, NZ = 4, 4, 8
ROW_TILES = 16
INTENSITY_FLOOR = 0.1
DAMPING = 4.0


def here():
    w = lax.axis_index("wide")
    m = lax.axis_index("medium")
    n = lax.axis_index("narrow")
    return w // NY, w % NY, (n // 2) * 2 + m, n % 2


def device(x, y, z, c):
    return (x * NY + y, z % 2, (z // 2) * 2 + c)


class Sends:
    def __init__(self, sem):
        self.sem = sem
        self.copies = []

    def start(self, src, dst, recv_sem, target):
        copy = pltpu.make_async_remote_copy(
            src_ref=src,
            dst_ref=dst,
            send_sem=self.sem.at[len(self.copies)],
            recv_sem=recv_sem,
            device_id=target,
            device_id_type=MESH,
        )
        copy.start()
        self.copies.append(copy)

    def arrived(self, dst, recv_sem, source):
        pltpu.make_async_remote_copy(
            src_ref=dst,
            dst_ref=dst,
            send_sem=self.sem.at[0],
            recv_sem=recv_sem,
            device_id=source,
            device_id_type=MESH,
        ).wait_recv()

    def finish(self):
        for copy in self.copies:
            copy.wait_send()


def greet(peers):
    barrier = pltpu.get_barrier_semaphore()
    for peer in peers:
        pl.semaphore_signal(barrier, inc=1, device_id=peer, device_id_type=MESH)


def met(peers):
    pl.semaphore_wait(pltpu.get_barrier_semaphore(), len(peers))


def dft_tables():
    steps = np.arange(FRAME)
    angle = (steps[:, None] * steps[None, :] % FRAME) * (2.0 * math.pi / FRAME)
    cosine = np.cos(angle) / math.sqrt(FRAME)
    sine = np.sin(angle) / math.sqrt(FRAME)
    found = []
    for table in (cosine, cosine + sine, cosine - sine):
        table = table.astype(np.float32)
        high = table.astype(jnp.bfloat16)
        found += [high, (table - high.astype(np.float32)).astype(jnp.bfloat16)]
    return np.stack(found)


def split(x):
    high = x.astype(bf16)
    return high, (x - high.astype(f32)).astype(bf16)


def dot(a, b):
    return jnp.dot(a, b, preferred_element_type=f32)


def side(re, im, product, sign):
    k1 = product(re + im, 0)
    k2 = product(re, 2 if sign > 0 else 4)
    k3 = product(im, 4 if sign > 0 else 2)
    return k1 - k3, k1 - k2


def transform(re, im, tables, sign):
    def right(x, t):
        high, low = split(x)
        return dot(high, tables[t]) + dot(high, tables[t + 1]) + dot(low, tables[t])

    def left(x, t):
        high, low = split(x)
        return dot(tables[t], high) + dot(tables[t], low) + dot(tables[t + 1], high)

    re, im = side(re, im, right, sign)
    return side(re, im, left, sign)


BLOCKS = (0, 6, 2, 7, 1, 3, 5, 4)
N_SENDS = 160


def one_hot(shape, hit):
    return jnp.where(hit(lax.broadcasted_iota(jnp.int32, shape, 0), lax.broadcasted_iota(jnp.int32, shape, 1)), 1.0, 0.0).astype(bf16)


def pick_columns(x, table):
    high, low = split(x)
    return dot(high, table) + dot(low, table)


def pick_rows(table, x):
    high, low = split(x)
    return dot(table, high) + dot(table, low)


def update_kernel(
    obj, probe_in, amp_in, tables_in, row_in, col_in,
    step_out, probe_out,
    rows_tile, probe, amp, tables, far, factor, light, grad, where,
    sib_out, sib_in, total, halo_in, in_four, in_two, in_side, weight, direction, lit,
    probe_part, part_in, part, in1, sum1, in2, sum2, in3, all3, all2, tile, tiles_in,
    send_sem, local_sem, gtwo_sem, gfour_sem, gside_sem, gsib_sem, ghalo_sem, gsibhalo_sem, where_sem,
    sib_sem, halo_sem, four_sem, two_sem, side_sem, part_sem, part_send_sem, sem1, send1_sem, sem2, sem3,
    asem3, asem2, asem1, asem0, tile_sem,
):
    x, y, z, c = here()
    m = z % 2
    zh = z // 2
    w = x * NY + y
    n = zh * 2 + c
    xs = [((x + i) % NX) for i in range(NX)]
    ys = [((y + i) % NY) for i in range(NY)]
    zs = [((z + i) % NZ) for i in range(NZ)]
    x_peer = [device(v, y, z, c) for v in xs]
    y_peer = [device(x, v, z, c) for v in ys]
    z_peer = [device(x, y, v, c) for v in zs]
    plane_peer = [((w + i) % ROW_TILES, m, n) for i in range(ROW_TILES)]
    sibling = device(x, y, z, 1 - c)
    wide_up, wide_down = plane_peer[1], plane_peer[15]
    onward = (z_peer[2], z_peer[6])
    behind = (z_peer[6], z_peer[2])
    near_peer = (z_peer[1], z_peer[7])
    sends = Sends(send_sem)

    locals_ = [
        pltpu.make_async_copy(a, b, local_sem.at[i])
        for i, (a, b) in enumerate(
            ((probe_in, probe), (amp_in, amp), (tables_in, tables))
        )
    ]
    for copy in locals_:
        copy.start()
    r0 = row_in[0, 0, 0]
    offset_col = col_in[0, 0, 0]
    c0 = offset_col - HALO * (1 - m)
    lane = lax.broadcasted_iota(jnp.int32, (1, 128), 1)
    where[1, 8 * c + z] = jnp.where(lane == 0, r0, offset_col)
    everyone = [sibling] + plane_peer[1:] + z_peer[1:]
    greet(everyone)
    locals_[0].wait()
    light[...] = jnp.zeros_like(light)

    @pl.loop(0, MODES)
    def _(k):
        light[...] += probe[0, k] * probe[0, k] + probe[1, k] * probe[1, k]

    met(everyone)

    def strip_of(zb, core):
        return (zb // 2) * 2 + core

    own_cols = pl.ds(pl.multiple_of(128 * m, 128), 512)
    side_cols = pl.ds(pl.multiple_of(512 * (1 - m), 128), 128)

    def columns_of(distance):
        return side_cols if distance % 2 else own_cols

    def place(zb, core):
        return pl.ds(pl.multiple_of(HALO + STRIP * strip_of(zb, core), STRIP), STRIP)

    def halo_place(zb, core):
        s = strip_of(zb, core)
        return pl.ds(pl.multiple_of(HALO + STRIP * s + 256 * (1 - 2 * (s // 4)), STRIP), STRIP)

    def pass_on(slot, src=None):
        distance = BLOCKS[slot]
        zb = zs[distance]
        cols = columns_of(distance)
        ref = rows_tile.at[:, place(zb, c), cols]
        towards = (w + ROW_TILES + 2 * (strip_of(zb, c) // 4) - 1) % ROW_TILES
        sends.start(
            ref if src is None else src,
            rows_tile.at[:, halo_place(zb, c), cols], ghalo_sem.at[slot], (towards, m, n),
        )
        sends.start(ref if src is None else src, ref, gsib_sem.at[slot], sibling)

    mine = where.at[1, pl.ds(8 * c + z, 1)]
    for i in range(1, 8):
        sends.start(mine, mine, where_sem.at[i - 1], z_peer[i])

    rows = place(z, c)
    for plane in range(2):
        for way in range(2):
            p = plane if way == 0 else 1 - plane
            sends.start(
                obj.at[p], rows_tile.at[p, rows, own_cols], gtwo_sem.at[way, p], onward[way]
            )
    pass_on(0, obj)
    out_cols = pl.ds(pl.multiple_of(384 * (1 - m), 128), 128)
    there = pl.ds(pl.multiple_of(512 * m, 128), 128)
    give_cols = pl.ds(pl.multiple_of(384 - 256 * m, 128), 128)
    for way in range(2):
        sends.start(obj.at[:, :, out_cols], rows_tile.at[:, rows, there], gside_sem.at[way, 0], near_peer[way])
    own = pltpu.make_async_copy(obj, rows_tile.at[:, rows, own_cols], local_sem.at[3])
    own.start()
    for way in range(2):
        zb = zs[6 if way == 0 else 2]
        ref = rows_tile.at[way, place(zb, c), own_cols]
        sends.arrived(ref, gtwo_sem.at[way, way], behind[way])
        sends.start(ref, ref, gfour_sem.at[way], onward[way])
    for way in range(2):
        zb = zs[6 if way == 0 else 2]
        sends.arrived(rows_tile.at[1 - way, place(zb, c), own_cols], gtwo_sem.at[way, 1 - way], behind[way])
        sends.start(
            rows_tile.at[:, place(zb, c), give_cols], rows_tile.at[:, place(zb, c), there],
            gside_sem.at[way, 1], near_peer[way],
        )
        pass_on(1 + way)
    for step in range(2):
        for way in range(2):
            distance = ((7, 5), (1, 3))[way][step]
            sends.arrived(
                rows_tile.at[:, place(zs[distance], c), side_cols], gside_sem.at[way, step], near_peer[1 - way]
            )
            pass_on(BLOCKS.index(distance))

    for i in range(1, 8):
        sends.arrived(where.at[1, pl.ds(8 * c + zs[8 - i], 1)], where_sem.at[i - 1], z_peer[8 - i])
    half = where.at[1, pl.ds(pl.multiple_of(8 * c, 8), 8)]
    sends.start(half, half, where_sem.at[7], sibling)

    def halo_arrived(slot):
        distance = BLOCKS[slot]
        ref = rows_tile.at[:, halo_place(zs[distance], c), columns_of(distance)]
        sends.arrived(ref, ghalo_sem.at[slot], wide_up)
        sends.start(ref, ref, gsibhalo_sem.at[slot], sibling)

    halo_arrived(0)
    for way in range(2):
        sends.arrived(rows_tile.at[way, place(zs[4], c), own_cols], gfour_sem.at[way], behind[way])
    pass_on(7)
    for slot in range(1, 7):
        halo_arrived(slot)
    sends.arrived(where.at[1, pl.ds(pl.multiple_of(8 * (1 - c), 8), 8)], where_sem.at[7], sibling)
    sends.start(where.at[1], where.at[0], where_sem.at[8], wide_up)
    sends.start(where.at[1], where.at[2], where_sem.at[9], wide_down)
    halo_arrived(7)
    for slot in range(8):
        distance = BLOCKS[slot]
        cols = columns_of(distance)
        sends.arrived(rows_tile.at[:, place(zs[distance], 1 - c), cols], gsib_sem.at[slot], sibling)
        sends.arrived(rows_tile.at[:, halo_place(zs[distance], 1 - c), cols], gsibhalo_sem.at[slot], sibling)
    own.wait()
    for copy in locals_[1:]:
        copy.wait()

    def on_object(row):
        at = row + (256 * w - HALO)
        return (at >= 0) & (at < 256 * ROW_TILES)

    columns = one_hot((640, FRAME), lambda i, j: i == j + c0)
    lines = one_hot((FRAME, 512), lambda i, j: (j == i + r0) & on_object(j))
    patch = far.at[MODES]

    @pl.loop(0, 2)
    def _(plane):
        narrowed = pick_columns(rows_tile[plane], columns)
        patch[pl.ds(pl.multiple_of(plane * FRAME, FRAME), FRAME)] = pick_rows(lines, narrowed)

    pr, pi = patch[:FRAME], patch[FRAME:]
    for k in range(MODES):
        a, b = probe[0, k], probe[1, k]
        fre, fim = transform(a * pr - b * pi, a * pi + b * pr, tables, 1)
        far[k, :FRAME] = fre
        far[k, FRAME:] = fim
        squares = fre * fre + fim * fim
        factor[...] = squares if k == 0 else factor[...] + squares

    factor[...] = amp[...] / jnp.sqrt(jnp.maximum(factor[...], INTENSITY_FLOOR)) - 1.0

    def part_copy(k):
        return pltpu.make_async_remote_copy(
            src_ref=probe_part.at[1 - c, k], dst_ref=part_in.at[k],
            send_sem=part_send_sem.at[k], recv_sem=part_sem.at[k],
            device_id=sibling, device_id_type=MESH,
        )

    def first_copy(k, i):
        h = k // 2
        tx, ty = (x + i * h) % NX, (y + i * (1 - h)) % NY
        q = h * tx + (1 - h) * ty
        return pltpu.make_async_remote_copy(
            src_ref=part.at[k, pl.ds(pl.multiple_of(64 * q, 64), 64)], dst_ref=in1.at[k, i - 1],
            send_sem=send1_sem.at[k, i - 1], recv_sem=sem1.at[k, i - 1],
            device_id=(tx * NY + ty, m, n), device_id_type=MESH,
        )

    def take_part(k):
        part_copy(k).wait_recv()
        part[k] = part_in[k] + probe_part[c, k]
        for i in range(1, 4):
            first_copy(k, i).start()

    for k in range(MODES):
        scale = factor[...]
        cre, cim = transform(far[k, :FRAME] * scale, far[k, FRAME:] * scale, tables, -1)
        a, b = probe[0, k], probe[1, k]
        pr, pi = patch[:FRAME], patch[FRAME:]
        probe_part[0, k] = pr * cre + pi * cim
        probe_part[1, k] = pr * cim - pi * cre
        part_copy(k).start()
        gre, gim = a * cre + b * cim, a * cim - b * cre
        grad[0] = gre if k == 0 else grad[0] + gre
        grad[1] = gim if k == 0 else grad[1] + gim
        if k > 0:
            take_part(k - 1)

    columns_back = one_hot((FRAME, 640), lambda i, j: j == i + c0)

    def put(core, dst):
        lines_back = one_hot(
            (FRAME, FRAME), lambda i, j: 64 * (i // STRIP) + STRIP * core + i % STRIP == j + r0
        )
        for plane in range(2):
            found = pick_columns(pick_rows(lines_back, grad[plane]), columns_back)
            for j in range(8):
                dst[j, plane] = found[STRIP * j : STRIP * (j + 1)]

    put(1 - c, sib_out)
    for k in (0, 3, 1, 2):
        both = pl.ds(2 * k, 2)
        sends.start(sib_out.at[both], sib_in.at[both], sib_sem.at[k], sibling)
    put(c, total)
    take_part(3)
    early = zh % 2
    for k in (0, 3, 1, 2):
        both = pl.ds(2 * k, 2)
        sends.arrived(sib_in.at[both], sib_sem.at[k], sibling)
        total[both] += sib_in[both]
        if k == 3:
            for i in (early, 1 - early):
                sends.start(total.at[i], halo_in.at[0, i], halo_sem.at[0, i], wide_down)
                sends.start(total.at[6 + i], halo_in.at[1, i], halo_sem.at[1, i], wide_up)

    weight[...] = jnp.zeros_like(weight)

    def lamp(t):
        light_high, light_low = split(light[...])
        a = w - 1 + t
        real = (a >= 0) & (a < ROW_TILES)
        shape = (16, STRIP, FRAME)
        rs = STRIP * n + 256 * (1 - t) + HALO - where[t][:, :, 0:1]
        hit = (lax.broadcasted_iota(jnp.int32, shape, 2) == lax.broadcasted_iota(jnp.int32, shape, 1) + rs) & real
        lines = jnp.where(hit, 1.0, 0.0).reshape((16 * STRIP, FRAME)).astype(bf16)
        lit[:, 0] = dot(lines, light_high).astype(bf16).reshape(shape)
        lit[:, 1] = dot(lines, light_low).astype(bf16).reshape(shape)

        def add(i, b, first, width):
            at = 8 * (i // 4) + 2 * (i % 4) + b
            cs = 512 * (m - b) + first + HALO - where[t, at][:, 1:2]
            columns = one_hot((FRAME, width), lambda p, q: p == q + cs)
            found = dot(lit[at].reshape((2 * STRIP, FRAME)), columns)
            return found[:STRIP] + found[STRIP:]

        @pl.loop(0, 8)
        def _(i):
            weight[...] += add(i, m, 0, 512)
            weight[:, out_cols] += add(i, 1 - m, 384 * (1 - m), 128)

    lamp(1)
    sends.arrived(where.at[0], where_sem.at[8], wide_down)

    def take_halo(i):
        for side in range(2):
            real = (w < ROW_TILES - 1) if side == 0 else (w > 0)
            sends.arrived(halo_in.at[side, i], halo_sem.at[side, i], wide_up if side == 0 else wide_down)
            total[(4 if side == 0 else 2) + i] += jnp.where(real, halo_in[side, i], 0.0)

    def block(zb):
        return total.at[2 + zb // 2, :, :, own_cols]

    def second_stage(half):
        first = (y if half == 0 else x)
        peers = (y_peer if half == 0 else x_peer)
        rows = pl.ds(pl.multiple_of(64 * first, 64), 64)
        for k in (2 * half, 2 * half + 1):
            for i in range(1, 4):
                first_copy(k, i).wait_recv()
            sum1[k] = part[k, rows] + in1[k, 0] + in1[k, 1] + in1[k, 2]
        both = pl.ds(2 * half, 2)
        for i in range(1, 4):
            q = (xs if half == 0 else ys)[i]
            sends.start(
                sum1.at[both, pl.ds(pl.multiple_of(16 * q, 16), 16)],
                in2.at[half, i - 1], sem2.at[half, i - 1],
                (x_peer if half == 0 else y_peer)[i],
            )

    second_stage(0)
    second_stage(1)
    take_halo(early)
    for way in range(2):
        sends.start(block(zs[4]).at[way], in_four.at[way], four_sem.at[way], onward[way])

    for half in range(2):
        second = (x if half == 0 else y)
        peers = (x_peer if half == 0 else y_peer)
        for i in range(1, 4):
            sends.arrived(in2.at[half, i - 1], sem2.at[half, i - 1], peers[4 - i])
        rows = pl.ds(pl.multiple_of(16 * second, 16), 16)
        both = pl.ds(2 * half, 2)
        sum2[both] = sum1[both, rows] + in2[half, 0] + in2[half, 1] + in2[half, 2]

    def z_tile(v):
        return (
            pl.ds(2 * (v // 4), 2),
            pl.ds(pl.multiple_of(8 * ((v // 2) % 2), 8), 8),
            pl.ds(pl.multiple_of(128 * (v % 2), 128), 128),
        )

    for i in range(1, 8):
        sends.start(sum2.at[z_tile(zs[i])], in3.at[i - 1], sem3.at[i - 1], z_peer[i])
    take_halo(1 - early)
    for way in range(2):
        sends.start(
            block(zs[2 if way == 0 else 6]).at[1 - way], in_two.at[way, 1 - way], two_sem.at[way, 1 - way], onward[way]
        )
    for i, distance in enumerate((1, 7, 3, 5)):
        sends.start(
            total.at[2 + zs[distance] // 2, :, :, side_cols], in_side.at[i], side_sem.at[i], z_peer[distance]
        )
    lamp(0)
    sends.arrived(where.at[2], where_sem.at[9], wide_up)
    for i in range(1, 8):
        sends.arrived(in3.at[i - 1], sem3.at[i - 1], z_peer[8 - i])
    whole = sum2[z_tile(z)]
    for i in range(1, 8):
        whole = whole + in3[i - 1]
    all3[z_tile(z)] = whole
    for i in range(1, 8):
        ref = all3.at[z_tile(z)]
        sends.start(ref, ref, asem3.at[i - 1], z_peer[i])
    for way in range(2):
        sends.arrived(in_four.at[way], four_sem.at[way], behind[way])
        in_four[way] += block(zs[2 if way == 0 else 6])[way]
        sends.start(in_four.at[way], in_two.at[way, way], two_sem.at[way, way], onward[way])

    for i in range(1, 8):
        sends.arrived(all3.at[z_tile(zs[8 - i])], asem3.at[i - 1], z_peer[8 - i])
    for half in range(2):
        second = (x if half == 0 else y)
        peers = (x_peer if half == 0 else y_peer)
        rows = pl.ds(pl.multiple_of(16 * second, 16), 16)
        both = pl.ds(2 * half, 2)
        all2[both, rows] = all3[both]
        for i in range(1, 4):
            sends.start(all3.at[both], all2.at[both, rows], asem2.at[half, i - 1], peers[i])

    lamp(2)
    for half in range(2):
        theirs = (xs if half == 0 else ys)
        peers = (x_peer if half == 0 else y_peer)
        both = pl.ds(2 * half, 2)
        for i in range(1, 4):
            rows = pl.ds(pl.multiple_of(16 * theirs[4 - i], 16), 16)
            sends.arrived(all2.at[both, rows], asem2.at[half, i - 1], peers[4 - i])
        first = (y if half == 0 else x)
        peers = (y_peer if half == 0 else x_peer)
        rows = pl.ds(pl.multiple_of(64 * first, 64), 64)
        for i in range(1, 4):
            sends.start(all2.at[both], probe_out.at[c, both, rows], asem1.at[half, i - 1], peers[i])
        sends.start(all2.at[both], probe_out.at[c, both, rows], asem0.at[half, 0], sibling)
        probe_out[c, both, rows] = all2[both]

    near = pl.ds(pl.multiple_of(384 - 256 * m, 128), 128)
    for i, distance in enumerate((7, 1, 5, 3)):
        sends.arrived(in_side.at[i], side_sem.at[i], z_peer[distance])
    total[2 + zh, :, :, near] += in_side[0] + in_side[1] + in_side[2] + in_side[3]
    for way in range(2):
        for plane in range(2):
            sends.arrived(in_two.at[way, plane], two_sem.at[way, plane], behind[way])
    numerator = jnp.zeros((), f32)
    under = 1.0 / (weight[...] + DAMPING)
    squares = jnp.zeros((STRIP, 512), f32)
    for plane in range(2):
        strip = total[2 + zh, plane, :, own_cols] + in_two[0, plane] + in_two[1, plane]
        step = strip * under
        direction[plane] = step
        numerator += jnp.sum(step * strip)
        squares += step * step
    denominator = jnp.sum(squares * weight[...])
    line = lax.broadcasted_iota(jnp.int32, (8, 128), 0)
    tile[0] = jnp.where(line == 0, numerator, denominator)

    def tile_send(stage, peers, first):
        for i in range(1, len(peers)):
            sends.start(tile.at[stage], tiles_in.at[first + i - 1], tile_sem.at[first + i - 1], peers[i])

    def tile_sum(stage, peers, first):
        for i in range(1, len(peers)):
            sends.arrived(tiles_in.at[first + i - 1], tile_sem.at[first + i - 1], peers[len(peers) - i])
        found = tile[stage]
        for i in range(1, len(peers)):
            found = found + tiles_in[first + i - 1]
        tile[stage + 1] = found

    tile_send(0, [None, sibling], 0)
    tile_sum(0, [None, sibling], 0)
    tile_send(1, plane_peer, 1)
    tile_sum(1, plane_peer, 1)
    tile_send(2, z_peer, 16)
    tile_sum(2, z_peer, 16)
    sums = tile[3]
    alpha = sums[0:1, 0:1] / sums[1:2, 0:1]
    step_out[...] = direction[...] * alpha
    for half in range(2):
        theirs = (ys if half == 0 else xs)
        peers = (y_peer if half == 0 else x_peer)
        both = pl.ds(2 * half, 2)
        for i in range(1, 4):
            rows = pl.ds(pl.multiple_of(64 * theirs[4 - i], 64), 64)
            ref = probe_out.at[c, both, rows]
            sends.arrived(ref, asem1.at[half, i - 1], peers[4 - i])
            sends.start(ref, ref, asem0.at[half, i], sibling)
    for half in range(2):
        theirs = (ys if half == 0 else xs)
        both = pl.ds(2 * half, 2)
        for i in range(4):
            rows = pl.ds(pl.multiple_of(64 * theirs[(4 - i) % 4], 64), 64)
            sends.arrived(probe_out.at[1 - c, both, rows], asem0.at[half, i], sibling)
    for k in range(MODES):
        part_copy(k).wait_send()
        for i in range(1, 4):
            first_copy(k, i).wait_send()
    sends.finish()


VMEM = pl.BlockSpec(memory_space=pltpu.VMEM)
SMEM = pl.BlockSpec(memory_space=pltpu.SMEM)
ANY = pl.BlockSpec(memory_space=pl.ANY)
DMA = pltpu.SemaphoreType.DMA


def update(obj, probe, amp, tables, row, col):
    v = lambda *shape: pltpu.VMEM(shape, f32)
    return pl.pallas_call(
        update_kernel,
        out_shape=[
            pltpu.VMEM((2, STRIP, 512), f32),
            pltpu.VMEM((2, MODES, FRAME, FRAME), f32),
        ],
        in_specs=[ANY, ANY, ANY, ANY, SMEM, SMEM],
        out_specs=[VMEM, VMEM],
        scratch_shapes=[
            v(2, 512, 640),
            v(2, MODES, FRAME, FRAME),
            v(FRAME, FRAME),
            pltpu.VMEM((6, FRAME, FRAME), bf16),
            v(MODES + 1, 512, FRAME),
            v(FRAME, FRAME),
            v(FRAME, FRAME),
            v(2, FRAME, FRAME),
            pltpu.VMEM((3, 16, 1, 128), jnp.int32),
            v(8, 2, STRIP, 640),
            v(8, 2, STRIP, 640),
            v(8, 2, STRIP, 640),
            v(2, 2, 2, STRIP, 640),
            v(2, STRIP, 512),
            v(2, 2, STRIP, 512),
            v(4, 2, STRIP, 128),
            v(STRIP, 512),
            v(2, STRIP, 512),
            pltpu.VMEM((16, 2, STRIP, FRAME), bf16),
            v(2, MODES, FRAME, FRAME),
            v(MODES, FRAME, FRAME),
            v(MODES, FRAME, FRAME),
            v(MODES, 3, 64, FRAME),
            v(MODES, 64, FRAME),
            v(2, 3, 2, 16, FRAME),
            v(MODES, 16, FRAME),
            v(7, 2, 8, 128),
            v(MODES, 16, FRAME),
            v(MODES, 64, FRAME),
            v(4, 8, 128),
            v(23, 8, 128),
            DMA((N_SENDS,)),
            DMA((4,)),
            DMA((2, 2)),
            DMA((2,)),
            DMA((2, 2)),
            DMA((8,)),
            DMA((8,)),
            DMA((8,)),
            DMA((10,)),
            DMA((4,)),
            DMA((2, 2)),
            DMA((2,)),
            DMA((2, 2)),
            DMA((4,)),
            DMA((MODES,)),
            DMA((MODES,)),
            DMA((MODES, 3)),
            DMA((MODES, 3)),
            DMA((2, 3)),
            DMA((7,)),
            DMA((7,)),
            DMA((2, 3)),
            DMA((2, 3)),
            DMA((2, 4)),
            DMA((23,)),
        ],
        compiler_params=pltpu.CompilerParams(
            collective_id=0, has_side_effects=True, vmem_limit_bytes=56 * 2**20
        ),
    )(obj, probe, amp, tables, row, col)


def per_device(obj_tile, probe, amplitude, row_offsets, col_offsets):
    step, gradient = update(
        obj_tile, probe, amplitude.reshape((FRAME, FRAME)), jnp.asarray(dft_tables()), row_offsets, col_offsets
    )
    return step, gradient


def solution(mesh):
    in_specs = (
        P(None, ("wide", "narrow"), "medium"),
        P(),
        P("wide", "medium", "narrow", None, None),
        P("wide", "medium", "narrow"),
        P("wide", "medium", "narrow"),
    )
    out_specs = (P(None, ("wide", "narrow"), "medium"), P())
    return jax.shard_map(
        per_device, mesh=mesh, in_specs=in_specs, out_specs=out_specs, check_vma=False
    )
```

```python
import functools
import math

import jax
import jax.numpy as jnp
import numpy as np
from jax import lax
from jax.experimental import pallas as pl
from jax.experimental.pallas import tpu as pltpu
from jax.sharding import PartitionSpec as P

MESH = pl.DeviceIdType.MESH
f32 = jnp.float32
bf16 = jnp.bfloat16
FRAME = 256
MODES = 4
HALO = 128
STRIP = 32
NX, NY, NZ = 4, 4, 8
ROW_TILES = 16
INTENSITY_FLOOR = 0.1
DAMPING = 4.0


def here():
    w = lax.axis_index("wide")
    m = lax.axis_index("medium")
    n = lax.axis_index("narrow")
    return w // NY, w % NY, (n // 2) * 2 + m, n % 2


def device(x, y, z, c):
    return (x * NY + y, z % 2, (z // 2) * 2 + c)


class Sends:
    def __init__(self, sem):
        self.sem = sem
        self.copies = []

    def start(self, src, dst, recv_sem, target):
        copy = pltpu.make_async_remote_copy(
            src_ref=src,
            dst_ref=dst,
            send_sem=self.sem.at[len(self.copies)],
            recv_sem=recv_sem,
            device_id=target,
            device_id_type=MESH,
        )
        copy.start()
        self.copies.append(copy)

    def arrived(self, dst, recv_sem, source):
        pltpu.make_async_remote_copy(
            src_ref=dst,
            dst_ref=dst,
            send_sem=self.sem.at[0],
            recv_sem=recv_sem,
            device_id=source,
            device_id_type=MESH,
        ).wait_recv()

    def finish(self):
        for copy in self.copies:
            copy.wait_send()


def greet(peers):
    barrier = pltpu.get_barrier_semaphore()
    for peer in peers:
        pl.semaphore_signal(barrier, inc=1, device_id=peer, device_id_type=MESH)


def met(peers):
    pl.semaphore_wait(pltpu.get_barrier_semaphore(), len(peers))


def dft_tables():
    steps = np.arange(FRAME)
    angle = (steps[:, None] * steps[None, :] % FRAME) * (2.0 * math.pi / FRAME)
    cosine = np.cos(angle) / math.sqrt(FRAME)
    sine = np.sin(angle) / math.sqrt(FRAME)
    found = []
    for table in (cosine, cosine + sine, cosine - sine):
        table = table.astype(np.float32)
        high = table.astype(jnp.bfloat16)
        found += [high, (table - high.astype(np.float32)).astype(jnp.bfloat16)]
    return np.stack(found)


def split(x):
    high = x.astype(bf16)
    return high, (x - high.astype(f32)).astype(bf16)


def dot(a, b):
    return jnp.dot(a, b, preferred_element_type=f32)


def side(re, im, product, sign):
    k1 = product(re + im, 0)
    k2 = product(re, 2 if sign > 0 else 4)
    k3 = product(im, 4 if sign > 0 else 2)
    return k1 - k3, k1 - k2


def transform(re, im, tables, sign):
    def right(x, t):
        high, low = split(x)
        return dot(high, tables[t]) + dot(high, tables[t + 1]) + dot(low, tables[t])

    def left(x, t):
        high, low = split(x)
        return dot(tables[t], high) + dot(tables[t], low) + dot(tables[t + 1], high)

    re, im = side(re, im, right, sign)
    return side(re, im, left, sign)


BLOCKS = (0, 6, 2, 7, 1, 3, 5, 4)
N_SENDS = 192


def one_hot(shape, hit):
    return jnp.where(hit(lax.broadcasted_iota(jnp.int32, shape, 0), lax.broadcasted_iota(jnp.int32, shape, 1)), 1.0, 0.0).astype(bf16)


def update_kernel(
    obj, probe_in, amp_in, tables_in, row_in, col_in,
    step_out, probe_out,
    rows_tile, probe, amp, tables, narrowed, far, factor, light, grad, where,
    sib_out, sib_in, total, halo_in, in_four, in_two, in_side, weight, direction, lit,
    probe_part, part_in, part, in1, sum1, in2, sum2, in3, all3, tile, tiles_in,
    send_sem, local_sem, gtwo_sem, gfour_sem, gcorner_sem, gside_sem, gsib_sem, ghalo_sem, gsibhalo_sem, where_sem,
    sib_sem, halo_sem, four_sem, two_sem, side_sem, part_sem, part_send_sem, sem1, send1_sem, sem2, sem3,
    asem3, asem2, asem1, asem0, tile_sem,
):
    x, y, z, c = here()
    m = z % 2
    zh = z // 2
    w = x * NY + y
    n = zh * 2 + c
    xs = [((x + i) % NX) for i in range(NX)]
    ys = [((y + i) % NY) for i in range(NY)]
    zs = [((z + i) % NZ) for i in range(NZ)]
    x_peer = [device(v, y, z, c) for v in xs]
    y_peer = [device(x, v, z, c) for v in ys]
    z_peer = [device(x, y, v, c) for v in zs]
    plane_peer = [((w + i) % ROW_TILES, m, n) for i in range(ROW_TILES)]
    sibling = device(x, y, z, 1 - c)
    wide_up, wide_down = plane_peer[1], plane_peer[15]
    onward = (z_peer[2], z_peer[6])
    behind = (z_peer[6], z_peer[2])
    near_peer = (z_peer[1], z_peer[7])
    sends = Sends(send_sem)

    locals_ = [
        pltpu.make_async_copy(a, b, local_sem.at[i])
        for i, (a, b) in enumerate(
            ((probe_in, probe), (amp_in, amp), (tables_in, tables))
        )
    ]
    for copy in locals_:
        copy.start()
    r0 = row_in[0, 0, 0]
    offset_col = col_in[0, 0, 0]
    c0 = offset_col - HALO * (1 - m)
    lane = lax.broadcasted_iota(jnp.int32, (1, 128), 1)
    where[1, 8 * c + z] = jnp.where(lane == 0, r0, offset_col)
    def beside(row_tile, way):
        return (row_tile % ROW_TILES, m, (zs[2 if way == 0 else 6] // 2) * 2 + c)

    corners = [beside(w + 1, 0), beside(w + 1, 1), beside(w + ROW_TILES - 1, 0), beside(w + ROW_TILES - 1, 1)]
    everyone = [sibling] + plane_peer[1:] + z_peer[1:] + corners
    greet(everyone)
    locals_[0].wait()
    light[...] = jnp.zeros_like(light)

    @pl.loop(0, MODES)
    def _(k):
        light[...] += probe[0, k] * probe[0, k] + probe[1, k] * probe[1, k]

    met(everyone)

    def strip_of(zb, core):
        return (zb // 2) * 2 + core

    own_cols = pl.ds(pl.multiple_of(128 * m, 128), 512)
    side_cols = pl.ds(pl.multiple_of(512 * (1 - m), 128), 128)

    def columns_of(distance):
        return side_cols if distance % 2 else own_cols

    def place(zb, core):
        return pl.ds(pl.multiple_of(HALO + STRIP * strip_of(zb, core), STRIP), STRIP)

    def halo_place(zb, core):
        s = strip_of(zb, core)
        return pl.ds(pl.multiple_of(HALO + STRIP * s + 256 * (1 - 2 * (s // 4)), STRIP), STRIP)

    def towards(zb):
        return (w + ROW_TILES + 2 * (strip_of(zb, c) // 4) - 1) % ROW_TILES

    def pass_on(slot, src=None):
        distance = BLOCKS[slot]
        zb = zs[distance]
        cols = columns_of(distance)
        ref = rows_tile.at[:, place(zb, c), cols]
        if distance != 4:
            sends.start(
                ref if src is None else src,
                rows_tile.at[:, halo_place(zb, c), cols], ghalo_sem.at[slot], (towards(zb), m, n),
            )
        sends.start(ref if src is None else src, ref, gsib_sem.at[slot], sibling)

    mine = where.at[1, pl.ds(8 * c + z, 1)]
    for i in range(1, 8):
        sends.start(mine, mine, where_sem.at[i - 1], z_peer[i])

    rows = place(z, c)
    for plane in range(2):
        for way in range(2):
            p = plane if way == 0 else 1 - plane
            sends.start(
                obj.at[p], rows_tile.at[p, rows, own_cols], gtwo_sem.at[way, p], onward[way]
            )
    pass_on(0, obj)
    out_cols = pl.ds(pl.multiple_of(384 * (1 - m), 128), 128)
    there = pl.ds(pl.multiple_of(512 * m, 128), 128)
    give_cols = pl.ds(pl.multiple_of(384 - 256 * m, 128), 128)
    for way in range(2):
        sends.start(obj.at[:, :, out_cols], rows_tile.at[:, rows, there], gside_sem.at[way, 0], near_peer[way])
    own = pltpu.make_async_copy(obj, rows_tile.at[:, rows, own_cols], local_sem.at[3])
    own.start()
    for way in range(2):
        zb = zs[6 if way == 0 else 2]
        ref = rows_tile.at[way, place(zb, c), own_cols]
        sends.arrived(ref, gtwo_sem.at[way, way], behind[way])
        sends.start(ref, ref, gfour_sem.at[way], onward[way])
    for way in range(2):
        zb = zs[6 if way == 0 else 2]
        sends.start(
            rows_tile.at[way, place(zb, c), own_cols], rows_tile.at[way, halo_place(zb, c), own_cols],
            gcorner_sem.at[way], beside(towards(zb), way),
        )
    for way in range(2):
        zb = zs[6 if way == 0 else 2]
        sends.arrived(rows_tile.at[1 - way, place(zb, c), own_cols], gtwo_sem.at[way, 1 - way], behind[way])
        sends.start(
            rows_tile.at[:, place(zb, c), give_cols], rows_tile.at[:, place(zb, c), there],
            gside_sem.at[way, 1], near_peer[way],
        )
        pass_on(1 + way)
    for step in range(2):
        for way in range(2):
            distance = ((7, 5), (1, 3))[way][step]
            sends.arrived(
                rows_tile.at[:, place(zs[distance], c), side_cols], gside_sem.at[way, step], near_peer[1 - way]
            )
            pass_on(BLOCKS.index(distance))

    for i in range(1, 8):
        sends.arrived(where.at[1, pl.ds(8 * c + zs[8 - i], 1)], where_sem.at[i - 1], z_peer[8 - i])
    half = where.at[1, pl.ds(pl.multiple_of(8 * c, 8), 8)]
    sends.start(half, half, where_sem.at[7], sibling)

    def halo_arrived(slot):
        distance = BLOCKS[slot]
        ref = rows_tile.at[:, halo_place(zs[distance], c), columns_of(distance)]
        sends.arrived(ref, ghalo_sem.at[slot], wide_up)
        sends.start(ref, ref, gsibhalo_sem.at[slot], sibling)

    halo_arrived(0)
    for way in range(2):
        sends.arrived(rows_tile.at[way, place(zs[4], c), own_cols], gfour_sem.at[way], behind[way])
    pass_on(7)
    for slot in range(1, 7):
        halo_arrived(slot)
    sends.arrived(where.at[1, pl.ds(pl.multiple_of(8 * (1 - c), 8), 8)], where_sem.at[7], sibling)
    sends.start(where.at[1], where.at[0], where_sem.at[8], wide_up)
    sends.start(where.at[1], where.at[2], where_sem.at[9], wide_down)
    for slot in range(8):
        distance = BLOCKS[slot]
        sends.arrived(rows_tile.at[:, place(zs[distance], 1 - c), columns_of(distance)], gsib_sem.at[slot], sibling)
    own.wait()

    def on_object(row):
        at = row + (256 * w - HALO)
        return (at >= 0) & (at < 256 * ROW_TILES)

    columns = one_hot((640, FRAME), lambda i, j: i == j + c0)
    lines = one_hot((FRAME, 512), lambda i, j: (j == i + r0) & on_object(j))
    patch = far.at[MODES]

    def narrow(rows):
        for plane in range(2):
            for part, value in enumerate(split(rows_tile[plane, rows])):
                narrowed[plane, part, rows] = dot(value, columns).astype(bf16)

    narrow(slice(HALO, HALO + 256))
    corner_rows = halo_place(zs[4], c)
    for way in range(2):
        sends.arrived(rows_tile.at[way, corner_rows, own_cols], gcorner_sem.at[way], corners[way])
    corner = rows_tile.at[:, corner_rows, own_cols]
    sends.start(corner, corner, gsibhalo_sem.at[7], sibling)
    for slot in range(8):
        distance = BLOCKS[slot]
        sends.arrived(
            rows_tile.at[:, halo_place(zs[distance], 1 - c), columns_of(distance)], gsibhalo_sem.at[slot], sibling
        )
    for copy in locals_[1:]:
        copy.wait()
    narrow(slice(0, HALO))
    narrow(slice(HALO + 256, 512))
    for plane in range(2):
        patch[FRAME * plane : FRAME * (plane + 1)] = dot(lines, narrowed[plane, 0]) + dot(lines, narrowed[plane, 1])

    pr, pi = patch[:FRAME], patch[FRAME:]
    for k in range(MODES):
        a, b = probe[0, k], probe[1, k]
        fre, fim = transform(a * pr - b * pi, a * pi + b * pr, tables, 1)
        far[k, :FRAME] = fre
        far[k, FRAME:] = fim
        squares = fre * fre + fim * fim
        factor[...] = squares if k == 0 else factor[...] + squares

    factor[...] = amp[...] / jnp.sqrt(jnp.maximum(factor[...], INTENSITY_FLOOR)) - 1.0

    def part_copy(k):
        return pltpu.make_async_remote_copy(
            src_ref=probe_part.at[1 - c, k], dst_ref=part_in.at[k],
            send_sem=part_send_sem.at[k], recv_sem=part_sem.at[k],
            device_id=sibling, device_id_type=MESH,
        )

    def first_copy(k, i):
        h = k % 2
        tx, ty = (x + i * h) % NX, (y + i * (1 - h)) % NY
        q = h * tx + (1 - h) * ty
        return pltpu.make_async_remote_copy(
            src_ref=part.at[k, pl.ds(pl.multiple_of(64 * q, 64), 64)], dst_ref=in1.at[k, i - 1],
            send_sem=send1_sem.at[k, i - 1], recv_sem=sem1.at[k, i - 1],
            device_id=(tx * NY + ty, m, n), device_id_type=MESH,
        )

    def take_part(k):
        part_copy(k).wait_recv()
        part[k] = part_in[k] + probe_part[c, k]
        for i in range(1, 4):
            first_copy(k, i).start()

    for k in range(MODES):
        scale = factor[...]
        cre, cim = transform(far[k, :FRAME] * scale, far[k, FRAME:] * scale, tables, -1)
        a, b = probe[0, k], probe[1, k]
        pr, pi = patch[:FRAME], patch[FRAME:]
        probe_part[0, k] = pr * cre + pi * cim
        probe_part[1, k] = pr * cim - pi * cre
        part_copy(k).start()
        gre, gim = a * cre + b * cim, a * cim - b * cre
        grad[0] = gre if k == 0 else grad[0] + gre
        grad[1] = gim if k == 0 else grad[1] + gim
        if k > 0:
            take_part(k - 1)

    def ways(k):
        if k % 2 == 0:
            return y, ys, y_peer, x, xs, x_peer
        return x, xs, x_peer, y, ys, y_peer

    def second_stage(k):
        first, _, _, _, theirs, peers = ways(k)
        rows = pl.ds(pl.multiple_of(64 * first, 64), 64)
        for i in range(1, 4):
            first_copy(k, i).wait_recv()
        sum1[k] = part[k, rows] + in1[k, 0] + in1[k, 1] + in1[k, 2]
        for i in range(1, 4):
            sends.start(
                sum1.at[k, pl.ds(pl.multiple_of(16 * theirs[i], 16), 16)],
                in2.at[k, i - 1], sem2.at[k, i - 1], peers[i],
            )

    def z_tile(pair, v):
        return (
            2 * pair + v // 4,
            pl.ds(pl.multiple_of(8 * ((v // 2) % 2), 8), 8),
            pl.ds(pl.multiple_of(128 * (v % 2), 128), 128),
        )

    def third_send(pair):
        for k in (2 * pair, 2 * pair + 1):
            _, _, _, second, _, peers = ways(k)
            for i in range(1, 4):
                sends.arrived(in2.at[k, i - 1], sem2.at[k, i - 1], peers[4 - i])
            rows = pl.ds(pl.multiple_of(16 * second, 16), 16)
            sum2[k] = sum1[k, rows] + in2[k, 0] + in2[k, 1] + in2[k, 2]
        for i in range(1, 8):
            sends.start(sum2.at[z_tile(pair, zs[i])], in3.at[pair, i - 1], sem3.at[pair, i - 1], z_peer[i])

    def third_sum(pair):
        for i in range(1, 8):
            sends.arrived(in3.at[pair, i - 1], sem3.at[pair, i - 1], z_peer[8 - i])
        whole = sum2[z_tile(pair, z)]
        for i in range(1, 8):
            whole = whole + in3[pair, i - 1]
        all3[z_tile(pair, z)] = whole
        for i in range(1, 8):
            ref = all3.at[z_tile(pair, z)]
            sends.start(ref, ref, asem3.at[pair, i - 1], z_peer[i])

    def out_rows(first, second, count):
        return pl.ds(pl.multiple_of(64 * first + 16 * second, 16), count)

    def back_second(pair):
        for i in range(1, 8):
            sends.arrived(all3.at[z_tile(pair, zs[8 - i])], asem3.at[pair, i - 1], z_peer[8 - i])
        for k in (2 * pair, 2 * pair + 1):
            first, _, _, second, _, peers = ways(k)
            rows = out_rows(first, second, 16)
            for i in range(1, 4):
                sends.start(all3.at[k], probe_out.at[c, k, rows], asem2.at[k, i - 1], peers[i])
            probe_out[c, k, rows] = all3[k]

    def back_first(pair):
        for k in (2 * pair, 2 * pair + 1):
            first, _, first_peers, _, theirs, peers = ways(k)
            for i in range(1, 4):
                ref = probe_out.at[c, k, out_rows(first, theirs[4 - i], 16)]
                sends.arrived(ref, asem2.at[k, i - 1], peers[4 - i])
            ref = probe_out.at[c, k, out_rows(first, 0, 64)]
            for i in range(1, 4):
                sends.start(ref, ref, asem1.at[k, i - 1], first_peers[i])
            sends.start(ref, ref, asem0.at[k, 0], sibling)

    def hand_over(pair):
        for k in (2 * pair, 2 * pair + 1):
            _, theirs, peers, _, _, _ = ways(k)
            for i in range(1, 4):
                ref = probe_out.at[c, k, out_rows(theirs[4 - i], 0, 64)]
                sends.arrived(ref, asem1.at[k, i - 1], peers[4 - i])
                sends.start(ref, ref, asem0.at[k, i], sibling)

    columns_back = one_hot((FRAME, 640), lambda i, j: j == i + c0)

    gradient_parts = split(jnp.concatenate([grad[0], grad[1]], axis=1))

    def put(core, dst, rims):
        strips = (0, 1, 6, 7) if rims else (2, 3, 4, 5)

        def hit(i, j):
            q = i // STRIP
            strip = q + 4 * (q // 2) if rims else q + 2
            return 64 * strip + STRIP * core + i % STRIP == j + r0

        lines_back = one_hot((128, FRAME), hit)
        found = 0.0
        for value in gradient_parts:
            rows = dot(lines_back, value).astype(bf16)
            found = found + dot(jnp.concatenate([rows[:, :FRAME], rows[:, FRAME:]], axis=0), columns_back)
        for plane in range(2):
            for q in range(4):
                dst[strips[q], plane] = found[128 * plane + STRIP * q : 128 * plane + STRIP * (q + 1)]

    def sib_send(k):
        both = pl.ds(2 * k, 2)
        sends.start(sib_out.at[both], sib_in.at[both], sib_sem.at[k], sibling)

    def sib_add(k):
        both = pl.ds(2 * k, 2)
        sends.arrived(sib_in.at[both], sib_sem.at[k], sibling)
        total[both] += sib_in[both]

    early = zh % 2
    put(1 - c, sib_out, True)
    sib_send(0)
    sib_send(3)
    second_stage(0)
    put(c, total, True)
    put(1 - c, sib_out, False)
    sib_send(1)
    sib_send(2)
    sib_add(0)
    sib_add(3)
    for i in (early, 1 - early):
        sends.start(total.at[i], halo_in.at[0, i], halo_sem.at[0, i], wide_down)
        sends.start(total.at[6 + i], halo_in.at[1, i], halo_sem.at[1, i], wide_up)
    take_part(3)
    second_stage(1)
    put(c, total, False)
    sib_add(1)
    sib_add(2)
    third_send(0)

    weight[...] = jnp.zeros_like(weight)

    def lamp(t):
        light_high, light_low = split(light[...])
        a = w - 1 + t
        real = (a >= 0) & (a < ROW_TILES)
        shape = (16, STRIP, FRAME)
        rs = STRIP * n + 256 * (1 - t) + HALO - where[t][:, :, 0:1]
        hit = (lax.broadcasted_iota(jnp.int32, shape, 2) == lax.broadcasted_iota(jnp.int32, shape, 1) + rs) & real
        lines = jnp.where(hit, 1.0, 0.0).reshape((16 * STRIP, FRAME)).astype(bf16)
        lit[:, 0] = dot(lines, light_high).astype(bf16).reshape(shape)
        lit[:, 1] = dot(lines, light_low).astype(bf16).reshape(shape)

        def add(i, b, first, width):
            at = 8 * (i // 4) + 2 * (i % 4) + b
            cs = 512 * (m - b) + first + HALO - where[t, at][:, 1:2]
            columns = one_hot((FRAME, width), lambda p, q: p == q + cs)
            found = dot(lit[at].reshape((2 * STRIP, FRAME)), columns)
            return found[:STRIP] + found[STRIP:]

        @pl.loop(0, 8)
        def _(i):
            weight[...] += add(i, m, 0, 512)
            weight[:, out_cols] += add(i, 1 - m, 384 * (1 - m), 128)

    lamp(1)
    sends.arrived(where.at[0], where_sem.at[8], wide_down)

    def take_halo(i):
        for side in range(2):
            real = (w < ROW_TILES - 1) if side == 0 else (w > 0)
            sends.arrived(halo_in.at[side, i], halo_sem.at[side, i], wide_up if side == 0 else wide_down)
            total[(4 if side == 0 else 2) + i] += jnp.where(real, halo_in[side, i], 0.0)

    def block(zb):
        return total.at[2 + zb // 2, :, :, own_cols]

    second_stage(2)
    second_stage(3)
    take_halo(early)
    for way in range(2):
        sends.start(block(zs[4]).at[way], in_four.at[way], four_sem.at[way], onward[way])
    third_sum(0)
    third_send(1)
    take_halo(1 - early)
    for way in range(2):
        for step in range(2):
            distance = ((1, 3), (7, 5))[way][step]
            sends.start(
                total.at[2 + zs[distance] // 2, :, :, side_cols], in_side.at[way, step], side_sem.at[way, step],
                near_peer[way],
            )
    lamp(0)
    sends.arrived(where.at[2], where_sem.at[9], wide_up)
    near = pl.ds(pl.multiple_of(384 - 256 * m, 128), 128)
    for way in range(2):
        sends.arrived(in_side.at[way, 1], side_sem.at[way, 1], near_peer[1 - way])
        zb = zs[2 if way == 0 else 6]
        total[2 + zb // 2, :, :, near] += in_side[way, 1]
        sends.start(block(zb).at[1 - way], in_two.at[way, 1 - way], two_sem.at[way, 1 - way], onward[way])
    for way in range(2):
        sends.arrived(in_four.at[way], four_sem.at[way], behind[way])
        in_four[way] += block(zs[2 if way == 0 else 6])[way]
        sends.start(in_four.at[way], in_two.at[way, way], two_sem.at[way, way], onward[way])
    back_second(0)
    third_sum(1)
    lamp(2)
    back_first(0)
    back_second(1)

    for way in range(2):
        sends.arrived(in_side.at[way, 0], side_sem.at[way, 0], near_peer[1 - way])
    total[2 + zh, :, :, near] += in_side[0, 0] + in_side[1, 0]
    for way in range(2):
        for plane in range(2):
            sends.arrived(in_two.at[way, plane], two_sem.at[way, plane], behind[way])
    numerator = jnp.zeros((), f32)
    under = 1.0 / (weight[...] + DAMPING)
    squares = jnp.zeros((STRIP, 512), f32)
    for plane in range(2):
        strip = total[2 + zh, plane, :, own_cols] + in_two[0, plane] + in_two[1, plane]
        step = strip * under
        direction[plane] = step
        numerator += jnp.sum(step * strip)
        squares += step * step
    denominator = jnp.sum(squares * weight[...])
    line = lax.broadcasted_iota(jnp.int32, (8, 128), 0)
    tile[0] = jnp.where(line == 0, numerator, denominator)

    def tile_send(stage, peers, first):
        for i in range(1, len(peers)):
            sends.start(tile.at[stage], tiles_in.at[first + i - 1], tile_sem.at[first + i - 1], peers[i])

    def tile_sum(stage, peers, first):
        for i in range(1, len(peers)):
            sends.arrived(tiles_in.at[first + i - 1], tile_sem.at[first + i - 1], peers[len(peers) - i])
        found = tile[stage]
        for i in range(1, len(peers)):
            found = found + tiles_in[first + i - 1]
        tile[stage + 1] = found

    tile_send(0, [None, sibling], 0)
    tile_sum(0, [None, sibling], 0)
    tile_send(1, plane_peer, 1)
    back_first(1)
    hand_over(0)
    tile_sum(1, plane_peer, 1)
    tile_send(2, z_peer, 16)
    hand_over(1)
    tile_sum(2, z_peer, 16)
    sums = tile[3]
    alpha = sums[0:1, 0:1] / sums[1:2, 0:1]
    step_out[...] = direction[...] * alpha
    for k in range(MODES):
        _, theirs, _, _, _, _ = ways(k)
        for i in range(4):
            sends.arrived(probe_out.at[1 - c, k, out_rows(theirs[(4 - i) % 4], 0, 64)], asem0.at[k, i], sibling)
    for k in range(MODES):
        part_copy(k).wait_send()
        for i in range(1, 4):
            first_copy(k, i).wait_send()
    sends.finish()


def hand_out_kernel(step_in, probe_in, step_out, probe_out, sem):
    copies = [pltpu.make_async_copy(step_in, step_out, sem.at[0])]
    for plane in range(2):
        copies.append(pltpu.make_async_copy(probe_in.at[plane], probe_out.at[plane], sem.at[1 + plane]))
    for copy in copies:
        copy.start()
    for copy in copies:
        copy.wait()


VMEM = pl.BlockSpec(memory_space=pltpu.VMEM)
SMEM = pl.BlockSpec(memory_space=pltpu.SMEM)
ANY = pl.BlockSpec(memory_space=pl.ANY)
DMA = pltpu.SemaphoreType.DMA


def update(obj, probe, amp, tables, row, col):
    v = lambda *shape: pltpu.VMEM(shape, f32)
    return pl.pallas_call(
        update_kernel,
        out_shape=[
            pltpu.VMEM((2, STRIP, 512), f32),
            pltpu.VMEM((2, MODES, FRAME, FRAME), f32),
        ],
        in_specs=[ANY, ANY, ANY, ANY, SMEM, SMEM],
        out_specs=[VMEM, VMEM],
        scratch_shapes=[
            v(2, 512, 640),
            v(2, MODES, FRAME, FRAME),
            v(FRAME, FRAME),
            pltpu.VMEM((6, FRAME, FRAME), bf16),
            pltpu.VMEM((2, 2, 512, FRAME), bf16),
            v(MODES + 1, 512, FRAME),
            v(FRAME, FRAME),
            v(FRAME, FRAME),
            v(2, FRAME, FRAME),
            pltpu.VMEM((3, 16, 1, 128), jnp.int32),
            v(8, 2, STRIP, 640),
            v(8, 2, STRIP, 640),
            v(8, 2, STRIP, 640),
            v(2, 2, 2, STRIP, 640),
            v(2, STRIP, 512),
            v(2, 2, STRIP, 512),
            v(2, 2, 2, STRIP, 128),
            v(STRIP, 512),
            v(2, STRIP, 512),
            pltpu.VMEM((16, 2, STRIP, FRAME), bf16),
            v(2, MODES, FRAME, FRAME),
            v(MODES, FRAME, FRAME),
            v(MODES, FRAME, FRAME),
            v(MODES, 3, 64, FRAME),
            v(MODES, 64, FRAME),
            v(MODES, 3, 16, FRAME),
            v(MODES, 16, FRAME),
            v(2, 7, 8, 128),
            v(MODES, 16, FRAME),
            v(4, 8, 128),
            v(23, 8, 128),
            DMA((N_SENDS,)),
            DMA((4,)),
            DMA((2, 2)),
            DMA((2,)),
            DMA((2,)),
            DMA((2, 2)),
            DMA((8,)),
            DMA((8,)),
            DMA((8,)),
            DMA((10,)),
            DMA((4,)),
            DMA((2, 2)),
            DMA((2,)),
            DMA((2, 2)),
            DMA((2, 2)),
            DMA((MODES,)),
            DMA((MODES,)),
            DMA((MODES, 3)),
            DMA((MODES, 3)),
            DMA((MODES, 3)),
            DMA((2, 7)),
            DMA((2, 7)),
            DMA((MODES, 3)),
            DMA((MODES, 3)),
            DMA((MODES, 4)),
            DMA((23,)),
        ],
        compiler_params=pltpu.CompilerParams(
            collective_id=0, has_side_effects=True, vmem_limit_bytes=56 * 2**20
        ),
    )(obj, probe, amp, tables, row, col)


def hand_out(step, gradient):
    return pl.pallas_call(
        hand_out_kernel,
        out_shape=[jax.ShapeDtypeStruct(step.shape, f32), jax.ShapeDtypeStruct(gradient.shape, f32)],
        in_specs=[ANY, ANY],
        out_specs=[ANY, ANY],
        scratch_shapes=[DMA((3,))],
    )(step, gradient)


def per_device(obj_tile, probe, amplitude, row_offsets, col_offsets):
    step, gradient = update(
        obj_tile, probe, amplitude.reshape((FRAME, FRAME)), jnp.asarray(dft_tables()), row_offsets, col_offsets
    )
    return hand_out(step, gradient)


def solution(mesh):
    in_specs = (
        P(None, ("wide", "narrow"), "medium"),
        P(),
        P("wide", "medium", "narrow", None, None),
        P("wide", "medium", "narrow"),
        P("wide", "medium", "narrow"),
    )
    out_specs = (P(None, ("wide", "narrow"), "medium"), P())
    return jax.shard_map(
        per_device, mesh=mesh, in_specs=in_specs, out_specs=out_specs, check_vma=False
    )
```

```python
import functools
import math

import jax
import jax.numpy as jnp
import numpy as np
from jax import lax
from jax.experimental import pallas as pl
from jax.experimental.pallas import tpu as pltpu
from jax.sharding import PartitionSpec as P

MESH = pl.DeviceIdType.MESH
f32 = jnp.float32
bf16 = jnp.bfloat16
FRAME = 256
MODES = 4
HALO = 128
STRIP = 32
NX, NY, NZ = 4, 4, 8
ROW_TILES = 16
INTENSITY_FLOOR = 0.1
DAMPING = 4.0


def here():
    w = lax.axis_index("wide")
    m = lax.axis_index("medium")
    n = lax.axis_index("narrow")
    return w // NY, w % NY, (n // 2) * 2 + m, n % 2


def device(x, y, z, c):
    return (x * NY + y, z % 2, (z // 2) * 2 + c)


class Sends:
    def __init__(self, sem):
        self.sem = sem
        self.copies = []
        self.waited = 0

    def start(self, src, dst, recv_sem, target):
        copy = pltpu.make_async_remote_copy(
            src_ref=src,
            dst_ref=dst,
            send_sem=self.sem.at[len(self.copies)],
            recv_sem=recv_sem,
            device_id=target,
            device_id_type=MESH,
        )
        copy.start()
        self.copies.append(copy)

    def arrived(self, dst, recv_sem, source):
        pltpu.make_async_remote_copy(
            src_ref=dst,
            dst_ref=dst,
            send_sem=self.sem.at[0],
            recv_sem=recv_sem,
            device_id=source,
            device_id_type=MESH,
        ).wait_recv()

    def drain(self, count):
        for copy in self.copies[self.waited : count]:
            copy.wait_send()
        self.waited = max(self.waited, count)

    def mark(self):
        return len(self.copies)

    def finish(self):
        self.drain(len(self.copies))


def greet(peers):
    barrier = pltpu.get_barrier_semaphore()
    for peer in peers:
        pl.semaphore_signal(barrier, inc=1, device_id=peer, device_id_type=MESH)


def met(peers):
    pl.semaphore_wait(pltpu.get_barrier_semaphore(), len(peers))


def dft_tables():
    steps = np.arange(FRAME)
    angle = (steps[:, None] * steps[None, :] % FRAME) * (2.0 * math.pi / FRAME)
    cosine = np.cos(angle) / math.sqrt(FRAME)
    sine = np.sin(angle) / math.sqrt(FRAME)
    found = []
    for table in (cosine, cosine + sine, cosine - sine):
        table = table.astype(np.float32)
        high = table.astype(jnp.bfloat16)
        found += [high, (table - high.astype(np.float32)).astype(jnp.bfloat16)]
    return np.stack(found)


def split(x):
    high = x.astype(bf16)
    return high, (x - high.astype(f32)).astype(bf16)


def dot(a, b):
    return jnp.dot(a, b, preferred_element_type=f32)


def side(re, im, product, sign):
    k1 = product(re + im, 0)
    k2 = product(re, 2 if sign > 0 else 4)
    k3 = product(im, 4 if sign > 0 else 2)
    return k1 - k3, k1 - k2


def transform(re, im, tables, sign):
    def right(x, t):
        high, low = split(x)
        return dot(high, tables[t]) + dot(high, tables[t + 1]) + dot(low, tables[t])

    def left(x, t):
        high, low = split(x)
        return dot(tables[t], high) + dot(tables[t], low) + dot(tables[t + 1], high)

    re, im = side(re, im, right, sign)
    return side(re, im, left, sign)


BLOCKS = (0, 6, 2, 7, 1, 3, 5, 4)
N_SENDS = 192


def one_hot(shape, hit):
    return jnp.where(hit(lax.broadcasted_iota(jnp.int32, shape, 0), lax.broadcasted_iota(jnp.int32, shape, 1)), 1.0, 0.0).astype(bf16)


def pick_columns(x, table):
    high, low = split(x)
    return dot(high, table) + dot(low, table)


def pick_rows(table, x):
    high, low = split(x)
    return dot(table, high) + dot(table, low)


def update_kernel(
    obj, probe_in, amp_in, tables_in, row_in, col_in,
    step_out, probe_out,
    rows_tile, probe, amp, tables, narrowed, far, factor, light, grad, where,
    sib_out, sib_in, total, halo_in, in_four, in_two, in_side, in_far, weight, direction, lit,
    probe_part, part_in, part, in1, sum1, in2, sum2, in3, all3, tile, tiles_in,
    send_sem, local_sem, gtwo_sem, gfour_sem, gside_sem, gsib_sem, ghalo_sem, gsibhalo_sem, where_sem,
    sib_sem, halo_sem, four_sem, two_sem, side_sem, far_sem, part_sem, part_send_sem, sem1, send1_sem, sem2, sem3,
    asem3, asem2, asem1, asem0, tile_sem,
):
    x, y, z, c = here()
    m = z % 2
    zh = z // 2
    w = x * NY + y
    n = zh * 2 + c
    xs = [((x + i) % NX) for i in range(NX)]
    ys = [((y + i) % NY) for i in range(NY)]
    zs = [((z + i) % NZ) for i in range(NZ)]
    x_peer = [device(v, y, z, c) for v in xs]
    y_peer = [device(x, v, z, c) for v in ys]
    z_peer = [device(x, y, v, c) for v in zs]
    plane_peer = [((w + i) % ROW_TILES, m, n) for i in range(ROW_TILES)]
    sibling = device(x, y, z, 1 - c)
    wide_up, wide_down = plane_peer[1], plane_peer[15]
    onward = (z_peer[2], z_peer[6])
    behind = (z_peer[6], z_peer[2])
    near_peer = (z_peer[1], z_peer[7])
    sends = Sends(send_sem)

    everyone = [sibling] + plane_peer[1:] + z_peer[1:]
    greet(everyone)
    locals_ = [
        pltpu.make_async_copy(a, b, local_sem.at[i])
        for i, (a, b) in enumerate(
            ((probe_in, probe), (amp_in, amp), (tables_in, tables))
        )
    ]
    for copy in locals_:
        copy.start()
    r0 = row_in[0, 0, 0]
    offset_col = col_in[0, 0, 0]
    c0 = offset_col - HALO * (1 - m)
    lane = lax.broadcasted_iota(jnp.int32, (1, 128), 1)
    where[1, 8 * c + z] = jnp.where(lane == 0, r0, offset_col)
    met(everyone)

    def strip_of(zb, core):
        return (zb // 2) * 2 + core

    own_cols = pl.ds(pl.multiple_of(128 * m, 128), 512)
    side_cols = pl.ds(pl.multiple_of(512 * (1 - m), 128), 128)

    def columns_of(distance):
        return side_cols if distance % 2 else own_cols

    def place(zb, core):
        return pl.ds(pl.multiple_of(HALO + STRIP * strip_of(zb, core), STRIP), STRIP)

    def halo_place(zb, core):
        s = strip_of(zb, core)
        return pl.ds(pl.multiple_of(HALO + STRIP * s + 256 * (1 - 2 * (s // 4)), STRIP), STRIP)

    def pass_on(slot, src=None):
        distance = BLOCKS[slot]
        zb = zs[distance]
        cols = columns_of(distance)
        ref = rows_tile.at[:, place(zb, c), cols]
        towards = (w + ROW_TILES + 2 * (strip_of(zb, c) // 4) - 1) % ROW_TILES
        sends.start(
            ref if src is None else src,
            rows_tile.at[:, halo_place(zb, c), cols], ghalo_sem.at[slot], (towards, m, n),
        )
        sends.start(ref if src is None else src, ref, gsib_sem.at[slot], sibling)

    mine = where.at[1, pl.ds(8 * c + z, 1)]
    for i in range(1, 8):
        sends.start(mine, mine, where_sem.at[i - 1], z_peer[i])

    rows = place(z, c)
    for plane in range(2):
        for way in range(2):
            p = plane if way == 0 else 1 - plane
            sends.start(
                obj.at[p], rows_tile.at[p, rows, own_cols], gtwo_sem.at[way, p], onward[way]
            )
    pass_on(0, obj)
    out_cols = pl.ds(pl.multiple_of(384 * (1 - m), 128), 128)
    there = pl.ds(pl.multiple_of(512 * m, 128), 128)
    give_cols = pl.ds(pl.multiple_of(384 - 256 * m, 128), 128)
    for way in range(2):
        sends.start(obj.at[:, :, out_cols], rows_tile.at[:, rows, there], gside_sem.at[way, 0], near_peer[way])
    own = pltpu.make_async_copy(obj, rows_tile.at[:, rows, own_cols], local_sem.at[3])
    own.start()
    locals_[0].wait()
    light[...] = jnp.zeros_like(light)

    @pl.loop(0, MODES)
    def _(k):
        light[...] += probe[0, k] * probe[0, k] + probe[1, k] * probe[1, k]

    for way in range(2):
        zb = zs[6 if way == 0 else 2]
        ref = rows_tile.at[way, place(zb, c), own_cols]
        sends.arrived(ref, gtwo_sem.at[way, way], behind[way])
        sends.start(ref, ref, gfour_sem.at[way], onward[way])
    for way in range(2):
        zb = zs[6 if way == 0 else 2]
        sends.arrived(rows_tile.at[1 - way, place(zb, c), own_cols], gtwo_sem.at[way, 1 - way], behind[way])
        sends.start(
            rows_tile.at[:, place(zb, c), give_cols], rows_tile.at[:, place(zb, c), there],
            gside_sem.at[way, 1], near_peer[way],
        )
        pass_on(1 + way)
    for step in range(2):
        for way in range(2):
            distance = ((7, 5), (1, 3))[way][step]
            sends.arrived(
                rows_tile.at[:, place(zs[distance], c), side_cols], gside_sem.at[way, step], near_peer[1 - way]
            )
            pass_on(BLOCKS.index(distance))

    for i in range(1, 8):
        sends.arrived(where.at[1, pl.ds(8 * c + zs[8 - i], 1)], where_sem.at[i - 1], z_peer[8 - i])
    half = where.at[1, pl.ds(pl.multiple_of(8 * c, 8), 8)]
    sends.start(half, half, where_sem.at[7], sibling)

    def halo_arrived(slot):
        distance = BLOCKS[slot]
        ref = rows_tile.at[:, halo_place(zs[distance], c), columns_of(distance)]
        sends.arrived(ref, ghalo_sem.at[slot], wide_up)
        sends.start(ref, ref, gsibhalo_sem.at[slot], sibling)

    halo_arrived(0)
    for way in range(2):
        sends.arrived(rows_tile.at[way, place(zs[4], c), own_cols], gfour_sem.at[way], behind[way])
    pass_on(7)
    for slot in range(1, 7):
        halo_arrived(slot)
    sends.arrived(where.at[1, pl.ds(pl.multiple_of(8 * (1 - c), 8), 8)], where_sem.at[7], sibling)
    sends.start(where.at[1], where.at[0], where_sem.at[8], wide_up)
    sends.start(where.at[1], where.at[2], where_sem.at[9], wide_down)
    for slot in range(8):
        distance = BLOCKS[slot]
        sends.arrived(rows_tile.at[:, place(zs[distance], 1 - c), columns_of(distance)], gsib_sem.at[slot], sibling)
    own.wait()

    def on_object(row):
        at = row + (256 * w - HALO)
        return (at >= 0) & (at < 256 * ROW_TILES)

    columns = one_hot((640, FRAME), lambda i, j: i == j + c0)
    lines = one_hot((FRAME, 512), lambda i, j: (j == i + r0) & on_object(j))
    patch = far.at[MODES]

    def narrow(rows):
        for plane in range(2):
            for part, value in enumerate(split(rows_tile[plane, rows])):
                narrowed[plane, part, rows] = dot(value, columns).astype(bf16)

    narrow(slice(HALO, HALO + 256))
    halo_arrived(7)
    for slot in range(8):
        distance = BLOCKS[slot]
        sends.arrived(
            rows_tile.at[:, halo_place(zs[distance], 1 - c), columns_of(distance)], gsibhalo_sem.at[slot], sibling
        )
    for copy in locals_[1:]:
        copy.wait()
    narrow(slice(0, HALO))
    narrow(slice(HALO + 256, 512))
    for plane in range(2):
        patch[FRAME * plane : FRAME * (plane + 1)] = dot(lines, narrowed[plane, 0]) + dot(lines, narrowed[plane, 1])

    pr, pi = patch[:FRAME], patch[FRAME:]
    for k in range(MODES):
        a, b = probe[0, k], probe[1, k]
        fre, fim = transform(a * pr - b * pi, a * pi + b * pr, tables, 1)
        far[k, :FRAME] = fre
        far[k, FRAME:] = fim
        squares = fre * fre + fim * fim
        factor[...] = squares if k == 0 else factor[...] + squares

    factor[...] = amp[...] / jnp.sqrt(jnp.maximum(factor[...], INTENSITY_FLOOR)) - 1.0

    def part_copy(k):
        return pltpu.make_async_remote_copy(
            src_ref=probe_part.at[1 - c, k], dst_ref=part_in.at[k],
            send_sem=part_send_sem.at[k], recv_sem=part_sem.at[k],
            device_id=sibling, device_id_type=MESH,
        )

    def first_copy(k, i):
        h = k % 2
        tx, ty = (x + i * h) % NX, (y + i * (1 - h)) % NY
        q = h * tx + (1 - h) * ty
        return pltpu.make_async_remote_copy(
            src_ref=part.at[k, pl.ds(pl.multiple_of(64 * q, 64), 64)], dst_ref=in1.at[k, i - 1],
            send_sem=send1_sem.at[k, i - 1], recv_sem=sem1.at[k, i - 1],
            device_id=(tx * NY + ty, m, n), device_id_type=MESH,
        )

    def take_part(k):
        part_copy(k).wait_recv()
        part[k] = part_in[k] + probe_part[c, k]
        for i in range(1, 4):
            first_copy(k, i).start()

    for k in range(MODES):
        scale = factor[...]
        cre, cim = transform(far[k, :FRAME] * scale, far[k, FRAME:] * scale, tables, -1)
        a, b = probe[0, k], probe[1, k]
        pr, pi = patch[:FRAME], patch[FRAME:]
        probe_part[0, k] = pr * cre + pi * cim
        probe_part[1, k] = pr * cim - pi * cre
        part_copy(k).start()
        gre, gim = a * cre + b * cim, a * cim - b * cre
        grad[0] = gre if k == 0 else grad[0] + gre
        grad[1] = gim if k == 0 else grad[1] + gim
        if k > 0:
            take_part(k - 1)

    def ways(k):
        if k % 2 == 0:
            return y, ys, y_peer, x, xs, x_peer
        return x, xs, x_peer, y, ys, y_peer

    def second_stage(k):
        first, _, _, _, theirs, peers = ways(k)
        rows = pl.ds(pl.multiple_of(64 * first, 64), 64)
        for i in range(1, 4):
            first_copy(k, i).wait_recv()
        sum1[k] = part[k, rows] + in1[k, 0] + in1[k, 1] + in1[k, 2]
        for i in range(1, 4):
            sends.start(
                sum1.at[k, pl.ds(pl.multiple_of(16 * theirs[i], 16), 16)],
                in2.at[k, i - 1], sem2.at[k, i - 1], peers[i],
            )

    def z_tile(pair, v):
        return (
            2 * pair + v // 4,
            pl.ds(pl.multiple_of(8 * ((v // 2) % 2), 8), 8),
            pl.ds(pl.multiple_of(128 * (v % 2), 128), 128),
        )

    def third_send(pair):
        for k in (2 * pair, 2 * pair + 1):
            _, _, _, second, _, peers = ways(k)
            for i in range(1, 4):
                sends.arrived(in2.at[k, i - 1], sem2.at[k, i - 1], peers[4 - i])
            rows = pl.ds(pl.multiple_of(16 * second, 16), 16)
            sum2[k] = sum1[k, rows] + in2[k, 0] + in2[k, 1] + in2[k, 2]
        for i in range(1, 8):
            sends.start(sum2.at[z_tile(pair, zs[i])], in3.at[pair, i - 1], sem3.at[pair, i - 1], z_peer[i])

    def third_sum(pair):
        for i in range(1, 8):
            sends.arrived(in3.at[pair, i - 1], sem3.at[pair, i - 1], z_peer[8 - i])
        whole = sum2[z_tile(pair, z)]
        for i in range(1, 8):
            whole = whole + in3[pair, i - 1]
        all3[z_tile(pair, z)] = whole
        for i in range(1, 8):
            ref = all3.at[z_tile(pair, z)]
            sends.start(ref, ref, asem3.at[pair, i - 1], z_peer[i])

    def out_rows(first, second, count):
        return pl.ds(pl.multiple_of(64 * first + 16 * second, 16), count)

    def back_second(pair):
        for i in range(1, 8):
            sends.arrived(all3.at[z_tile(pair, zs[8 - i])], asem3.at[pair, i - 1], z_peer[8 - i])
        for k in (2 * pair, 2 * pair + 1):
            first, _, _, second, _, peers = ways(k)
            rows = out_rows(first, second, 16)
            for i in range(1, 4):
                sends.start(all3.at[k], probe_out.at[c, k, rows], asem2.at[k, i - 1], peers[i])
            probe_out[c, k, rows] = all3[k]

    def back_first(pair):
        for k in (2 * pair, 2 * pair + 1):
            first, _, first_peers, _, theirs, peers = ways(k)
            for i in range(1, 4):
                ref = probe_out.at[c, k, out_rows(first, theirs[4 - i], 16)]
                sends.arrived(ref, asem2.at[k, i - 1], peers[4 - i])
            ref = probe_out.at[c, k, out_rows(first, 0, 64)]
            for i in range(1, 4):
                sends.start(ref, ref, asem1.at[k, i - 1], first_peers[i])
            sends.start(ref, ref, asem0.at[k, 0], sibling)

    def hand_over(pair):
        for k in (2 * pair, 2 * pair + 1):
            _, theirs, peers, _, _, _ = ways(k)
            for i in range(1, 4):
                ref = probe_out.at[c, k, out_rows(theirs[4 - i], 0, 64)]
                sends.arrived(ref, asem1.at[k, i - 1], peers[4 - i])
                sends.start(ref, ref, asem0.at[k, i], sibling)

    columns_back = one_hot((FRAME, 640), lambda i, j: j == i + c0)

    def put(core, dst):
        lines_back = one_hot(
            (FRAME, FRAME), lambda i, j: 64 * (i // STRIP) + STRIP * core + i % STRIP == j + r0
        )
        for plane in range(2):
            found = pick_columns(pick_rows(lines_back, grad[plane]), columns_back)
            for j in range(8):
                dst[j, plane] = found[STRIP * j : STRIP * (j + 1)]

    gathered = sends.mark()
    put(1 - c, sib_out)
    for k in (0, 3, 1, 2):
        both = pl.ds(2 * k, 2)
        sends.start(sib_out.at[both], sib_in.at[both], sib_sem.at[k], sibling)
    take_part(3)
    put(c, total)
    second_stage(0)
    early = zh % 2
    for k in (0, 3, 1, 2):
        both = pl.ds(2 * k, 2)
        sends.arrived(sib_in.at[both], sib_sem.at[k], sibling)
        total[both] += sib_in[both]
        if k == 3:
            for i in (early, 1 - early):
                sends.start(total.at[i], halo_in.at[0, i], halo_sem.at[0, i], wide_down)
                sends.start(total.at[6 + i], halo_in.at[1, i], halo_sem.at[1, i], wide_up)
    second_stage(1)

    weight[...] = jnp.zeros_like(weight)

    def lamp(t):
        light_high, light_low = split(light[...])
        a = w - 1 + t
        real = (a >= 0) & (a < ROW_TILES)
        shape = (16, STRIP, FRAME)
        rs = STRIP * n + 256 * (1 - t) + HALO - where[t][:, :, 0:1]
        hit = (lax.broadcasted_iota(jnp.int32, shape, 2) == lax.broadcasted_iota(jnp.int32, shape, 1) + rs) & real
        lines = jnp.where(hit, 1.0, 0.0).reshape((16 * STRIP, FRAME)).astype(bf16)
        lit[:, 0] = dot(lines, light_high).astype(bf16).reshape(shape)
        lit[:, 1] = dot(lines, light_low).astype(bf16).reshape(shape)

        def add(i, b, first, width):
            at = 8 * (i // 4) + 2 * (i % 4) + b
            cs = 512 * (m - b) + first + HALO - where[t, at][:, 1:2]
            columns = one_hot((FRAME, width), lambda p, q: p == q + cs)
            found = dot(lit[at].reshape((2 * STRIP, FRAME)), columns)
            return found[:STRIP] + found[STRIP:]

        @pl.loop(0, 8)
        def _(i):
            weight[...] += add(i, m, 0, 512)
            weight[:, out_cols] += add(i, 1 - m, 384 * (1 - m), 128)

    lamp(1)
    sends.arrived(where.at[0], where_sem.at[8], wide_down)
    sends.drain(gathered)

    def take_halo(i):
        for side in range(2):
            real = (w < ROW_TILES - 1) if side == 0 else (w > 0)
            sends.arrived(halo_in.at[side, i], halo_sem.at[side, i], wide_up if side == 0 else wide_down)
            total[(4 if side == 0 else 2) + i] += jnp.where(real, halo_in[side, i], 0.0)

    def block(zb):
        return total.at[2 + zb // 2, :, :, own_cols]

    second_stage(2)
    second_stage(3)
    third_send(0)
    take_halo(early)
    for way in range(2):
        sends.start(block(zs[4]).at[way], in_four.at[way], four_sem.at[way], onward[way])
    third_send(1)
    take_halo(1 - early)
    for way in range(2):
        zb = zs[2 if way == 0 else 6]
        sends.start(block(zb).at[1 - way], in_two.at[way, 1 - way], two_sem.at[way, 1 - way], onward[way])
    for way in range(2):
        distance, beyond = ((1, 3), (7, 5))[way]
        sends.start(
            total.at[2 + zs[beyond] // 2, way, :, side_cols], in_far.at[way, 0], far_sem.at[way, 0], near_peer[way]
        )
        sends.start(
            total.at[2 + zs[distance] // 2, :, :, side_cols], in_side.at[way], side_sem.at[way], near_peer[way]
        )
        sends.start(
            total.at[2 + zs[beyond] // 2, 1 - way, :, side_cols], in_far.at[way, 1], far_sem.at[way, 1], z_peer[beyond]
        )
    third_sum(0)
    lamp(0)
    sends.arrived(where.at[2], where_sem.at[9], wide_up)
    near = pl.ds(pl.multiple_of(384 - 256 * m, 128), 128)
    for way in range(2):
        zb = zs[2 if way == 0 else 6]
        sends.arrived(in_far.at[way, 0], far_sem.at[way, 0], near_peer[1 - way])
        total[2 + zb // 2, way, :, near] += in_far[way, 0]
        sends.arrived(in_four.at[way], four_sem.at[way], behind[way])
        in_four[way] += block(zb)[way]
        sends.start(in_four.at[way], in_two.at[way, way], two_sem.at[way, way], onward[way])
    scattered = sends.mark()
    third_sum(1)
    back_second(0)
    lamp(2)
    back_second(1)
    back_first(0)
    sends.drain(scattered)

    for way in range(2):
        sends.arrived(in_side.at[way], side_sem.at[way], near_peer[1 - way])
        sends.arrived(in_far.at[way, 1], far_sem.at[way, 1], z_peer[5 if way == 0 else 3])
        total[2 + zh, 1 - way, :, near] += in_far[way, 1]
    total[2 + zh, :, :, near] += in_side[0] + in_side[1]
    for way in range(2):
        for plane in range(2):
            sends.arrived(in_two.at[way, plane], two_sem.at[way, plane], behind[way])
    numerator = jnp.zeros((), f32)
    under = 1.0 / (weight[...] + DAMPING)
    squares = jnp.zeros((STRIP, 512), f32)
    for plane in range(2):
        strip = total[2 + zh, plane, :, own_cols] + in_two[0, plane] + in_two[1, plane]
        step = strip * under
        direction[plane] = step
        numerator += jnp.sum(step * strip)
        squares += step * step
    denominator = jnp.sum(squares * weight[...])
    line = lax.broadcasted_iota(jnp.int32, (8, 128), 0)
    tile[0] = jnp.where(line == 0, numerator, denominator)

    def tile_send(stage, peers, first):
        for i in range(1, len(peers)):
            sends.start(tile.at[stage], tiles_in.at[first + i - 1], tile_sem.at[first + i - 1], peers[i])

    def tile_sum(stage, peers, first):
        for i in range(1, len(peers)):
            sends.arrived(tiles_in.at[first + i - 1], tile_sem.at[first + i - 1], peers[len(peers) - i])
        found = tile[stage]
        for i in range(1, len(peers)):
            found = found + tiles_in[first + i - 1]
        tile[stage + 1] = found

    tile_send(0, [None, sibling], 0)
    back_first(1)
    tile_sum(0, [None, sibling], 0)
    tile_send(1, plane_peer, 1)
    hand_over(0)
    for k in range(MODES):
        part_copy(k).wait_send()
        for i in range(1, 4):
            first_copy(k, i).wait_send()
    tile_sum(1, plane_peer, 1)
    tile_send(2, z_peer, 16)
    closing = sends.mark()
    hand_over(1)
    sends.drain(closing)
    tile_sum(2, z_peer, 16)
    sums = tile[3]
    alpha = sums[0:1, 0:1] / sums[1:2, 0:1]
    step_out[...] = direction[...] * alpha
    for k in range(MODES):
        _, theirs, _, _, _, _ = ways(k)
        for i in range(4):
            sends.arrived(probe_out.at[1 - c, k, out_rows(theirs[(4 - i) % 4], 0, 64)], asem0.at[k, i], sibling)
    sends.finish()


VMEM = pl.BlockSpec(memory_space=pltpu.VMEM)
SMEM = pl.BlockSpec(memory_space=pltpu.SMEM)
ANY = pl.BlockSpec(memory_space=pl.ANY)
DMA = pltpu.SemaphoreType.DMA


def update(obj, probe, amp, tables, row, col):
    v = lambda *shape: pltpu.VMEM(shape, f32)
    return pl.pallas_call(
        update_kernel,
        out_shape=[
            pltpu.VMEM((2, STRIP, 512), f32),
            pltpu.VMEM((2, MODES, FRAME, FRAME), f32),
        ],
        in_specs=[ANY, ANY, ANY, ANY, SMEM, SMEM],
        out_specs=[VMEM, VMEM],
        scratch_shapes=[
            v(2, 512, 640),
            v(2, MODES, FRAME, FRAME),
            v(FRAME, FRAME),
            pltpu.VMEM((6, FRAME, FRAME), bf16),
            pltpu.VMEM((2, 2, 512, FRAME), bf16),
            v(MODES + 1, 512, FRAME),
            v(FRAME, FRAME),
            v(FRAME, FRAME),
            v(2, FRAME, FRAME),
            pltpu.VMEM((3, 16, 1, 128), jnp.int32),
            v(8, 2, STRIP, 640),
            v(8, 2, STRIP, 640),
            v(8, 2, STRIP, 640),
            v(2, 2, 2, STRIP, 640),
            v(2, STRIP, 512),
            v(2, 2, STRIP, 512),
            v(2, 2, STRIP, 128),
            v(2, 2, STRIP, 128),
            v(STRIP, 512),
            v(2, STRIP, 512),
            pltpu.VMEM((16, 2, STRIP, FRAME), bf16),
            v(2, MODES, FRAME, FRAME),
            v(MODES, FRAME, FRAME),
            v(MODES, FRAME, FRAME),
            v(MODES, 3, 64, FRAME),
            v(MODES, 64, FRAME),
            v(MODES, 3, 16, FRAME),
            v(MODES, 16, FRAME),
            v(2, 7, 8, 128),
            v(MODES, 16, FRAME),
            v(4, 8, 128),
            v(23, 8, 128),
            DMA((N_SENDS,)),
            DMA((4,)),
            DMA((2, 2)),
            DMA((2,)),
            DMA((2, 2)),
            DMA((8,)),
            DMA((8,)),
            DMA((8,)),
            DMA((10,)),
            DMA((4,)),
            DMA((2, 2)),
            DMA((2,)),
            DMA((2, 2)),
            DMA((2,)),
            DMA((2, 2)),
            DMA((MODES,)),
            DMA((MODES,)),
            DMA((MODES, 3)),
            DMA((MODES, 3)),
            DMA((MODES, 3)),
            DMA((2, 7)),
            DMA((2, 7)),
            DMA((MODES, 3)),
            DMA((MODES, 3)),
            DMA((MODES, 4)),
            DMA((23,)),
        ],
        compiler_params=pltpu.CompilerParams(
            collective_id=0, has_side_effects=True, vmem_limit_bytes=56 * 2**20
        ),
    )(obj, probe, amp, tables, row, col)


def per_device(obj_tile, probe, amplitude, row_offsets, col_offsets):
    step, gradient = update(
        obj_tile, probe, amplitude.reshape((FRAME, FRAME)), jnp.asarray(dft_tables()), row_offsets, col_offsets
    )
    return step, gradient


def solution(mesh):
    in_specs = (
        P(None, ("wide", "narrow"), "medium"),
        P(),
        P("wide", "medium", "narrow", None, None),
        P("wide", "medium", "narrow"),
        P("wide", "medium", "narrow"),
    )
    out_specs = (P(None, ("wide", "narrow"), "medium"), P())
    return jax.shard_map(
        per_device, mesh=mesh, in_specs=in_specs, out_specs=out_specs, check_vma=False
    )
```

```python
import functools
import math

import jax
import jax.numpy as jnp
import numpy as np
from jax import lax
from jax.experimental import pallas as pl
from jax.experimental.pallas import tpu as pltpu
from jax.sharding import PartitionSpec as P

MESH = pl.DeviceIdType.MESH
f32 = jnp.float32
bf16 = jnp.bfloat16
FRAME = 256
MODES = 4
HALO = 128
STRIP = 32
NX, NY, NZ = 4, 4, 8
ROW_TILES = 16
INTENSITY_FLOOR = 0.1
DAMPING = 4.0


def here():
    w = lax.axis_index("wide")
    m = lax.axis_index("medium")
    n = lax.axis_index("narrow")
    return w // NY, w % NY, (n // 2) * 2 + m, n % 2


def device(x, y, z, c):
    return (x * NY + y, z % 2, (z // 2) * 2 + c)


class Sends:
    def __init__(self, sem):
        self.sem = sem
        self.copies = []
        self.waited = 0

    def start(self, src, dst, recv_sem, target):
        copy = pltpu.make_async_remote_copy(
            src_ref=src,
            dst_ref=dst,
            send_sem=self.sem.at[len(self.copies)],
            recv_sem=recv_sem,
            device_id=target,
            device_id_type=MESH,
        )
        copy.start()
        self.copies.append(copy)

    def arrived(self, dst, recv_sem, source):
        pltpu.make_async_remote_copy(
            src_ref=dst,
            dst_ref=dst,
            send_sem=self.sem.at[0],
            recv_sem=recv_sem,
            device_id=source,
            device_id_type=MESH,
        ).wait_recv()

    def drain(self, count):
        for copy in self.copies[self.waited : count]:
            copy.wait_send()
        self.waited = max(self.waited, count)

    def finish(self):
        self.drain(len(self.copies))


def greet(peers):
    barrier = pltpu.get_barrier_semaphore()
    for peer in peers:
        pl.semaphore_signal(barrier, inc=1, device_id=peer, device_id_type=MESH)


def met(peers):
    pl.semaphore_wait(pltpu.get_barrier_semaphore(), len(peers))


def dft_tables():
    steps = np.arange(FRAME)
    angle = (steps[:, None] * steps[None, :] % FRAME) * (2.0 * math.pi / FRAME)
    cosine = np.cos(angle) / math.sqrt(FRAME)
    sine = np.sin(angle) / math.sqrt(FRAME)
    found = []
    for table in (cosine, cosine + sine, cosine - sine):
        table = table.astype(np.float32)
        high = table.astype(jnp.bfloat16)
        found += [high, (table - high.astype(np.float32)).astype(jnp.bfloat16)]
    return np.stack(found)


def split(x):
    high = x.astype(bf16)
    return high, (x - high.astype(f32)).astype(bf16)


def dot(a, b):
    return jnp.dot(a, b, preferred_element_type=f32)


def side(re, im, product, sign):
    k1 = product(re + im, 0)
    k2 = product(re, 2 if sign > 0 else 4)
    k3 = product(im, 4 if sign > 0 else 2)
    return k1 - k3, k1 - k2


def transform(re, im, tables, sign):
    def right(x, t):
        high, low = split(x)
        return dot(high, tables[t]) + dot(high, tables[t + 1]) + dot(low, tables[t])

    def left(x, t):
        high, low = split(x)
        return dot(tables[t], high) + dot(tables[t], low) + dot(tables[t + 1], high)

    re, im = side(re, im, right, sign)
    return side(re, im, left, sign)


BLOCKS = (0, 6, 2, 7, 1, 3, 5, 4)
N_SENDS = 192


def one_hot(shape, hit):
    return jnp.where(hit(lax.broadcasted_iota(jnp.int32, shape, 0), lax.broadcasted_iota(jnp.int32, shape, 1)), 1.0, 0.0).astype(bf16)


def pick_columns(x, table):
    high, low = split(x)
    return dot(high, table) + dot(low, table)


def pick_rows(table, x):
    high, low = split(x)
    return dot(table, high) + dot(table, low)


def update_kernel(
    obj, probe_in, amp_in, tables_in, row_in, col_in,
    step_out, probe_out,
    rows_tile, probe, amp, tables, narrowed, far, factor, light, grad, where,
    sib_out, sib_in, total, halo_in, in_four, in_two, in_side, weight, direction, lit,
    probe_part, part_in, part, in1, sum1, in2, sum2, in3, all3, tile, tiles_in,
    send_sem, local_sem, gtwo_sem, gfour_sem, gside_sem, gsib_sem, ghalo_sem, gsibhalo_sem, where_sem,
    sib_sem, halo_sem, four_sem, two_sem, side_sem, part_sem, part_send_sem, sem1, send1_sem, sem2, sem3,
    asem3, asem2, asem1, asem0, tile_sem,
):
    x, y, z, c = here()
    m = z % 2
    zh = z // 2
    w = x * NY + y
    n = zh * 2 + c
    xs = [((x + i) % NX) for i in range(NX)]
    ys = [((y + i) % NY) for i in range(NY)]
    zs = [((z + i) % NZ) for i in range(NZ)]
    x_peer = [device(v, y, z, c) for v in xs]
    y_peer = [device(x, v, z, c) for v in ys]
    z_peer = [device(x, y, v, c) for v in zs]
    plane_peer = [((w + i) % ROW_TILES, m, n) for i in range(ROW_TILES)]
    sibling = device(x, y, z, 1 - c)
    wide_up, wide_down = plane_peer[1], plane_peer[15]
    onward = (z_peer[2], z_peer[6])
    behind = (z_peer[6], z_peer[2])
    near_peer = (z_peer[1], z_peer[7])
    sends = Sends(send_sem)

    locals_ = [
        pltpu.make_async_copy(a, b, local_sem.at[i])
        for i, (a, b) in enumerate(
            ((probe_in, probe), (amp_in, amp), (tables_in, tables))
        )
    ]
    for copy in locals_:
        copy.start()
    r0 = row_in[0, 0, 0]
    offset_col = col_in[0, 0, 0]
    c0 = offset_col - HALO * (1 - m)
    lane = lax.broadcasted_iota(jnp.int32, (1, 128), 1)
    where[1, 8 * c + z] = jnp.where(lane == 0, r0, offset_col)
    everyone = [sibling] + plane_peer[1:] + z_peer[1:]
    greet(everyone)
    met(everyone)

    def strip_of(zb, core):
        return (zb // 2) * 2 + core

    own_cols = pl.ds(pl.multiple_of(128 * m, 128), 512)
    side_cols = pl.ds(pl.multiple_of(512 * (1 - m), 128), 128)

    def columns_of(distance):
        return side_cols if distance % 2 else own_cols

    def place(zb, core):
        return pl.ds(pl.multiple_of(HALO + STRIP * strip_of(zb, core), STRIP), STRIP)

    def halo_place(zb, core):
        s = strip_of(zb, core)
        return pl.ds(pl.multiple_of(HALO + STRIP * s + 256 * (1 - 2 * (s // 4)), STRIP), STRIP)

    def pass_on(slot, src=None):
        distance = BLOCKS[slot]
        zb = zs[distance]
        cols = columns_of(distance)
        ref = rows_tile.at[:, place(zb, c), cols]
        towards = (w + ROW_TILES + 2 * (strip_of(zb, c) // 4) - 1) % ROW_TILES
        sends.start(
            ref if src is None else src,
            rows_tile.at[:, halo_place(zb, c), cols], ghalo_sem.at[slot], (towards, m, n),
        )
        sends.start(ref if src is None else src, ref, gsib_sem.at[slot], sibling)

    mine = where.at[1, pl.ds(8 * c + z, 1)]
    for i in range(1, 8):
        sends.start(mine, mine, where_sem.at[i - 1], z_peer[i])

    rows = place(z, c)
    for plane in range(2):
        for way in range(2):
            p = plane if way == 0 else 1 - plane
            sends.start(
                obj.at[p], rows_tile.at[p, rows, own_cols], gtwo_sem.at[way, p], onward[way]
            )
    pass_on(0, obj)
    out_cols = pl.ds(pl.multiple_of(384 * (1 - m), 128), 128)
    there = pl.ds(pl.multiple_of(512 * m, 128), 128)
    give_cols = pl.ds(pl.multiple_of(384 - 256 * m, 128), 128)
    for way in range(2):
        sends.start(obj.at[:, :, out_cols], rows_tile.at[:, rows, there], gside_sem.at[way, 0], near_peer[way])
    own = pltpu.make_async_copy(obj, rows_tile.at[:, rows, own_cols], local_sem.at[3])
    own.start()
    for way in range(2):
        zb = zs[6 if way == 0 else 2]
        ref = rows_tile.at[way, place(zb, c), own_cols]
        sends.arrived(ref, gtwo_sem.at[way, way], behind[way])
        sends.start(ref, ref, gfour_sem.at[way], onward[way])
    for way in range(2):
        zb = zs[6 if way == 0 else 2]
        sends.arrived(rows_tile.at[1 - way, place(zb, c), own_cols], gtwo_sem.at[way, 1 - way], behind[way])
        sends.start(
            rows_tile.at[:, place(zb, c), give_cols], rows_tile.at[:, place(zb, c), there],
            gside_sem.at[way, 1], near_peer[way],
        )
        pass_on(1 + way)
    for step in range(2):
        for way in range(2):
            distance = ((7, 5), (1, 3))[way][step]
            sends.arrived(
                rows_tile.at[:, place(zs[distance], c), side_cols], gside_sem.at[way, step], near_peer[1 - way]
            )
            pass_on(BLOCKS.index(distance))

    for i in range(1, 8):
        sends.arrived(where.at[1, pl.ds(8 * c + zs[8 - i], 1)], where_sem.at[i - 1], z_peer[8 - i])
    half = where.at[1, pl.ds(pl.multiple_of(8 * c, 8), 8)]
    sends.start(half, half, where_sem.at[7], sibling)

    def halo_arrived(slot):
        distance = BLOCKS[slot]
        ref = rows_tile.at[:, halo_place(zs[distance], c), columns_of(distance)]
        sends.arrived(ref, ghalo_sem.at[slot], wide_up)
        sends.start(ref, ref, gsibhalo_sem.at[slot], sibling)

    halo_arrived(0)
    for way in range(2):
        sends.arrived(rows_tile.at[way, place(zs[4], c), own_cols], gfour_sem.at[way], behind[way])
    pass_on(7)
    for slot in range(1, 7):
        halo_arrived(slot)
    sends.arrived(where.at[1, pl.ds(pl.multiple_of(8 * (1 - c), 8), 8)], where_sem.at[7], sibling)
    sends.start(where.at[1], where.at[0], where_sem.at[8], wide_up)
    sends.start(where.at[1], where.at[2], where_sem.at[9], wide_down)
    for slot in range(8):
        distance = BLOCKS[slot]
        sends.arrived(rows_tile.at[:, place(zs[distance], 1 - c), columns_of(distance)], gsib_sem.at[slot], sibling)
    own.wait()

    def on_object(row):
        at = row + (256 * w - HALO)
        return (at >= 0) & (at < 256 * ROW_TILES)

    columns = one_hot((640, FRAME), lambda i, j: i == j + c0)
    lines = one_hot((FRAME, 512), lambda i, j: (j == i + r0) & on_object(j))
    patch = far.at[MODES]

    def narrow(rows):
        for plane in range(2):
            for part, value in enumerate(split(rows_tile[plane, rows])):
                narrowed[plane, part, rows] = dot(value, columns).astype(bf16)

    locals_[0].wait()
    light[...] = jnp.zeros_like(light)

    @pl.loop(0, MODES)
    def _(k):
        light[...] += probe[0, k] * probe[0, k] + probe[1, k] * probe[1, k]

    narrow(slice(HALO, HALO + 256))
    halo_arrived(7)
    for slot in range(8):
        distance = BLOCKS[slot]
        sends.arrived(
            rows_tile.at[:, halo_place(zs[distance], 1 - c), columns_of(distance)], gsibhalo_sem.at[slot], sibling
        )
    for copy in locals_[1:]:
        copy.wait()
    narrow(slice(0, HALO))
    narrow(slice(HALO + 256, 512))
    for plane in range(2):
        patch[FRAME * plane : FRAME * (plane + 1)] = dot(lines, narrowed[plane, 0]) + dot(lines, narrowed[plane, 1])

    pr, pi = patch[:FRAME], patch[FRAME:]
    for k in range(MODES):
        a, b = probe[0, k], probe[1, k]
        fre, fim = transform(a * pr - b * pi, a * pi + b * pr, tables, 1)
        far[k, :FRAME] = fre
        far[k, FRAME:] = fim
        squares = fre * fre + fim * fim
        factor[...] = squares if k == 0 else factor[...] + squares

    factor[...] = amp[...] / jnp.sqrt(jnp.maximum(factor[...], INTENSITY_FLOOR)) - 1.0

    def part_copy(k):
        return pltpu.make_async_remote_copy(
            src_ref=probe_part.at[1 - c, k], dst_ref=part_in.at[k],
            send_sem=part_send_sem.at[k], recv_sem=part_sem.at[k],
            device_id=sibling, device_id_type=MESH,
        )

    def first_copy(k, i):
        h = k % 2
        tx, ty = (x + i * h) % NX, (y + i * (1 - h)) % NY
        q = h * tx + (1 - h) * ty
        return pltpu.make_async_remote_copy(
            src_ref=part.at[k, pl.ds(pl.multiple_of(64 * q, 64), 64)], dst_ref=in1.at[k, i - 1],
            send_sem=send1_sem.at[k, i - 1], recv_sem=sem1.at[k, i - 1],
            device_id=(tx * NY + ty, m, n), device_id_type=MESH,
        )

    def take_part(k):
        part_copy(k).wait_recv()
        part[k] = part_in[k] + probe_part[c, k]
        for i in range(1, 4):
            first_copy(k, i).start()

    for k in range(MODES):
        scale = factor[...]
        cre, cim = transform(far[k, :FRAME] * scale, far[k, FRAME:] * scale, tables, -1)
        a, b = probe[0, k], probe[1, k]
        pr, pi = patch[:FRAME], patch[FRAME:]
        probe_part[0, k] = pr * cre + pi * cim
        probe_part[1, k] = pr * cim - pi * cre
        part_copy(k).start()
        gre, gim = a * cre + b * cim, a * cim - b * cre
        grad[0] = gre if k == 0 else grad[0] + gre
        grad[1] = gim if k == 0 else grad[1] + gim
        if k > 0:
            take_part(k - 1)

    def ways(k):
        if k % 2 == 0:
            return y, ys, y_peer, x, xs, x_peer
        return x, xs, x_peer, y, ys, y_peer

    def second_stage(k):
        first, _, _, _, theirs, peers = ways(k)
        rows = pl.ds(pl.multiple_of(64 * first, 64), 64)
        for i in range(1, 4):
            first_copy(k, i).wait_recv()
        sum1[k] = part[k, rows] + in1[k, 0] + in1[k, 1] + in1[k, 2]
        for i in range(1, 4):
            sends.start(
                sum1.at[k, pl.ds(pl.multiple_of(16 * theirs[i], 16), 16)],
                in2.at[k, i - 1], sem2.at[k, i - 1], peers[i],
            )

    def z_tile(pair, v):
        return (
            2 * pair + v // 4,
            pl.ds(pl.multiple_of(8 * ((v // 2) % 2), 8), 8),
            pl.ds(pl.multiple_of(128 * (v % 2), 128), 128),
        )

    def third_send(pair):
        for k in (2 * pair, 2 * pair + 1):
            _, _, _, second, _, peers = ways(k)
            for i in range(1, 4):
                sends.arrived(in2.at[k, i - 1], sem2.at[k, i - 1], peers[4 - i])
            rows = pl.ds(pl.multiple_of(16 * second, 16), 16)
            sum2[k] = sum1[k, rows] + in2[k, 0] + in2[k, 1] + in2[k, 2]
        for i in range(1, 8):
            sends.start(sum2.at[z_tile(pair, zs[i])], in3.at[pair, i - 1], sem3.at[pair, i - 1], z_peer[i])

    def third_sum(pair):
        for i in range(1, 8):
            sends.arrived(in3.at[pair, i - 1], sem3.at[pair, i - 1], z_peer[8 - i])
        whole = sum2[z_tile(pair, z)]
        for i in range(1, 8):
            whole = whole + in3[pair, i - 1]
        all3[z_tile(pair, z)] = whole
        for i in range(1, 8):
            ref = all3.at[z_tile(pair, z)]
            sends.start(ref, ref, asem3.at[pair, i - 1], z_peer[i])

    def out_rows(first, second, count):
        return pl.ds(pl.multiple_of(64 * first + 16 * second, 16), count)

    def back_second(pair):
        for i in range(1, 8):
            sends.arrived(all3.at[z_tile(pair, zs[8 - i])], asem3.at[pair, i - 1], z_peer[8 - i])
        for k in (2 * pair, 2 * pair + 1):
            first, _, _, second, _, peers = ways(k)
            rows = out_rows(first, second, 16)
            for i in range(1, 4):
                sends.start(all3.at[k], probe_out.at[c, k, rows], asem2.at[k, i - 1], peers[i])
            probe_out[c, k, rows] = all3[k]

    def back_first(pair):
        for k in (2 * pair, 2 * pair + 1):
            first, _, first_peers, _, theirs, peers = ways(k)
            for i in range(1, 4):
                ref = probe_out.at[c, k, out_rows(first, theirs[4 - i], 16)]
                sends.arrived(ref, asem2.at[k, i - 1], peers[4 - i])
            ref = probe_out.at[c, k, out_rows(first, 0, 64)]
            for i in range(1, 4):
                sends.start(ref, ref, asem1.at[k, i - 1], first_peers[i])
            sends.start(ref, ref, asem0.at[k, 0], sibling)

    def hand_over(pair):
        for k in (2 * pair, 2 * pair + 1):
            _, theirs, peers, _, _, _ = ways(k)
            for i in range(1, 4):
                ref = probe_out.at[c, k, out_rows(theirs[4 - i], 0, 64)]
                sends.arrived(ref, asem1.at[k, i - 1], peers[4 - i])
                sends.start(ref, ref, asem0.at[k, i], sibling)

    columns_back = one_hot((FRAME, 640), lambda i, j: j == i + c0)

    def put(core, dst):
        lines_back = one_hot(
            (FRAME, FRAME), lambda i, j: 64 * (i // STRIP) + STRIP * core + i % STRIP == j + r0
        )
        for plane in range(2):
            found = pick_columns(pick_rows(lines_back, grad[plane]), columns_back)
            for j in range(8):
                dst[j, plane] = found[STRIP * j : STRIP * (j + 1)]

    gathered = len(sends.copies)
    second_stage(0)
    put(1 - c, sib_out)
    for k in (0, 3, 1, 2):
        both = pl.ds(2 * k, 2)
        sends.start(sib_out.at[both], sib_in.at[both], sib_sem.at[k], sibling)
    take_part(3)
    second_stage(1)
    put(c, total)
    early = zh % 2
    for k in (0, 3, 1, 2):
        both = pl.ds(2 * k, 2)
        sends.arrived(sib_in.at[both], sib_sem.at[k], sibling)
        total[both] += sib_in[both]
        if k == 3:
            for i in (early, 1 - early):
                sends.start(total.at[i], halo_in.at[0, i], halo_sem.at[0, i], wide_down)
                sends.start(total.at[6 + i], halo_in.at[1, i], halo_sem.at[1, i], wide_up)
    third_send(0)

    weight[...] = jnp.zeros_like(weight)

    def lamp(t):
        light_high, light_low = split(light[...])
        a = w - 1 + t
        real = (a >= 0) & (a < ROW_TILES)
        shape = (16, STRIP, FRAME)
        rs = STRIP * n + 256 * (1 - t) + HALO - where[t][:, :, 0:1]
        hit = (lax.broadcasted_iota(jnp.int32, shape, 2) == lax.broadcasted_iota(jnp.int32, shape, 1) + rs) & real
        lines = jnp.where(hit, 1.0, 0.0).reshape((16 * STRIP, FRAME)).astype(bf16)
        lit[:, 0] = dot(lines, light_high).astype(bf16).reshape(shape)
        lit[:, 1] = dot(lines, light_low).astype(bf16).reshape(shape)

        def add(i, b, first, width):
            at = 8 * (i // 4) + 2 * (i % 4) + b
            cs = 512 * (m - b) + first + HALO - where[t, at][:, 1:2]
            columns = one_hot((FRAME, width), lambda p, q: p == q + cs)
            found = dot(lit[at].reshape((2 * STRIP, FRAME)), columns)
            return found[:STRIP] + found[STRIP:]

        @pl.loop(0, 8)
        def _(i):
            weight[...] += add(i, m, 0, 512)
            weight[:, out_cols] += add(i, 1 - m, 384 * (1 - m), 128)

    lamp(1)
    sends.arrived(where.at[0], where_sem.at[8], wide_down)

    def take_halo(i):
        for side in range(2):
            real = (w < ROW_TILES - 1) if side == 0 else (w > 0)
            sends.arrived(halo_in.at[side, i], halo_sem.at[side, i], wide_up if side == 0 else wide_down)
            total[(4 if side == 0 else 2) + i] += jnp.where(real, halo_in[side, i], 0.0)

    def block(zb):
        return total.at[2 + zb // 2, :, :, own_cols]

    second_stage(2)
    second_stage(3)
    sends.drain(gathered)
    take_halo(early)
    for way in range(2):
        sends.start(block(zs[4]).at[way], in_four.at[way], four_sem.at[way], onward[way])
    third_sum(0)
    third_send(1)
    take_halo(1 - early)
    for way in range(2):
        for step in range(2):
            distance = ((1, 3), (7, 5))[way][step]
            sends.start(
                total.at[2 + zs[distance] // 2, :, :, side_cols], in_side.at[way, step], side_sem.at[way, step],
                near_peer[way],
            )
    lamp(0)
    sends.arrived(where.at[2], where_sem.at[9], wide_up)
    near = pl.ds(pl.multiple_of(384 - 256 * m, 128), 128)
    for way in range(2):
        sends.arrived(in_side.at[way, 1], side_sem.at[way, 1], near_peer[1 - way])
        zb = zs[2 if way == 0 else 6]
        total[2 + zb // 2, :, :, near] += in_side[way, 1]
        sends.start(block(zb).at[1 - way], in_two.at[way, 1 - way], two_sem.at[way, 1 - way], onward[way])
    for way in range(2):
        sends.arrived(in_four.at[way], four_sem.at[way], behind[way])
        in_four[way] += block(zs[2 if way == 0 else 6])[way]
        sends.start(in_four.at[way], in_two.at[way, way], two_sem.at[way, way], onward[way])
    scattered = len(sends.copies)
    back_second(0)
    third_sum(1)
    lamp(2)
    back_first(0)
    back_second(1)
    sends.drain(scattered)

    for way in range(2):
        sends.arrived(in_side.at[way, 0], side_sem.at[way, 0], near_peer[1 - way])
    total[2 + zh, :, :, near] += in_side[0, 0] + in_side[1, 0]
    for way in range(2):
        for plane in range(2):
            sends.arrived(in_two.at[way, plane], two_sem.at[way, plane], behind[way])
    numerator = jnp.zeros((), f32)
    under = 1.0 / (weight[...] + DAMPING)
    squares = jnp.zeros((STRIP, 512), f32)
    for plane in range(2):
        strip = total[2 + zh, plane, :, own_cols] + in_two[0, plane] + in_two[1, plane]
        step = strip * under
        direction[plane] = step
        numerator += jnp.sum(step * strip)
        squares += step * step
    denominator = jnp.sum(squares * weight[...])
    line = lax.broadcasted_iota(jnp.int32, (8, 128), 0)
    tile[0] = jnp.where(line == 0, numerator, denominator)

    def tile_send(stage, peers, first):
        for i in range(1, len(peers)):
            sends.start(tile.at[stage], tiles_in.at[first + i - 1], tile_sem.at[first + i - 1], peers[i])

    def tile_sum(stage, peers, first):
        for i in range(1, len(peers)):
            sends.arrived(tiles_in.at[first + i - 1], tile_sem.at[first + i - 1], peers[len(peers) - i])
        found = tile[stage]
        for i in range(1, len(peers)):
            found = found + tiles_in[first + i - 1]
        tile[stage + 1] = found

    tile_send(0, [None, sibling], 0)
    tile_sum(0, [None, sibling], 0)
    tile_send(1, plane_peer, 1)
    back_first(1)
    hand_over(0)
    for k in range(MODES):
        part_copy(k).wait_send()
        for i in range(1, 4):
            first_copy(k, i).wait_send()
    tile_sum(1, plane_peer, 1)
    tile_send(2, z_peer, 16)
    closing = len(sends.copies)
    hand_over(1)
    sends.drain(closing)
    tile_sum(2, z_peer, 16)
    sums = tile[3]
    alpha = sums[0:1, 0:1] / sums[1:2, 0:1]
    step_out[...] = direction[...] * alpha
    for k in range(MODES):
        _, theirs, _, _, _, _ = ways(k)
        for i in range(4):
            sends.arrived(probe_out.at[1 - c, k, out_rows(theirs[(4 - i) % 4], 0, 64)], asem0.at[k, i], sibling)
    sends.finish()


VMEM = pl.BlockSpec(memory_space=pltpu.VMEM)
SMEM = pl.BlockSpec(memory_space=pltpu.SMEM)
ANY = pl.BlockSpec(memory_space=pl.ANY)
DMA = pltpu.SemaphoreType.DMA


def update(obj, probe, amp, tables, row, col):
    v = lambda *shape: pltpu.VMEM(shape, f32)
    return pl.pallas_call(
        update_kernel,
        out_shape=[
            pltpu.VMEM((2, STRIP, 512), f32),
            pltpu.VMEM((2, MODES, FRAME, FRAME), f32),
        ],
        in_specs=[ANY, ANY, ANY, ANY, SMEM, SMEM],
        out_specs=[VMEM, VMEM],
        scratch_shapes=[
            v(2, 512, 640),
            v(2, MODES, FRAME, FRAME),
            v(FRAME, FRAME),
            pltpu.VMEM((6, FRAME, FRAME), bf16),
            pltpu.VMEM((2, 2, 512, FRAME), bf16),
            v(MODES + 1, 512, FRAME),
            v(FRAME, FRAME),
            v(FRAME, FRAME),
            v(2, FRAME, FRAME),
            pltpu.VMEM((3, 16, 1, 128), jnp.int32),
            v(8, 2, STRIP, 640),
            v(8, 2, STRIP, 640),
            v(8, 2, STRIP, 640),
            v(2, 2, 2, STRIP, 640),
            v(2, STRIP, 512),
            v(2, 2, STRIP, 512),
            v(2, 2, 2, STRIP, 128),
            v(STRIP, 512),
            v(2, STRIP, 512),
            pltpu.VMEM((16, 2, STRIP, FRAME), bf16),
            v(2, MODES, FRAME, FRAME),
            v(MODES, FRAME, FRAME),
            v(MODES, FRAME, FRAME),
            v(MODES, 3, 64, FRAME),
            v(MODES, 64, FRAME),
            v(MODES, 3, 16, FRAME),
            v(MODES, 16, FRAME),
            v(2, 7, 8, 128),
            v(MODES, 16, FRAME),
            v(4, 8, 128),
            v(23, 8, 128),
            DMA((N_SENDS,)),
            DMA((4,)),
            DMA((2, 2)),
            DMA((2,)),
            DMA((2, 2)),
            DMA((8,)),
            DMA((8,)),
            DMA((8,)),
            DMA((10,)),
            DMA((4,)),
            DMA((2, 2)),
            DMA((2,)),
            DMA((2, 2)),
            DMA((2, 2)),
            DMA((MODES,)),
            DMA((MODES,)),
            DMA((MODES, 3)),
            DMA((MODES, 3)),
            DMA((MODES, 3)),
            DMA((2, 7)),
            DMA((2, 7)),
            DMA((MODES, 3)),
            DMA((MODES, 3)),
            DMA((MODES, 4)),
            DMA((23,)),
        ],
        compiler_params=pltpu.CompilerParams(
            collective_id=0, has_side_effects=True, vmem_limit_bytes=56 * 2**20
        ),
    )(obj, probe, amp, tables, row, col)


def per_device(obj_tile, probe, amplitude, row_offsets, col_offsets):
    step, gradient = update(
        obj_tile, probe, amplitude.reshape((FRAME, FRAME)), jnp.asarray(dft_tables()), row_offsets, col_offsets
    )
    return step, gradient


def solution(mesh):
    in_specs = (
        P(None, ("wide", "narrow"), "medium"),
        P(),
        P("wide", "medium", "narrow", None, None),
        P("wide", "medium", "narrow"),
        P("wide", "medium", "narrow"),
    )
    out_specs = (P(None, ("wide", "narrow"), "medium"), P())
    return jax.shard_map(
        per_device, mesh=mesh, in_specs=in_specs, out_specs=out_specs, check_vma=False
    )
```

```python
import functools
import math

import jax
import jax.numpy as jnp
import numpy as np
from jax import lax
from jax.experimental import pallas as pl
from jax.experimental.pallas import tpu as pltpu
from jax.sharding import PartitionSpec as P

MESH = pl.DeviceIdType.MESH
f32 = jnp.float32
bf16 = jnp.bfloat16
FRAME = 256
MODES = 4
HALO = 128
STRIP = 32
NX, NY, NZ = 4, 4, 8
ROW_TILES = 16
INTENSITY_FLOOR = 0.1
DAMPING = 4.0


def here():
    w = lax.axis_index("wide")
    m = lax.axis_index("medium")
    n = lax.axis_index("narrow")
    return w // NY, w % NY, (n // 2) * 2 + m, n % 2


def device(x, y, z, c):
    return (x * NY + y, z % 2, (z // 2) * 2 + c)


class Sends:
    def __init__(self, sem):
        self.sem = sem
        self.copies = []
        self.waited = 0

    def start(self, src, dst, recv_sem, target):
        copy = pltpu.make_async_remote_copy(
            src_ref=src,
            dst_ref=dst,
            send_sem=self.sem.at[len(self.copies)],
            recv_sem=recv_sem,
            device_id=target,
            device_id_type=MESH,
        )
        copy.start()
        self.copies.append(copy)

    def arrived(self, dst, recv_sem, source):
        pltpu.make_async_remote_copy(
            src_ref=dst,
            dst_ref=dst,
            send_sem=self.sem.at[0],
            recv_sem=recv_sem,
            device_id=source,
            device_id_type=MESH,
        ).wait_recv()

    def drain(self, count):
        for copy in self.copies[self.waited : count]:
            copy.wait_send()
        self.waited = max(self.waited, count)

    def finish(self):
        self.drain(len(self.copies))


def greet(peers):
    barrier = pltpu.get_barrier_semaphore()
    for peer in peers:
        pl.semaphore_signal(barrier, inc=1, device_id=peer, device_id_type=MESH)


def met(peers):
    pl.semaphore_wait(pltpu.get_barrier_semaphore(), len(peers))


def dft_tables():
    steps = np.arange(FRAME)
    angle = (steps[:, None] * steps[None, :] % FRAME) * (2.0 * math.pi / FRAME)
    cosine = np.cos(angle) / math.sqrt(FRAME)
    sine = np.sin(angle) / math.sqrt(FRAME)
    found = []
    for table in (cosine, cosine + sine, cosine - sine):
        table = table.astype(np.float32)
        high = table.astype(jnp.bfloat16)
        found += [high, (table - high.astype(np.float32)).astype(jnp.bfloat16)]
    return np.stack(found)


def split(x):
    high = x.astype(bf16)
    return high, (x - high.astype(f32)).astype(bf16)


def dot(a, b):
    return jnp.dot(a, b, preferred_element_type=f32)


def side(re, im, product, sign):
    k1 = product(re + im, 0)
    k2 = product(re, 2 if sign > 0 else 4)
    k3 = product(im, 4 if sign > 0 else 2)
    return k1 - k3, k1 - k2


def transform(re, im, tables, sign):
    def right(x, t):
        high, low = split(x)
        return dot(high, tables[t]) + dot(high, tables[t + 1]) + dot(low, tables[t])

    def left(x, t):
        high, low = split(x)
        return dot(tables[t], high) + dot(tables[t], low) + dot(tables[t + 1], high)

    re, im = side(re, im, right, sign)
    return side(re, im, left, sign)


BLOCKS = (0, 6, 2, 7, 1, 3, 5, 4)
N_SENDS = 192


def one_hot(shape, hit):
    return jnp.where(hit(lax.broadcasted_iota(jnp.int32, shape, 0), lax.broadcasted_iota(jnp.int32, shape, 1)), 1.0, 0.0).astype(bf16)


def pick_columns(x, table):
    high, low = split(x)
    return dot(high, table) + dot(low, table)


def pick_rows(table, x):
    high, low = split(x)
    return dot(table, high) + dot(table, low)


def update_kernel(
    obj, probe_in, amp_in, tables_in, row_in, col_in,
    step_out, probe_out,
    rows_tile, probe, amp, tables, narrowed, far, factor, light, grad, where,
    sib_out, sib_in, total, halo_in, in_four, in_two, in_side, weight, direction, lit,
    probe_part, part_in, part, in1, sum1, in2, sum2, in3, all3, tile, tiles_in,
    send_sem, local_sem, gtwo_sem, gfour_sem, gside_sem, gsib_sem, ghalo_sem, gsibhalo_sem, where_sem,
    sib_sem, halo_sem, four_sem, two_sem, side_sem, part_sem, part_send_sem, sem1, send1_sem, sem2, sem3,
    asem3, asem2, asem1, asem0, tile_sem,
):
    x, y, z, c = here()
    m = z % 2
    zh = z // 2
    w = x * NY + y
    n = zh * 2 + c
    xs = [((x + i) % NX) for i in range(NX)]
    ys = [((y + i) % NY) for i in range(NY)]
    zs = [((z + i) % NZ) for i in range(NZ)]
    x_peer = [device(v, y, z, c) for v in xs]
    y_peer = [device(x, v, z, c) for v in ys]
    z_peer = [device(x, y, v, c) for v in zs]
    plane_peer = [((w + i) % ROW_TILES, m, n) for i in range(ROW_TILES)]
    sibling = device(x, y, z, 1 - c)
    wide_up, wide_down = plane_peer[1], plane_peer[15]
    onward = (z_peer[2], z_peer[6])
    behind = (z_peer[6], z_peer[2])
    near_peer = (z_peer[1], z_peer[7])
    sends = Sends(send_sem)

    locals_ = [
        pltpu.make_async_copy(a, b, local_sem.at[i])
        for i, (a, b) in enumerate(
            ((probe_in, probe), (amp_in, amp), (tables_in, tables))
        )
    ]
    for copy in locals_:
        copy.start()
    r0 = row_in[0, 0, 0]
    offset_col = col_in[0, 0, 0]
    c0 = offset_col - HALO * (1 - m)
    lane = lax.broadcasted_iota(jnp.int32, (1, 128), 1)
    where[1, 8 * c + z] = jnp.where(lane == 0, r0, offset_col)
    everyone = [sibling] + plane_peer[1:] + z_peer[1:]
    greet(everyone)
    met(everyone)

    def strip_of(zb, core):
        return (zb // 2) * 2 + core

    own_cols = pl.ds(pl.multiple_of(128 * m, 128), 512)
    side_cols = pl.ds(pl.multiple_of(512 * (1 - m), 128), 128)

    def columns_of(distance):
        return side_cols if distance % 2 else own_cols

    def place(zb, core):
        return pl.ds(pl.multiple_of(HALO + STRIP * strip_of(zb, core), STRIP), STRIP)

    def halo_place(zb, core):
        s = strip_of(zb, core)
        return pl.ds(pl.multiple_of(HALO + STRIP * s + 256 * (1 - 2 * (s // 4)), STRIP), STRIP)

    def pass_on(slot, src=None):
        distance = BLOCKS[slot]
        zb = zs[distance]
        cols = columns_of(distance)
        ref = rows_tile.at[:, place(zb, c), cols]
        towards = (w + ROW_TILES + 2 * (strip_of(zb, c) // 4) - 1) % ROW_TILES
        sends.start(
            ref if src is None else src,
            rows_tile.at[:, halo_place(zb, c), cols], ghalo_sem.at[slot], (towards, m, n),
        )
        sends.start(ref if src is None else src, ref, gsib_sem.at[slot], sibling)

    mine = where.at[1, pl.ds(8 * c + z, 1)]
    for i in range(1, 8):
        sends.start(mine, mine, where_sem.at[i - 1], z_peer[i])

    rows = place(z, c)
    for plane in range(2):
        for way in range(2):
            p = plane if way == 0 else 1 - plane
            sends.start(
                obj.at[p], rows_tile.at[p, rows, own_cols], gtwo_sem.at[way, p], onward[way]
            )
    pass_on(0, obj)
    out_cols = pl.ds(pl.multiple_of(384 * (1 - m), 128), 128)
    there = pl.ds(pl.multiple_of(512 * m, 128), 128)
    give_cols = pl.ds(pl.multiple_of(384 - 256 * m, 128), 128)
    for way in range(2):
        sends.start(obj.at[:, :, out_cols], rows_tile.at[:, rows, there], gside_sem.at[way, 0], near_peer[way])
    own = pltpu.make_async_copy(obj, rows_tile.at[:, rows, own_cols], local_sem.at[3])
    own.start()
    for way in range(2):
        zb = zs[6 if way == 0 else 2]
        ref = rows_tile.at[way, place(zb, c), own_cols]
        sends.arrived(ref, gtwo_sem.at[way, way], behind[way])
        sends.start(ref, ref, gfour_sem.at[way], onward[way])
    for way in range(2):
        zb = zs[6 if way == 0 else 2]
        sends.arrived(rows_tile.at[1 - way, place(zb, c), own_cols], gtwo_sem.at[way, 1 - way], behind[way])
        sends.start(
            rows_tile.at[:, place(zb, c), give_cols], rows_tile.at[:, place(zb, c), there],
            gside_sem.at[way, 1], near_peer[way],
        )
        pass_on(1 + way)
    for step in range(2):
        for way in range(2):
            distance = ((7, 5), (1, 3))[way][step]
            sends.arrived(
                rows_tile.at[:, place(zs[distance], c), side_cols], gside_sem.at[way, step], near_peer[1 - way]
            )
            pass_on(BLOCKS.index(distance))

    for i in range(1, 8):
        sends.arrived(where.at[1, pl.ds(8 * c + zs[8 - i], 1)], where_sem.at[i - 1], z_peer[8 - i])
    half = where.at[1, pl.ds(pl.multiple_of(8 * c, 8), 8)]
    sends.start(half, half, where_sem.at[7], sibling)

    def halo_arrived(slot):
        distance = BLOCKS[slot]
        ref = rows_tile.at[:, halo_place(zs[distance], c), columns_of(distance)]
        sends.arrived(ref, ghalo_sem.at[slot], wide_up)
        sends.start(ref, ref, gsibhalo_sem.at[slot], sibling)

    halo_arrived(0)
    for way in range(2):
        sends.arrived(rows_tile.at[way, place(zs[4], c), own_cols], gfour_sem.at[way], behind[way])
    pass_on(7)
    for slot in range(1, 7):
        halo_arrived(slot)
    sends.arrived(where.at[1, pl.ds(pl.multiple_of(8 * (1 - c), 8), 8)], where_sem.at[7], sibling)
    sends.start(where.at[1], where.at[0], where_sem.at[8], wide_up)
    sends.start(where.at[1], where.at[2], where_sem.at[9], wide_down)
    for slot in range(8):
        distance = BLOCKS[slot]
        sends.arrived(rows_tile.at[:, place(zs[distance], 1 - c), columns_of(distance)], gsib_sem.at[slot], sibling)
    own.wait()

    def on_object(row):
        at = row + (256 * w - HALO)
        return (at >= 0) & (at < 256 * ROW_TILES)

    columns = one_hot((640, FRAME), lambda i, j: i == j + c0)
    lines = one_hot((FRAME, 512), lambda i, j: (j == i + r0) & on_object(j))
    patch = far.at[MODES]

    def narrow(rows):
        for plane in range(2):
            for part, value in enumerate(split(rows_tile[plane, rows])):
                narrowed[plane, part, rows] = dot(value, columns).astype(bf16)

    locals_[0].wait()
    light[...] = jnp.zeros_like(light)

    @pl.loop(0, MODES)
    def _(k):
        light[...] += probe[0, k] * probe[0, k] + probe[1, k] * probe[1, k]

    narrow(slice(HALO, HALO + 256))
    halo_arrived(7)
    for slot in range(8):
        distance = BLOCKS[slot]
        sends.arrived(
            rows_tile.at[:, halo_place(zs[distance], 1 - c), columns_of(distance)], gsibhalo_sem.at[slot], sibling
        )
    for copy in locals_[1:]:
        copy.wait()
    narrow(slice(0, HALO))
    narrow(slice(HALO + 256, 512))
    for plane in range(2):
        patch[FRAME * plane : FRAME * (plane + 1)] = dot(lines, narrowed[plane, 0]) + dot(lines, narrowed[plane, 1])

    pr, pi = patch[:FRAME], patch[FRAME:]
    for k in range(MODES):
        a, b = probe[0, k], probe[1, k]
        fre, fim = transform(a * pr - b * pi, a * pi + b * pr, tables, 1)
        far[k, :FRAME] = fre
        far[k, FRAME:] = fim
        squares = fre * fre + fim * fim
        factor[...] = squares if k == 0 else factor[...] + squares

    factor[...] = amp[...] / jnp.sqrt(jnp.maximum(factor[...], INTENSITY_FLOOR)) - 1.0

    def part_copy(k):
        return pltpu.make_async_remote_copy(
            src_ref=probe_part.at[1 - c, k], dst_ref=part_in.at[k],
            send_sem=part_send_sem.at[k], recv_sem=part_sem.at[k],
            device_id=sibling, device_id_type=MESH,
        )

    def first_copy(k, i):
        h = k % 2
        tx, ty = (x + i * h) % NX, (y + i * (1 - h)) % NY
        q = h * tx + (1 - h) * ty
        return pltpu.make_async_remote_copy(
            src_ref=part.at[k, pl.ds(pl.multiple_of(64 * q, 64), 64)], dst_ref=in1.at[k, i - 1],
            send_sem=send1_sem.at[k, i - 1], recv_sem=sem1.at[k, i - 1],
            device_id=(tx * NY + ty, m, n), device_id_type=MESH,
        )

    def take_part(k):
        part_copy(k).wait_recv()
        part[k] = part_in[k] + probe_part[c, k]
        for i in range(1, 4):
            first_copy(k, i).start()

    for k in range(MODES):
        scale = factor[...]
        cre, cim = transform(far[k, :FRAME] * scale, far[k, FRAME:] * scale, tables, -1)
        a, b = probe[0, k], probe[1, k]
        pr, pi = patch[:FRAME], patch[FRAME:]
        probe_part[0, k] = pr * cre + pi * cim
        probe_part[1, k] = pr * cim - pi * cre
        part_copy(k).start()
        gre, gim = a * cre + b * cim, a * cim - b * cre
        grad[0] = gre if k == 0 else grad[0] + gre
        grad[1] = gim if k == 0 else grad[1] + gim
        if k > 0:
            take_part(k - 1)

    def ways(k):
        if k % 2 == 0:
            return y, ys, y_peer, x, xs, x_peer
        return x, xs, x_peer, y, ys, y_peer

    def second_stage(k):
        first, _, _, _, theirs, peers = ways(k)
        rows = pl.ds(pl.multiple_of(64 * first, 64), 64)
        for i in range(1, 4):
            first_copy(k, i).wait_recv()
        sum1[k] = part[k, rows] + in1[k, 0] + in1[k, 1] + in1[k, 2]
        for i in range(1, 4):
            sends.start(
                sum1.at[k, pl.ds(pl.multiple_of(16 * theirs[i], 16), 16)],
                in2.at[k, i - 1], sem2.at[k, i - 1], peers[i],
            )

    def z_tile(pair, v):
        return (
            2 * pair + v // 4,
            pl.ds(pl.multiple_of(8 * ((v // 2) % 2), 8), 8),
            pl.ds(pl.multiple_of(128 * (v % 2), 128), 128),
        )

    def third_send(pair):
        for k in (2 * pair, 2 * pair + 1):
            _, _, _, second, _, peers = ways(k)
            for i in range(1, 4):
                sends.arrived(in2.at[k, i - 1], sem2.at[k, i - 1], peers[4 - i])
            rows = pl.ds(pl.multiple_of(16 * second, 16), 16)
            sum2[k] = sum1[k, rows] + in2[k, 0] + in2[k, 1] + in2[k, 2]
        for i in range(1, 8):
            sends.start(sum2.at[z_tile(pair, zs[i])], in3.at[pair, i - 1], sem3.at[pair, i - 1], z_peer[i])

    def third_sum(pair):
        for i in range(1, 8):
            sends.arrived(in3.at[pair, i - 1], sem3.at[pair, i - 1], z_peer[8 - i])
        whole = sum2[z_tile(pair, z)]
        for i in range(1, 8):
            whole = whole + in3[pair, i - 1]
        all3[z_tile(pair, z)] = whole
        for i in range(1, 8):
            ref = all3.at[z_tile(pair, z)]
            sends.start(ref, ref, asem3.at[pair, i - 1], z_peer[i])

    def out_rows(first, second, count):
        return pl.ds(pl.multiple_of(64 * first + 16 * second, 16), count)

    def back_second(pair):
        for i in range(1, 8):
            sends.arrived(all3.at[z_tile(pair, zs[8 - i])], asem3.at[pair, i - 1], z_peer[8 - i])
        for k in (2 * pair, 2 * pair + 1):
            first, _, _, second, _, peers = ways(k)
            rows = out_rows(first, second, 16)
            for i in range(1, 4):
                sends.start(all3.at[k], probe_out.at[c, k, rows], asem2.at[k, i - 1], peers[i])
            probe_out[c, k, rows] = all3[k]

    def back_first(pair):
        for k in (2 * pair, 2 * pair + 1):
            first, _, first_peers, _, theirs, peers = ways(k)
            for i in range(1, 4):
                ref = probe_out.at[c, k, out_rows(first, theirs[4 - i], 16)]
                sends.arrived(ref, asem2.at[k, i - 1], peers[4 - i])
            ref = probe_out.at[c, k, out_rows(first, 0, 64)]
            for i in range(1, 4):
                sends.start(ref, ref, asem1.at[k, i - 1], first_peers[i])
            sends.start(ref, ref, asem0.at[k, 0], sibling)

    def hand_over(pair):
        for k in (2 * pair, 2 * pair + 1):
            _, theirs, peers, _, _, _ = ways(k)
            for i in range(1, 4):
                ref = probe_out.at[c, k, out_rows(theirs[4 - i], 0, 64)]
                sends.arrived(ref, asem1.at[k, i - 1], peers[4 - i])
                sends.start(ref, ref, asem0.at[k, i], sibling)

    columns_back = one_hot((FRAME, 640), lambda i, j: j == i + c0)

    def put(core, dst):
        lines_back = one_hot(
            (FRAME, FRAME), lambda i, j: 64 * (i // STRIP) + STRIP * core + i % STRIP == j + r0
        )
        for plane in range(2):
            found = pick_columns(pick_rows(lines_back, grad[plane]), columns_back)
            for j in range(8):
                dst[j, plane] = found[STRIP * j : STRIP * (j + 1)]

    gathered = len(sends.copies)
    second_stage(0)
    put(1 - c, sib_out)
    for k in (0, 3, 1, 2):
        both = pl.ds(2 * k, 2)
        sends.start(sib_out.at[both], sib_in.at[both], sib_sem.at[k], sibling)
    take_part(3)
    second_stage(1)
    put(c, total)
    early = zh % 2
    for k in (0, 3, 1, 2):
        both = pl.ds(2 * k, 2)
        sends.arrived(sib_in.at[both], sib_sem.at[k], sibling)
        total[both] += sib_in[both]
        if k == 3:
            for i in (early, 1 - early):
                sends.start(total.at[i], halo_in.at[0, i], halo_sem.at[0, i], wide_down)
                sends.start(total.at[6 + i], halo_in.at[1, i], halo_sem.at[1, i], wide_up)
    third_send(0)

    weight[...] = jnp.zeros_like(weight)

    def lamp(t):
        light_high, light_low = split(light[...])
        a = w - 1 + t
        real = (a >= 0) & (a < ROW_TILES)
        shape = (16, STRIP, FRAME)
        rs = STRIP * n + 256 * (1 - t) + HALO - where[t][:, :, 0:1]
        hit = (lax.broadcasted_iota(jnp.int32, shape, 2) == lax.broadcasted_iota(jnp.int32, shape, 1) + rs) & real
        lines = jnp.where(hit, 1.0, 0.0).reshape((16 * STRIP, FRAME)).astype(bf16)
        lit[:, 0] = dot(lines, light_high).astype(bf16).reshape(shape)
        lit[:, 1] = dot(lines, light_low).astype(bf16).reshape(shape)

        def add(i, b, first, width):
            at = 8 * (i // 4) + 2 * (i % 4) + b
            cs = 512 * (m - b) + first + HALO - where[t, at][:, 1:2]
            columns = one_hot((FRAME, width), lambda p, q: p == q + cs)
            found = dot(lit[at].reshape((2 * STRIP, FRAME)), columns)
            return found[:STRIP] + found[STRIP:]

        @pl.loop(0, 8)
        def _(i):
            weight[...] += add(i, m, 0, 512)
            weight[:, out_cols] += add(i, 1 - m, 384 * (1 - m), 128)

    lamp(1)
    sends.arrived(where.at[0], where_sem.at[8], wide_down)

    def take_halo(i):
        for side in range(2):
            real = (w < ROW_TILES - 1) if side == 0 else (w > 0)
            sends.arrived(halo_in.at[side, i], halo_sem.at[side, i], wide_up if side == 0 else wide_down)
            total[(4 if side == 0 else 2) + i] += jnp.where(real, halo_in[side, i], 0.0)

    def block(zb):
        return total.at[2 + zb // 2, :, :, own_cols]

    second_stage(2)
    second_stage(3)
    sends.drain(gathered)
    take_halo(early)
    for way in range(2):
        sends.start(block(zs[4]).at[way], in_four.at[way], four_sem.at[way], onward[way])
    third_sum(0)
    third_send(1)
    take_halo(1 - early)
    for way in range(2):
        for step in range(2):
            distance = ((1, 3), (7, 5))[way][step]
            sends.start(
                total.at[2 + zs[distance] // 2, :, :, side_cols], in_side.at[way, step], side_sem.at[way, step],
                near_peer[way],
            )
    near = pl.ds(pl.multiple_of(384 - 256 * m, 128), 128)
    for way in range(2):
        sends.arrived(in_side.at[way, 1], side_sem.at[way, 1], near_peer[1 - way])
        zb = zs[2 if way == 0 else 6]
        total[2 + zb // 2, :, :, near] += in_side[way, 1]
        sends.start(block(zb).at[1 - way], in_two.at[way, 1 - way], two_sem.at[way, 1 - way], onward[way])
    for way in range(2):
        sends.arrived(in_four.at[way], four_sem.at[way], behind[way])
        in_four[way] += block(zs[2 if way == 0 else 6])[way]
        sends.start(in_four.at[way], in_two.at[way, way], two_sem.at[way, way], onward[way])
    scattered = len(sends.copies)
    back_second(0)
    third_sum(1)
    lamp(0)
    sends.arrived(where.at[2], where_sem.at[9], wide_up)
    lamp(2)
    back_first(0)
    back_second(1)
    sends.drain(scattered)

    for way in range(2):
        sends.arrived(in_side.at[way, 0], side_sem.at[way, 0], near_peer[1 - way])
    total[2 + zh, :, :, near] += in_side[0, 0] + in_side[1, 0]
    for way in range(2):
        for plane in range(2):
            sends.arrived(in_two.at[way, plane], two_sem.at[way, plane], behind[way])
    numerator = jnp.zeros((), f32)
    under = 1.0 / (weight[...] + DAMPING)
    squares = jnp.zeros((STRIP, 512), f32)
    for plane in range(2):
        strip = total[2 + zh, plane, :, own_cols] + in_two[0, plane] + in_two[1, plane]
        step = strip * under
        direction[plane] = step
        numerator += jnp.sum(step * strip)
        squares += step * step
    denominator = jnp.sum(squares * weight[...])
    line = lax.broadcasted_iota(jnp.int32, (8, 128), 0)
    tile[0] = jnp.where(line == 0, numerator, denominator)

    def tile_send(stage, peers, first):
        for i in range(1, len(peers)):
            sends.start(tile.at[stage], tiles_in.at[first + i - 1], tile_sem.at[first + i - 1], peers[i])

    def tile_sum(stage, peers, first):
        for i in range(1, len(peers)):
            sends.arrived(tiles_in.at[first + i - 1], tile_sem.at[first + i - 1], peers[len(peers) - i])
        found = tile[stage]
        for i in range(1, len(peers)):
            found = found + tiles_in[first + i - 1]
        tile[stage + 1] = found

    tile_send(0, [None, sibling], 0)
    tile_sum(0, [None, sibling], 0)
    tile_send(1, plane_peer, 1)
    back_first(1)
    for k in range(MODES):
        part_copy(k).wait_send()
        for i in range(1, 4):
            first_copy(k, i).wait_send()
    tile_sum(1, plane_peer, 1)
    tile_send(2, z_peer, 16)
    hand_over(0)
    closing = len(sends.copies)
    hand_over(1)
    sends.drain(closing)
    tile_sum(2, z_peer, 16)
    sums = tile[3]
    alpha = sums[0:1, 0:1] / sums[1:2, 0:1]
    step_out[...] = direction[...] * alpha
    for k in range(MODES):
        _, theirs, _, _, _, _ = ways(k)
        for i in range(4):
            sends.arrived(probe_out.at[1 - c, k, out_rows(theirs[(4 - i) % 4], 0, 64)], asem0.at[k, i], sibling)
    sends.finish()


VMEM = pl.BlockSpec(memory_space=pltpu.VMEM)
SMEM = pl.BlockSpec(memory_space=pltpu.SMEM)
ANY = pl.BlockSpec(memory_space=pl.ANY)
DMA = pltpu.SemaphoreType.DMA


def update(obj, probe, amp, tables, row, col):
    v = lambda *shape: pltpu.VMEM(shape, f32)
    return pl.pallas_call(
        update_kernel,
        out_shape=[
            pltpu.VMEM((2, STRIP, 512), f32),
            pltpu.VMEM((2, MODES, FRAME, FRAME), f32),
        ],
        in_specs=[ANY, ANY, ANY, ANY, SMEM, SMEM],
        out_specs=[VMEM, VMEM],
        scratch_shapes=[
            v(2, 512, 640),
            v(2, MODES, FRAME, FRAME),
            v(FRAME, FRAME),
            pltpu.VMEM((6, FRAME, FRAME), bf16),
            pltpu.VMEM((2, 2, 512, FRAME), bf16),
            v(MODES + 1, 512, FRAME),
            v(FRAME, FRAME),
            v(FRAME, FRAME),
            v(2, FRAME, FRAME),
            pltpu.VMEM((3, 16, 1, 128), jnp.int32),
            v(8, 2, STRIP, 640),
            v(8, 2, STRIP, 640),
            v(8, 2, STRIP, 640),
            v(2, 2, 2, STRIP, 640),
            v(2, STRIP, 512),
            v(2, 2, STRIP, 512),
            v(2, 2, 2, STRIP, 128),
            v(STRIP, 512),
            v(2, STRIP, 512),
            pltpu.VMEM((16, 2, STRIP, FRAME), bf16),
            v(2, MODES, FRAME, FRAME),
            v(MODES, FRAME, FRAME),
            v(MODES, FRAME, FRAME),
            v(MODES, 3, 64, FRAME),
            v(MODES, 64, FRAME),
            v(MODES, 3, 16, FRAME),
            v(MODES, 16, FRAME),
            v(2, 7, 8, 128),
            v(MODES, 16, FRAME),
            v(4, 8, 128),
            v(23, 8, 128),
            DMA((N_SENDS,)),
            DMA((4,)),
            DMA((2, 2)),
            DMA((2,)),
            DMA((2, 2)),
            DMA((8,)),
            DMA((8,)),
            DMA((8,)),
            DMA((10,)),
            DMA((4,)),
            DMA((2, 2)),
            DMA((2,)),
            DMA((2, 2)),
            DMA((2, 2)),
            DMA((MODES,)),
            DMA((MODES,)),
            DMA((MODES, 3)),
            DMA((MODES, 3)),
            DMA((MODES, 3)),
            DMA((2, 7)),
            DMA((2, 7)),
            DMA((MODES, 3)),
            DMA((MODES, 3)),
            DMA((MODES, 4)),
            DMA((23,)),
        ],
        compiler_params=pltpu.CompilerParams(
            collective_id=0, has_side_effects=True, vmem_limit_bytes=56 * 2**20
        ),
    )(obj, probe, amp, tables, row, col)


def per_device(obj_tile, probe, amplitude, row_offsets, col_offsets):
    step, gradient = update(
        obj_tile, probe, amplitude.reshape((FRAME, FRAME)), jnp.asarray(dft_tables()), row_offsets, col_offsets
    )
    return step, gradient


def solution(mesh):
    in_specs = (
        P(None, ("wide", "narrow"), "medium"),
        P(),
        P("wide", "medium", "narrow", None, None),
        P("wide", "medium", "narrow"),
        P("wide", "medium", "narrow"),
    )
    out_specs = (P(None, ("wide", "narrow"), "medium"), P())
    return jax.shard_map(
        per_device, mesh=mesh, in_specs=in_specs, out_specs=out_specs, check_vma=False
    )
```
